256 devices in a mesh: grp: 2 (over core), cell: 128 (over y, x, z).
Axes of the slice: x: 4, y: 4, z: 8, core: 2. Of those that a mesh axis runs over, the one named last changes fastest.
Arguments:
- path_delay: float32 [1064960], P('cell'), may hold values from 0 to 64
- path_angle: float32 [1064960], P('cell'), may hold values from -3.140625 to 3.140625
- path_gain: float32 [2, 1064960], P(None, 'cell'), may hold values from -0.9 to 0.9
- slot_counts: int32 [32768], P('cell'), may hold values from 1 to 64, as said below
- slot_offsets: int32 [32768], P('cell'), may hold values from 0 to 8319, as said below
- ray_link: int32 [32768], P('cell'), may hold values from 0 to 32767, as said below
- nearby_sectors: int32 [8, 4096], P(None, 'cell'), may hold values from 0 to 4095, as said below
- serving_slot: int32 [4096], P('cell'), may hold values from 0 to 7
- symbols: bfloat16 [4096, 2, 128], P('cell'), may hold values from -4 to 4
Outputs:
- received: float32 [4096, 2, 128], P('cell')
The draws below stay inside these ranges and needn't reach their ends.
Inputs may be any that keep to these rules, and one draw needn't show every extreme that they name: `slot_counts`: the counts of one device's 256 ray slots sum to 8320, and every device has a slot of 64 paths. The ray slots of one device hold at most 130 paths of links of one owner, and exactly 130 for some owner. Within one device, the ranges slot_offsets to slot_offsets + slot_counts - 1 of its 256 slots cover the device's 8320 paths once each. `ray_link`: every link appears in exactly one ray slot. The owner of link g is the device g // 256, which holds its user; within the ray slots of one device the owners never fall. The ray slots of one device hold at most 4 links of one owner, and exactly 4 of some owner; every owner has 256 links in all. `nearby_sectors`: entry serving_slot[u] of user u is its serving sector, one of the sectors of the device that holds the user; every other entry lies within 16 sector indices of the serving sector, and on every device some user has entries at distance exactly 16.
All inputs are finite; a program needn't handle non-finite values.
Results may differ from the reference program's by a relative error of at most 0.0027.
Values may be sent and summed in bfloat16 or wider, within the bound.
A program may use at most 64 MiB of HBM per device.

```python
import math
import jax
import jax.numpy as jnp
from jax import lax

SECTOR_ANTENNAS = 64
FRAME_TONES = 128
PMAX = 64
NEARBY_COUNT = 8
CELL_SECTORS = 32
USR_DEV = 32
LINK_DEV = 256
PATH_DEV = 8320
REACH = 16
USERS = 4096
SECTOR_TOTAL = 4096
LINKS = 32768
PATHS = 1064960
N_CELL = 128


def layout_parts(key):
    subkeys = jax.random.split(jax.random.fold_in(key, 5), 5)
    mean_load = LINK_DEV // N_CELL
    swing = jax.random.randint(subkeys[0], (N_CELL // 2,), 0, mean_load + 1)
    swing = swing.at[0].set(mean_load)
    pair_loads = jnp.stack([mean_load + swing, mean_load - swing], axis=1).reshape(N_CELL)
    pair_loads = jax.random.permutation(subkeys[1], pair_loads)
    sender_shift = jax.random.permutation(subkeys[2], N_CELL)
    owner_shift = jax.random.permutation(subkeys[3], N_CELL)
    load_table = pair_loads[(sender_shift[:, None] + owner_shift[None, :]) % N_CELL]
    owner_start = jnp.cumsum(load_table, axis=0) - load_table
    slot_end = jnp.cumsum(load_table, axis=1)
    slot_start = slot_end - load_table
    slot_grid = jnp.arange(LINK_DEV)
    owner_pick = jax.vmap(lambda ends_row: jnp.searchsorted(ends_row, slot_grid, side='right'))(slot_end)
    owner_pick = jnp.minimum(owner_pick, N_CELL - 1)
    within = slot_grid[None, :] - jnp.take_along_axis(slot_start, owner_pick, axis=1)
    slot_load = jnp.take_along_axis(load_table, owner_pick, axis=1)
    owner_pos = jnp.take_along_axis(owner_start, owner_pick, axis=1) + within
    owner_perm = jax.vmap(lambda one_key: jax.random.permutation(one_key, LINK_DEV))(jax.random.split(subkeys[4], N_CELL))
    link_ids = owner_pick * LINK_DEV + owner_perm[owner_pick, owner_pos]
    return (link_ids.reshape(LINKS).astype(jnp.int32), within, slot_load)


def last_single(storage_row, count_row):
    single = jnp.argmax((count_row == 1).astype(jnp.int32))
    where_single = jnp.argmax((storage_row == single).astype(jnp.int32))
    tail_slot = storage_row[LINK_DEV - 1]
    return storage_row.at[where_single].set(tail_slot).at[LINK_DEV - 1].set(single)


def spread_leftover(rank_row, left_row, value_row):
    target = jnp.where(left_row, rank_row, LINK_DEV)
    return jnp.zeros((LINK_DEV + 1,), value_row.dtype).at[target].set(value_row)


def path_plan(key):
    link_ids, within, slot_load = layout_parts(key)
    subkeys = jax.random.split(jax.random.fold_in(key, 7), 3)
    value = jax.random.randint(subkeys[0], (N_CELL, LINK_DEV), 1, PMAX + 1)
    value = value.at[:, 0].set(PMAX)
    leftover = (slot_load % 2 == 1) & (within == slot_load - 1)
    left_rank = jnp.cumsum(leftover.astype(jnp.int32), axis=1) - 1
    left_value = jax.vmap(spread_leftover)(left_rank, leftover, value)
    prev_left = jnp.take_along_axis(left_value, jnp.maximum(left_rank - 1, 0), axis=1)
    prev_value = jnp.concatenate([value[:, :1], value[:, :-1]], axis=1)
    paired = jnp.where(within % 2 == 0, value, PMAX + 1 - prev_value)
    odd_pair = jnp.where(left_rank % 2 == 0, value, PMAX + 1 - prev_left)
    counts = jnp.where(leftover, odd_pair, paired)
    storage = jax.vmap(lambda one_key: jax.random.permutation(one_key, LINK_DEV))(jax.random.split(subkeys[2], N_CELL))
    storage = jax.vmap(last_single)(storage, counts)
    stored_counts = jnp.take_along_axis(counts, storage, axis=1)
    stored_start = jnp.cumsum(stored_counts, axis=1) - stored_counts
    offsets = jax.vmap(lambda order_row, start_row: jnp.zeros((LINK_DEV,), start_row.dtype).at[order_row].set(start_row))(storage, stored_start)
    return (counts.reshape(LINKS).astype(jnp.int32), offsets.reshape(LINKS).astype(jnp.int32))


def sector_plan(key):
    subkeys = jax.random.split(jax.random.fold_in(key, 23), 4)
    user_index = jnp.arange(USERS)
    home_sector = user_index // USR_DEV * CELL_SECTORS + jax.random.randint(subkeys[0], (USERS,), 0, CELL_SECTORS)
    home_sector = jnp.where(user_index == 0, 0, home_sector)
    home_sector = jnp.where(user_index == USERS - 1, SECTOR_TOTAL - 1, home_sector)
    serve_slot = jax.random.randint(subkeys[1], (USERS,), 0, NEARBY_COUNT)
    distance = jax.random.randint(subkeys[2], (NEARBY_COUNT, USERS), 1, REACH + 1)
    distance = jnp.where((user_index % USR_DEV == 0)[None, :], REACH, distance)
    sign_pick = 2 * jax.random.randint(subkeys[3], (NEARBY_COUNT, USERS), 0, 2) - 1
    forward = home_sector[None, :] + sign_pick * distance
    inside = (forward >= 0) & (forward < SECTOR_TOTAL)
    chosen = jnp.where(inside, forward, home_sector[None, :] - sign_pick * distance)
    slot_grid = jnp.arange(NEARBY_COUNT)[:, None]
    nearby = jnp.where(slot_grid == serve_slot[None, :], home_sector[None, :], chosen)
    return (nearby.astype(jnp.int32), serve_slot.astype(jnp.int32))


def draw_ray_link(key, part):
    return layout_parts(key)[0]


def draw_slot_counts(key, part):
    return path_plan(key)[0]


def draw_slot_offsets(key, part):
    return path_plan(key)[1]


def draw_nearby_sectors(key, part):
    return sector_plan(key)[0]


def draw_serving_slot(key, part):
    return sector_plan(key)[1]


def shard_levels(stream_key, extent, cuts, least, high):
    def one(axis_at, blocks):
        heights = jax.random.uniform(jax.random.fold_in(jax.random.fold_in(stream_key, 6), axis_at), (blocks,), jnp.float32, least / len(cuts), high / len(cuts))
        return jnp.repeat(jnp.exp(heights), extent[axis_at] // blocks).reshape((-1,) + (1,) * (len(extent) - axis_at - 1))

    level = one(*cuts[0])
    for cut in cuts[1:]:
        level = level * one(*cut)
    return level


def normal_values(rng, dims, deviation, reach, cuts=(), kind=jnp.bfloat16):
    level = shard_levels(rng, dims, cuts, -0.22, 0.18) if cuts else 1.0
    values = jax.random.normal(rng, dims, jnp.float32) * deviation * level
    return jnp.minimum(jnp.maximum(values, -reach), reach).astype(kind)


def setup_inputs(seed: int = 0) -> dict:
    splits = jax.random.split(jax.random.key(seed), 10)
    path_delay = jnp.clip(64.0 * jax.random.uniform(splits[0], (PATHS,), jnp.float32) ** shard_levels(splits[0], (PATHS,), ((0, 128),), -0.2, 0.2), 0.0, 64.0)
    path_angle = jnp.clip(jax.random.uniform(splits[1], (PATHS,), jnp.float32, -3.140625, 3.140625), -3.140625, 3.140625)
    path_gain = normal_values(splits[2], (2, PATHS), 0.15, 0.9, ((1, 128),), jnp.float32)
    slot_counts = draw_slot_counts(jax.random.fold_in(splits[9], 71), 0)
    slot_offsets = draw_slot_offsets(jax.random.fold_in(splits[9], 71), 0)
    ray_link = draw_ray_link(jax.random.fold_in(splits[9], 71), 0)
    nearby_sectors = draw_nearby_sectors(jax.random.fold_in(splits[9], 71), 0)
    serving_slot = draw_serving_slot(jax.random.fold_in(splits[9], 71), 0)
    symbols = normal_values(splits[8], (USERS, 2, FRAME_TONES), 1.0, 4.0, ((0, 128),))
    return {"path_delay": path_delay, "path_angle": path_angle, "path_gain": path_gain, "slot_counts": slot_counts, "slot_offsets": slot_offsets, "ray_link": ray_link, "nearby_sectors": nearby_sectors, "serving_slot": serving_slot, "symbols": symbols}


EPSILON = 1e-06

def rounded(value):
    return lax.optimization_barrier(value.astype(jnp.bfloat16)).astype(jnp.float32)

def make_response(delay_rows, angle_rows, real_rows, imag_rows, antenna_array):
    tone_freq = (jnp.arange(FRAME_TONES, dtype=jnp.float32) - FRAME_TONES // 2) / FRAME_TONES
    delay_phase = 2 * math.pi * delay_rows[:, :, None] * tone_freq[None, None, :]
    delay_real = rounded(jnp.cos(delay_phase))
    delay_imag = rounded(-jnp.sin(delay_phase))
    steer_phase = math.pi * antenna_array[None, :, None] * jnp.sin(angle_rows)[:, None, :]
    steer_cos = jnp.cos(steer_phase)
    steer_sin = jnp.sin(steer_phase)
    spread_real = rounded(real_rows[:, None, :] * steer_cos + imag_rows[:, None, :] * steer_sin)
    spread_imag = rounded(imag_rows[:, None, :] * steer_cos - real_rows[:, None, :] * steer_sin)
    resp_real = jnp.einsum('bap,bpf->baf', spread_real, delay_real) - jnp.einsum('bap,bpf->baf', spread_imag, delay_imag)
    resp_imag = jnp.einsum('bap,bpf->baf', spread_real, delay_imag) + jnp.einsum('bap,bpf->baf', spread_imag, delay_real)
    return rounded(jnp.stack([resp_real, resp_imag], axis=1))

def link_tables(path_delay, path_angle, path_gain, slot_counts, slot_offsets, ray_link):
    slot_index = jnp.arange(LINKS, dtype=jnp.int32)
    source = jnp.zeros((LINKS,), jnp.int32).at[ray_link].set(slot_index)
    counts = slot_counts[source]
    first_path = source // LINK_DEV * PATH_DEV + slot_offsets[source]
    path_steps = jnp.arange(PMAX, dtype=jnp.int32)
    live_mask = path_steps[None, :] < counts[:, None]
    where_path = jnp.clip(first_path[:, None] + path_steps[None, :], 0, PATHS - 1)
    columns = (path_delay, path_angle, path_gain[0], path_gain[1])
    return jnp.stack([jnp.where(live_mask, column[where_path], 0.0) for column in columns])

def reference(path_delay, path_angle, path_gain, slot_counts, slot_offsets, ray_link, nearby_sectors, serving_slot, symbols):
    tables = link_tables(path_delay, path_angle, path_gain, slot_counts, slot_offsets, ray_link)
    antenna_array = jnp.arange(SECTOR_ANTENNAS, dtype=jnp.float32)

    def owner_emission(owner):
        user_ids = owner * USR_DEV + jnp.arange(USR_DEV, dtype=jnp.int32)
        slot_pick = serving_slot[user_ids]
        serve_links = user_ids * NEARBY_COUNT + slot_pick
        link_rows = tables[:, serve_links, :]
        response = make_response(link_rows[0], link_rows[1], link_rows[2], link_rows[3], antenna_array)
        symbol_rows = symbols[user_ids].astype(jnp.float32)
        contribution_real = response[:, 0] * symbol_rows[:, 0, None, :] + response[:, 1] * symbol_rows[:, 1, None, :]
        contribution_imag = response[:, 0] * symbol_rows[:, 1, None, :] - response[:, 1] * symbol_rows[:, 0, None, :]
        sector_ids = nearby_sectors[slot_pick, user_ids] - owner * CELL_SECTORS
        unscaled_signal = jax.ops.segment_sum(jnp.stack([contribution_real, contribution_imag], axis=1), sector_ids, num_segments=CELL_SECTORS)
        antenna_power = lax.optimization_barrier(jnp.mean(unscaled_signal[:, 0] * unscaled_signal[:, 0] + unscaled_signal[:, 1] * unscaled_signal[:, 1], axis=2))
        return (unscaled_signal / jnp.sqrt(antenna_power + EPSILON)[:, None, :, None]).astype(jnp.bfloat16)
    transmit_weights = lax.map(owner_emission, jnp.arange(N_CELL, dtype=jnp.int32)).reshape(SECTOR_TOTAL, 2, SECTOR_ANTENNAS, FRAME_TONES)

    def owner_received(owner):
        user_ids = owner * USR_DEV + jnp.arange(USR_DEV, dtype=jnp.int32)
        link_rows = lax.dynamic_slice_in_dim(tables, owner * LINK_DEV, LINK_DEV, axis=1)
        response = make_response(link_rows[0], link_rows[1], link_rows[2], link_rows[3], antenna_array)
        sector_ids = nearby_sectors[:, user_ids].T.reshape(LINK_DEV)
        remote = transmit_weights[sector_ids].astype(jnp.float32)
        recv_real = lax.optimization_barrier(jnp.sum(response[:, 0] * remote[:, 0] - response[:, 1] * remote[:, 1], axis=1))
        recv_imag = lax.optimization_barrier(jnp.sum(response[:, 0] * remote[:, 1] + response[:, 1] * remote[:, 0], axis=1))
        link_values = jnp.stack([recv_real, recv_imag], axis=1).reshape(USR_DEV, NEARBY_COUNT, 2, FRAME_TONES)
        return lax.optimization_barrier(jnp.sum(link_values, axis=1)) / math.sqrt(SECTOR_ANTENNAS)
    return lax.map(owner_received, jnp.arange(N_CELL, dtype=jnp.int32)).reshape(USERS, 2, FRAME_TONES)
```

```python
import functools
import math

import jax
import jax.numpy as jnp
from jax import lax
from jax.experimental import pallas as pl
from jax.experimental.pallas import tpu as pltpu
from jax.sharding import PartitionSpec as P

SECTOR_ANTENNAS = 64
FRAME_TONES = 128
NEARBY_COUNT = 8
CELL_SECTORS = 32
REACH = 16
EPSILON = 1e-06

CELLS = 128
SLOTS = 256
USERS = 32
LINKS = USERS * NEARBY_COUNT
PATH_ROWS = 65
ANT = SECTOR_ANTENNAS // 2
RESP = 2 * ANT
TAG_LANE = 8
VMEM_LIMIT = 48 * 1024 * 1024
MESH = pl.DeviceIdType.MESH


def lanes(shape):
    return lax.broadcasted_iota(jnp.int32, shape, len(shape) - 1)


def rows_of(shape):
    return lax.broadcasted_iota(jnp.int32, shape, len(shape) - 2)


def sincos_turns(turns):
    r = turns - jnp.round(turns)
    r2 = r * r
    sin_c = [(-1) ** n * math.pi ** (2 * n + 1) / math.factorial(2 * n + 1) for n in range(7)]
    cos_c = [(-1) ** n * math.pi ** (2 * n) / math.factorial(2 * n) for n in range(7)]
    sh = jnp.full_like(r, sin_c[-1])
    ch = jnp.full_like(r, cos_c[-1])
    for n in range(5, -1, -1):
        sh = sh * r2 + sin_c[n]
        ch = ch * r2 + cos_c[n]
    sh = sh * r
    return 2.0 * sh * ch, 1.0 - 2.0 * sh * sh


def pack_kernel(counts, offsets, links, delay, angle, gain, out, store):
    for c in range(0, PATH_ROWS, 8):
        n = min(8, PATH_ROWS - c)
        for f, ref in ((0, delay), (1, angle)):
            value = ref[c : c + n, :]
            value = value * (1.0 / FRAME_TONES) if f == 0 else jnp.sin(value)
            store[pl.ds(8 * (c + 1) + f, n, stride=8), :] = value
            store[pl.ds(8 * c + 4 + f, n, stride=8), :] = value
    for q in range(PATH_ROWS):
        pair = gain[:, 128 * q : 128 * (q + 1)]
        store[8 * (q + 1) + 2 : 8 * (q + 1) + 4, :] = pair
        store[8 * q + 6 : 8 * q + 8, :] = pair

    def clear(i, carry):
        out[pl.ds(pl.multiple_of(64 * i, 64), 64), :] = jnp.zeros((64, 128), jnp.float32)
        return carry

    lax.fori_loop(0, CELLS * 8 // 64, clear, 0)
    lane = lanes((8, 128))
    row = rows_of((8, 128))
    high = row >= 4
    place = lane + jnp.where(high, 128, 0)
    tag_place = jnp.where(row == 4, lane - TAG_LANE, -1000)

    def one(r, carry):
        before, k, base, last = carry
        link = links[r]
        owner = link >> 8
        same = owner == before
        k = jnp.where(same, k + 1, 0)
        base = jnp.where(same, base + last, 0)
        off = offsets[r]
        cnt = counts[r]
        q = off >> 7
        s = off & 127
        block = store[pl.ds(pl.multiple_of(8 * q + 8, 8), 8), :]
        turned = pltpu.roll(block, (base - s) & 127, 1)
        swapped = pltpu.roll(turned, 4, 0)
        j = place - base
        second = (j + s) >= 128
        value = jnp.where(second == high, turned, swapped)
        at = pl.ds(pl.multiple_of(8 * owner, 8), 8)
        new = jnp.where((j >= 0) & (j < cnt), value, out[at, :])
        new = jnp.where(tag_place == 2 * k, ((link & 255) + 1).astype(jnp.float32), new)
        new = jnp.where(tag_place == 2 * k + 1, cnt.astype(jnp.float32), new)
        out[at, :] = new
        return owner, k, base, cnt

    zero = jnp.int32(0)
    lax.fori_loop(0, SLOTS, one, (jnp.int32(-1), zero, zero, zero), unroll=8)


def exchange_kernel(sent, got, send_sem, recv_sem):
    me = lax.axis_index("cell")
    barrier = pltpu.get_barrier_semaphore()

    def greet(d, carry):
        other = lax.rem(me + d, CELLS)
        pl.semaphore_signal(barrier, inc=1, device_id={"cell": other}, device_id_type=MESH)
        return carry

    lax.fori_loop(1, CELLS, greet, 0)
    mine = pl.ds(pl.multiple_of(8 * me, 8), 8)
    got[mine, :] = sent[mine, :]
    pl.semaphore_wait(barrier, CELLS - 1)

    def send(d, carry):
        other = lax.rem(me + d, CELLS)
        pltpu.make_async_remote_copy(
            src_ref=sent.at[pl.ds(pl.multiple_of(8 * other, 8), 8), :],
            dst_ref=got.at[mine, :],
            send_sem=send_sem,
            recv_sem=recv_sem,
            device_id={"cell": other},
            device_id_type=MESH,
        ).start()
        return carry

    lax.fori_loop(1, CELLS, send, 0)
    rest = pl.ds(0, 8 * (CELLS - 1))
    whole = pltpu.make_async_remote_copy(
        src_ref=sent.at[rest, :],
        dst_ref=got.at[rest, :],
        send_sem=send_sem,
        recv_sem=recv_sem,
        device_id={"cell": lax.rem(me + 1, CELLS)},
        device_id_type=MESH,
    )
    whole.wait_send()
    whole.wait_recv()


def seeds_of(fields, grp, e_seed, s_seed, coef):
    turns, sine, real, imag = fields
    hi = lanes((8, 128)) >= 64
    s1, c1 = sincos_turns(turns)
    e = jnp.where(hi, 0.0, 1.0)
    f = jnp.where(hi, 1.0, 0.0)
    e_seed[pl.ds(8, 8, stride=16), :] = e
    for j in range(1, 9):
        e, f = e * c1 - f * s1, f * c1 + e * s1
        if j < 8:
            e_seed[pl.ds(8 + j, 8, stride=16), :] = e
        e_seed[pl.ds(8 - j, 8, stride=16), :] = jnp.where(hi, -e, e)
    _, c8 = sincos_turns(8.0 * turns)
    coef[0:8, :] = 2.0 * c8
    sa, ca = sincos_turns(0.5 * sine)
    first = (grp * (ANT // 2)).astype(jnp.float32)
    s0, c0 = sincos_turns(first * sine)
    _, a8 = sincos_turns(4.0 * sine)
    coef[8:16, :] = 2.0 * a8
    g1 = jnp.where(hi, -imag, real)
    g2 = jnp.where(hi, real, imag)
    x = g1 * c0 + g2 * s0
    y = g2 * c0 - g1 * s0
    for a in range(16):
        s_seed[pl.ds(a, 8, stride=32), :] = x
        s_seed[pl.ds(16 + a, 8, stride=32), :] = y
        if a < 15:
            x, y = x * ca + y * sa, y * ca - x * sa


def response_of(l, e_seed, s_seed, coef):
    c = jnp.broadcast_to(coef[l : l + 1, :], (8, 128))
    low = e_seed[16 * l : 16 * l + 8, :]
    top = e_seed[16 * l + 8 : 16 * l + 16, :]
    down = [top, low]
    up = [low, top]
    for _ in range(7):
        down.append(c * down[-1] - down[-2])
        up.append(c * up[-1] - up[-2])
    table = jnp.concatenate(down[:0:-1] + up[1:], axis=0).astype(jnp.bfloat16)
    c = jnp.broadcast_to(coef[8 + l : 9 + l, :], (8, 128))
    parts = []
    for h in range(2):
        at = 32 * l + 16 * h
        run = [s_seed[at : at + 8, :], s_seed[at + 8 : at + 16, :]]
        for _ in range(2):
            run.append(c * run[-1] - run[-2])
        parts += run
    spread = jnp.concatenate(parts, axis=0).astype(jnp.bfloat16)
    return lax.dot_general(
        spread, table, (((1,), (1,)), ((), ())), preferred_element_type=jnp.float32
    )


SEED_SCRATCH = [
    pltpu.VMEM((8 * 16, 128), jnp.float32),
    pltpu.VMEM((8 * 32, 128), jnp.float32),
    pltpu.VMEM((16, 128), jnp.float32),
]


def transmit_kernel(
    slots, nearby, got, symbols, rows, weights, tag_v, tag_s, table, raw, serving, e_seed, s_seed, coef, sem
):
    me = lax.axis_index("cell")
    grp = lax.axis_index("grp")
    for c in range(0, CELLS, 8):
        tag_v[c : c + 8, :] = got[pl.ds(8 * c + 4, 8, stride=8), :].astype(jnp.int32)
    copy = pltpu.make_async_copy(tag_v, tag_s, sem)
    copy.start()

    def clear(i, carry):
        raw[pl.ds(pl.multiple_of(64 * i, 64), 64), :] = jnp.zeros((64, 128), jnp.float32)
        return carry

    lax.fori_loop(0, CELL_SECTORS * RESP // 64, clear, 0)
    copy.wait()

    def index(i, carry):
        base = jnp.int32(0)
        for k in range(4):
            tag = tag_s[i, TAG_LANE + 2 * k]
            cnt = tag_s[i, TAG_LANE + 2 * k + 1]
            table[tag] = (i << 16) + (base << 8) + cnt
            base = base + cnt
        return carry

    lax.fori_loop(0, CELLS, index, 0, unroll=4)
    lane = lanes((8, 128))

    def unpack(g, carry):
        code = table[g + 1]
        i = code >> 16
        base = (code >> 8) & 255
        cnt = code & 255
        block = got[pl.ds(pl.multiple_of(8 * i, 8), 8), :]
        turned = pltpu.roll(block, (0 - base) & 127, 1)
        swapped = pltpu.roll(turned, 4, 0)
        value = jnp.where(lane + base >= 128, swapped, turned)
        value = jnp.where(lane < cnt, value, 0.0)
        rows[pl.ds(pl.multiple_of(8 * g, 8), 8), :] = value + pltpu.roll(value, 64, 1)
        return carry

    lax.fori_loop(0, LINKS, unpack, 0, unroll=8)

    def serve(u, carry):
        link = u * NEARBY_COUNT + slots[u]
        serving[pl.ds(pl.multiple_of(8 * u, 8), 8), :] = rows[pl.ds(pl.multiple_of(8 * link, 8), 8), :]
        return carry

    lax.fori_loop(0, USERS, serve, 0, unroll=8)

    def eight_users(c, carry):
        fields = [serving[pl.ds(64 * c + f, 8, stride=8), :] for f in range(4)]
        seeds_of(fields, grp, e_seed, s_seed, coef)
        for l in range(8):
            u = 8 * c + l
            resp = response_of(l, e_seed, s_seed, coef).astype(jnp.bfloat16).astype(jnp.float32)
            sym = symbols[u].astype(jnp.float32)
            sym_r, sym_i = sym[0:1, :], sym[1:2, :]
            real, imag = resp[:ANT, :], resp[ANT:, :]
            part = jnp.concatenate(
                [real * sym_r + imag * sym_i, real * sym_i - imag * sym_r], axis=0
            )
            sector = nearby[slots[u], u] - me * CELL_SECTORS
            at = pl.ds(pl.multiple_of(RESP * sector, RESP), RESP)
            raw[at, :] = raw[at, :] + part
        return carry

    lax.fori_loop(0, USERS // 8, eight_users, 0)

    def normalise(s, carry):
        at = pl.ds(pl.multiple_of(RESP * s, RESP), RESP)
        value = raw[at, :]
        real, imag = value[:ANT, :], value[ANT:, :]
        power = jnp.mean(real * real + imag * imag, axis=1, keepdims=True)
        scale = 1.0 / jnp.sqrt(power + EPSILON)
        weights[s] = jnp.concatenate([real * scale, imag * scale], axis=0).astype(jnp.bfloat16)
        return carry

    lax.fori_loop(0, CELL_SECTORS, normalise, 0, unroll=2)


def receive_kernel(
    nearby, rows, weights, out, near, resp, part, other, e_seed, s_seed, coef, sems
):
    me = lax.axis_index("cell")
    grp = lax.axis_index("grp")
    right = lax.rem(me + 1, CELLS)
    left = lax.rem(me + CELLS - 1, CELLS)
    barrier = pltpu.get_barrier_semaphore()
    for target in ({"cell": left}, {"cell": right}, {"grp": 1 - grp}):
        pl.semaphore_signal(barrier, inc=1, device_id=target, device_id_type=MESH)
    pl.semaphore_wait(barrier, 3)
    to_right = pltpu.make_async_remote_copy(
        src_ref=weights.at[pl.ds(CELL_SECTORS - REACH, REACH)],
        dst_ref=near.at[pl.ds(0, REACH)],
        send_sem=sems.at[0],
        recv_sem=sems.at[1],
        device_id={"cell": right},
        device_id_type=MESH,
    )
    to_left = pltpu.make_async_remote_copy(
        src_ref=weights.at[pl.ds(0, REACH)],
        dst_ref=near.at[pl.ds(REACH + CELL_SECTORS, REACH)],
        send_sem=sems.at[2],
        recv_sem=sems.at[3],
        device_id={"cell": left},
        device_id_type=MESH,
    )
    to_right.start()
    to_left.start()
    keep = pltpu.make_async_copy(weights, near.at[pl.ds(REACH, CELL_SECTORS)], sems.at[4])
    keep.start()

    def respond(u, carry):
        fields = [rows[pl.ds(64 * u + f, 8, stride=8), :] for f in range(4)]
        seeds_of(fields, grp, e_seed, s_seed, coef)
        for l in range(8):
            at = pl.ds(pl.multiple_of(u * (8 * RESP) + RESP * l, RESP), RESP)
            resp[at, :] = response_of(l, e_seed, s_seed, coef).astype(jnp.bfloat16)
        return carry

    lax.fori_loop(0, USERS, respond, 0)
    keep.wait()
    to_right.wait()
    to_left.wait()

    def combine(u, carry):
        real = jnp.zeros((ANT, 128), jnp.float32)
        imag = jnp.zeros((ANT, 128), jnp.float32)
        for k in range(NEARBY_COUNT):
            sector = nearby[k, u] - me * CELL_SECTORS + REACH
            sector = jnp.clip(sector, 0, CELL_SECTORS + 2 * REACH - 1)
            tx = near[sector].astype(jnp.float32)
            at = pl.ds(pl.multiple_of(u * (8 * RESP) + RESP * k, RESP), RESP)
            ch = resp[at, :].astype(jnp.float32)
            real = real + (ch[:ANT] * tx[:ANT] - ch[ANT:] * tx[ANT:])
            imag = imag + (ch[:ANT] * tx[ANT:] + ch[ANT:] * tx[:ANT])
        part[u] = jnp.concatenate(
            [jnp.sum(real, axis=0, keepdims=True), jnp.sum(imag, axis=0, keepdims=True)], axis=0
        )
        return carry

    lax.fori_loop(0, USERS, combine, 0)
    swap = pltpu.make_async_remote_copy(
        src_ref=part,
        dst_ref=other,
        send_sem=sems.at[5],
        recv_sem=sems.at[6],
        device_id={"grp": 1 - grp},
        device_id_type=MESH,
    )
    swap.start()
    swap.wait()
    out[...] = (part[...] + other[...]) * (1.0 / math.sqrt(SECTOR_ANTENNAS))


VMEM = pl.BlockSpec(memory_space=pltpu.VMEM)
SMEM = pl.BlockSpec(memory_space=pltpu.SMEM)


def call(kernel, name, out_shape, in_specs, scratch, remote=None):
    extra = {} if remote is None else {"collective_id": remote, "has_side_effects": True}
    many = isinstance(out_shape, (tuple, list))
    return pl.pallas_call(
        kernel,
        name=name,
        out_shape=out_shape,
        in_specs=in_specs,
        out_specs=[VMEM] * len(out_shape) if many else VMEM,
        scratch_shapes=scratch,
        compiler_params=pltpu.CompilerParams(vmem_limit_bytes=VMEM_LIMIT, **extra),
    )


def shards(
    path_delay,
    path_angle,
    path_gain,
    slot_counts,
    slot_offsets,
    ray_link,
    nearby_sectors,
    serving_slot,
    symbols,
):
    f32, bf16, i32 = jnp.float32, jnp.bfloat16, jnp.int32
    message = jax.ShapeDtypeStruct((CELLS * 8, 128), f32)
    sent = call(
        pack_kernel,
        "pack",
        message,
        [SMEM, SMEM, SMEM, VMEM, VMEM, VMEM],
        [pltpu.VMEM((8 * (PATH_ROWS + 1), 128), f32)],
    )(
        slot_counts,
        slot_offsets,
        ray_link,
        path_delay.reshape(PATH_ROWS, 128),
        path_angle.reshape(PATH_ROWS, 128),
        path_gain,
    )
    got = call(
        exchange_kernel,
        "exchange",
        message,
        [VMEM],
        [pltpu.SemaphoreType.DMA, pltpu.SemaphoreType.DMA],
        remote=0,
    )(sent)
    rows, weights = call(
        transmit_kernel,
        "transmit",
        (
            jax.ShapeDtypeStruct((LINKS * 8, 128), f32),
            jax.ShapeDtypeStruct((CELL_SECTORS, RESP, 128), bf16),
        ),
        [SMEM, SMEM, VMEM, VMEM],
        [
            pltpu.VMEM((CELLS, 128), i32),
            pltpu.SMEM((CELLS, 128), i32),
            pltpu.SMEM((LINKS + 8,), i32),
            pltpu.VMEM((CELL_SECTORS * RESP, 128), f32),
            pltpu.VMEM((USERS * 8, 128), f32),
            *SEED_SCRATCH,
            pltpu.SemaphoreType.DMA,
        ],
    )(serving_slot, nearby_sectors, got, symbols)
    return call(
        receive_kernel,
        "receive",
        jax.ShapeDtypeStruct((USERS, 2, FRAME_TONES), f32),
        [SMEM, VMEM, VMEM],
        [
            pltpu.VMEM((CELL_SECTORS + 2 * REACH, RESP, 128), bf16),
            pltpu.VMEM((LINKS * RESP, 128), bf16),
            pltpu.VMEM((USERS, 2, FRAME_TONES), f32),
            pltpu.VMEM((USERS, 2, FRAME_TONES), f32),
            *SEED_SCRATCH,
            pltpu.SemaphoreType.DMA((7,)),
        ],
        remote=1,
    )(nearby_sectors, rows, weights)


def solution(mesh):
    placed = (
        P("cell"),
        P("cell"),
        P(None, "cell"),
        P("cell"),
        P("cell"),
        P("cell"),
        P(None, "cell"),
        P("cell"),
        P("cell", None, None),
    )
    return jax.shard_map(
        shards, mesh=mesh, in_specs=placed, out_specs=P("cell", None, None), check_vma=False
    )
```

```python
import functools
import math

import jax
import jax.numpy as jnp
from jax import lax
from jax.experimental import pallas as pl
from jax.experimental.pallas import tpu as pltpu
from jax.sharding import PartitionSpec as P

SECTOR_ANTENNAS = 64
FRAME_TONES = 128
NEARBY_COUNT = 8
CELL_SECTORS = 32
REACH = 16
EPSILON = 1e-06

CELLS = 128
SLOTS = 256
USERS = 32
LINKS = USERS * NEARBY_COUNT
PATH_ROWS = 65
ANT = SECTOR_ANTENNAS // 2
RESP = 2 * ANT
TAG_LANE = 8
HALF = CELLS // 2
WIRE_ROWS = 5
MIB = 1024 * 1024
MESH = pl.DeviceIdType.MESH


def lanes(shape):
    return lax.broadcasted_iota(jnp.int32, shape, len(shape) - 1)


def rows_of(shape):
    return lax.broadcasted_iota(jnp.int32, shape, len(shape) - 2)


def sincos_turns(turns):
    r = turns - jnp.round(turns)
    r2 = r * r
    sin_c = [(-1) ** n * math.pi ** (2 * n + 1) / math.factorial(2 * n + 1) for n in range(7)]
    cos_c = [(-1) ** n * math.pi ** (2 * n) / math.factorial(2 * n) for n in range(7)]
    sh = jnp.full_like(r, sin_c[-1])
    ch = jnp.full_like(r, cos_c[-1])
    for n in range(5, -1, -1):
        sh = sh * r2 + sin_c[n]
        ch = ch * r2 + cos_c[n]
    sh = sh * r
    return 2.0 * sh * ch, 1.0 - 2.0 * sh * sh


def pack_kernel(counts, offsets, links, delay, angle, gain, out, store):
    for c in range(0, PATH_ROWS, 8):
        n = min(8, PATH_ROWS - c)
        for f, ref in ((0, delay), (1, angle)):
            value = ref[c : c + n, :]
            value = value * (1.0 / FRAME_TONES) if f == 0 else jnp.sin(value)
            store[pl.ds(8 * (c + 1) + f, n, stride=8), :] = value
            store[pl.ds(8 * c + 4 + f, n, stride=8), :] = value
    for q in range(PATH_ROWS):
        pair = gain[:, 128 * q : 128 * (q + 1)]
        store[8 * (q + 1) + 2 : 8 * (q + 1) + 4, :] = pair
        store[8 * q + 6 : 8 * q + 8, :] = pair

    def clear(i, carry):
        out[pl.ds(pl.multiple_of(64 * i, 64), 64), :] = jnp.zeros((64, 128), jnp.float32)
        return carry

    lax.fori_loop(0, HALF * 8 // 64, clear, 0)
    lane = lanes((8, 128))
    row = rows_of((8, 128))
    high = row >= 4
    place = lane + jnp.where(high, 128, 0)
    tag_place = jnp.where(row == 4, lane - TAG_LANE, -1000)
    half = my_half()

    def narrow(_, carry):
        low, top = carry
        mid = (low + top) >> 1
        below = (links[jnp.minimum(mid, SLOTS - 1)] >> 8) < HALF
        below = below & (low < top)
        return jnp.where(below, mid + 1, low), jnp.where(below, top, mid)

    split, _ = lax.fori_loop(0, 9, narrow, (jnp.int32(0), jnp.int32(SLOTS)))
    begin = jnp.where(half == 0, 0, split)
    end = jnp.where(half == 0, split, SLOTS)

    def one(r, carry):
        before, k, base, last = carry
        live = r < end
        r = jnp.minimum(r, SLOTS - 1)
        link = links[r]
        owner = jnp.where(live, (link >> 8) - half * HALF, HALF)
        same = owner == before
        k = jnp.where(same, k + 1, 0)
        base = jnp.where(same, base + last, 0)
        off = offsets[r]
        cnt = counts[r]
        q = off >> 7
        s = off & 127
        block = store[pl.ds(pl.multiple_of(8 * q + 8, 8), 8), :]
        turned = pltpu.roll(block, (base - s) & 127, 1)
        swapped = pltpu.roll(turned, 4, 0)
        j = place - base
        second = (j + s) >= 128
        value = jnp.where(second == high, turned, swapped)
        at = pl.ds(pl.multiple_of(8 * owner, 8), 8)
        new = jnp.where((j >= 0) & (j < cnt), value, out[at, :])
        new = jnp.where(tag_place == 2 * k, ((link & 255) + 1).astype(jnp.float32), new)
        new = jnp.where(tag_place == 2 * k + 1, cnt.astype(jnp.float32), new)
        out[at, :] = new
        return owner, k, base, cnt

    def eight(b, carry):
        for j in range(8):
            carry = one(begin + 8 * b + j, carry)
        return carry

    zero = jnp.int32(0)
    lax.fori_loop(0, (end - begin + 7) >> 3, eight, (jnp.int32(-1), zero, zero, zero))
    for c in range(0, HALF * 8, 64):
        extra = [out[pl.ds(c + 4 + f, 8, stride=8), :] for f in range(4)]
        total = extra[0]
        for f in range(1, 4):
            total = total + pltpu.roll(extra[f], 2 * f, 1)
        out[pl.ds(c + 4, 8, stride=8), :] = total


def my_half():
    return lax.rem(lax.axis_index("grp") + lax.axis_index("cell") // HALF, 2)


def exchange_kernel(sent, got, sems):
    me = lax.axis_index("cell")
    grp = lax.axis_index("grp")
    start = my_half() * HALF
    sibling = {"grp": 1 - grp}
    barrier = pltpu.get_barrier_semaphore()
    pl.semaphore_signal(barrier, inc=1, device_id=sibling, device_id_type=MESH)

    def greet(d, carry):
        other = start + lax.rem(me + d, HALF)
        pl.semaphore_signal(barrier, inc=1, device_id={"cell": other}, device_id_type=MESH)
        return carry

    lax.fori_loop(1 - grp, HALF, greet, 0)

    @pl.when(grp == 0)
    def _():
        got[me] = sent[lax.rem(me, HALF)]

    pl.semaphore_wait(barrier, HALF + grp)
    wire = pl.ds(0, WIRE_ROWS)

    def send(d, carry):
        near = lax.rem(me + d, HALF)
        pltpu.make_async_remote_copy(
            src_ref=sent.at[near, wire],
            dst_ref=got.at[me, wire],
            send_sem=sems.at[0],
            recv_sem=sems.at[1],
            device_id={"cell": start + near},
            device_id_type=MESH,
        ).start()
        return carry

    lax.fori_loop(1 - grp, HALF, send, 0)

    for g in range(2):

        @pl.when(grp == g)
        def _():
            whole = pltpu.make_async_remote_copy(
                src_ref=sent.at[pl.ds(0, HALF - 1 + g), wire],
                dst_ref=got.at[pl.ds(start, HALF - 1 + g), wire],
                send_sem=sems.at[0],
                recv_sem=sems.at[1],
                device_id=sibling,
                device_id_type=MESH,
            )
            whole.wait_recv()
            whole.wait_send()

    swap = pltpu.make_async_remote_copy(
        src_ref=got.at[pl.ds(start, HALF), wire],
        dst_ref=got.at[pl.ds(start, HALF), wire],
        send_sem=sems.at[2],
        recv_sem=sems.at[3],
        device_id=sibling,
        device_id_type=MESH,
    )
    swap.start()
    swap.wait()


def seeds_of(fields, grp, e_seed, s_seed, coef):
    turns, sine, real, imag = [v + pltpu.roll(v, 64, 1) for v in fields]
    hi = lanes((8, 128)) >= 64
    s1, c1 = sincos_turns(turns)
    e = jnp.where(hi, 0.0, 1.0)
    f = jnp.where(hi, 1.0, 0.0)
    e_seed[pl.ds(8, 8, stride=16), :] = e
    for j in range(1, 9):
        e, f = e * c1 - f * s1, f * c1 + e * s1
        if j < 8:
            e_seed[pl.ds(8 + j, 8, stride=16), :] = e
        e_seed[pl.ds(8 - j, 8, stride=16), :] = jnp.where(hi, -e, e)
    _, c8 = sincos_turns(8.0 * turns)
    coef[0:8, :] = 2.0 * c8
    sa, ca = sincos_turns(0.5 * sine)
    first = (grp * (ANT // 2)).astype(jnp.float32)
    s0, c0 = sincos_turns(first * sine)
    _, a8 = sincos_turns(4.0 * sine)
    coef[8:16, :] = 2.0 * a8
    g1 = jnp.where(hi, -imag, real)
    g2 = jnp.where(hi, real, imag)
    x = g1 * c0 + g2 * s0
    y = g2 * c0 - g1 * s0
    for a in range(16):
        s_seed[pl.ds(a, 8, stride=32), :] = x
        s_seed[pl.ds(16 + a, 8, stride=32), :] = y
        if a < 15:
            x, y = x * ca + y * sa, y * ca - x * sa


def response_of(l, e_seed, s_seed, coef):
    c = jnp.broadcast_to(coef[l : l + 1, :], (8, 128))
    low = e_seed[16 * l : 16 * l + 8, :]
    top = e_seed[16 * l + 8 : 16 * l + 16, :]
    down = [top, low]
    up = [low, top]
    for _ in range(7):
        down.append(c * down[-1] - down[-2])
        up.append(c * up[-1] - up[-2])
    table = jnp.concatenate(down[:0:-1] + up[1:], axis=0).astype(jnp.bfloat16)
    c = jnp.broadcast_to(coef[8 + l : 9 + l, :], (8, 128))
    parts = []
    for h in range(2):
        at = 32 * l + 16 * h
        run = [s_seed[at : at + 8, :], s_seed[at + 8 : at + 16, :]]
        for _ in range(2):
            run.append(c * run[-1] - run[-2])
        parts += run
    spread = jnp.concatenate(parts, axis=0).astype(jnp.bfloat16)
    return lax.dot_general(
        spread, table, (((1,), (1,)), ((), ())), preferred_element_type=jnp.float32
    )


SEED_SCRATCH = [
    pltpu.VMEM((8 * 16, 128), jnp.float32),
    pltpu.VMEM((8 * 32, 128), jnp.float32),
    pltpu.VMEM((16, 128), jnp.float32),
]


def transmit_kernel(
    slots, nearby, got, symbols, rows, weights, over, tag_v, tag_s, table, raw, serving, e_seed, s_seed, coef, sem
):
    me = lax.axis_index("cell")
    grp = lax.axis_index("grp")
    for c in range(0, CELLS, 8):
        extra = got[pl.ds(8 * c + 4, 8, stride=8), :]
        tag_v[c : c + 8, :] = jnp.where(lanes((8, 128)) >= TAG_LANE, extra, 0.0).astype(jnp.int32)
    copy = pltpu.make_async_copy(tag_v, tag_s, sem)
    copy.start()

    def clear(i, carry):
        raw[pl.ds(pl.multiple_of(64 * i, 64), 64), :] = jnp.zeros((64, 128), jnp.float32)
        return carry

    lax.fori_loop(0, CELL_SECTORS * RESP // 64, clear, 0)
    for c in range(0, CELLS, 8):
        extra = got[pl.ds(8 * c + 4, 8, stride=8), :]
        for f in range(4):
            over[pl.ds(8 * c + f, 8, stride=8), :] = extra if f == 0 else pltpu.roll(extra, 128 - 2 * f, 1)
    copy.wait()

    def index(i, carry):
        base = jnp.int32(0)
        for k in range(4):
            tag = tag_s[i, TAG_LANE + 2 * k]
            cnt = tag_s[i, TAG_LANE + 2 * k + 1]
            table[tag] = (i << 16) + (base << 8) + cnt
            base = base + cnt
        return carry

    lax.fori_loop(0, CELLS, index, 0, unroll=4)
    lane = lanes((8, 128))

    def unpack(g, carry):
        code = table[g + 1]
        i = code >> 16
        base = (code >> 8) & 255
        cnt = code & 255
        at = pl.ds(pl.multiple_of(8 * i, 8), 8)
        value = jnp.where(lane < base + cnt - 128, over[at, :], got[at, :])
        value = pltpu.roll(value, (0 - base) & 127, 1)
        rows[pl.ds(pl.multiple_of(8 * g, 8), 8), :] = jnp.where(lane < cnt, value, 0.0)
        return carry

    lax.fori_loop(0, LINKS, unpack, 0, unroll=8)

    def serve(u, carry):
        link = u * NEARBY_COUNT + slots[u]
        serving[pl.ds(pl.multiple_of(8 * u, 8), 8), :] = rows[pl.ds(pl.multiple_of(8 * link, 8), 8), :]
        return carry

    lax.fori_loop(0, USERS, serve, 0, unroll=8)

    def eight_users(c, carry):
        fields = [serving[pl.ds(64 * c + f, 8, stride=8), :] for f in range(4)]
        seeds_of(fields, grp, e_seed, s_seed, coef)
        for l in range(8):
            u = 8 * c + l
            resp = response_of(l, e_seed, s_seed, coef).astype(jnp.bfloat16).astype(jnp.float32)
            sym = symbols[u].astype(jnp.float32)
            sym_r, sym_i = sym[0:1, :], sym[1:2, :]
            real, imag = resp[:ANT, :], resp[ANT:, :]
            part = jnp.concatenate(
                [real * sym_r + imag * sym_i, real * sym_i - imag * sym_r], axis=0
            )
            sector = nearby[slots[u], u] - me * CELL_SECTORS
            at = pl.ds(pl.multiple_of(RESP * sector, RESP), RESP)
            raw[at, :] = raw[at, :] + part
        return carry

    lax.fori_loop(0, USERS // 8, eight_users, 0)

    def normalise(s, carry):
        at = pl.ds(pl.multiple_of(RESP * s, RESP), RESP)
        value = raw[at, :]
        real, imag = value[:ANT, :], value[ANT:, :]
        power = jnp.mean(real * real + imag * imag, axis=1, keepdims=True)
        scale = 1.0 / jnp.sqrt(power + EPSILON)
        weights[s] = jnp.concatenate([real * scale, imag * scale], axis=0).astype(jnp.bfloat16)
        return carry

    lax.fori_loop(0, CELL_SECTORS, normalise, 0, unroll=2)


def receive_kernel(
    nearby, rows, weights, out, near, resp, part, other,
    e_seed, s_seed, coef, e_seed2, s_seed2, coef2, sems
):
    me = lax.axis_index("cell")
    grp = lax.axis_index("grp")
    right = lax.rem(me + 1, CELLS)
    left = lax.rem(me + CELLS - 1, CELLS)
    barrier = pltpu.get_barrier_semaphore()
    for target in ({"cell": left}, {"cell": right}, {"grp": 1 - grp}):
        pl.semaphore_signal(barrier, inc=1, device_id=target, device_id_type=MESH)
    pl.semaphore_wait(barrier, 3)
    to_right = pltpu.make_async_remote_copy(
        src_ref=weights.at[pl.ds(CELL_SECTORS - REACH, REACH)],
        dst_ref=near.at[pl.ds(0, REACH)],
        send_sem=sems.at[0],
        recv_sem=sems.at[1],
        device_id={"cell": right},
        device_id_type=MESH,
    )
    to_left = pltpu.make_async_remote_copy(
        src_ref=weights.at[pl.ds(0, REACH)],
        dst_ref=near.at[pl.ds(REACH + CELL_SECTORS, REACH)],
        send_sem=sems.at[2],
        recv_sem=sems.at[3],
        device_id={"cell": left},
        device_id_type=MESH,
    )
    to_right.start()
    to_left.start()
    keep = pltpu.make_async_copy(weights, near.at[pl.ds(REACH, CELL_SECTORS)], sems.at[4])
    keep.start()

    first, second = (e_seed, s_seed, coef), (e_seed2, s_seed2, coef2)

    def prepare(u, seeds):
        fields = [rows[pl.ds(pl.multiple_of(64 * u, 64) + f, 8, stride=8), :] for f in range(4)]
        seeds_of(fields, grp, *seeds)

    def respond(u, seeds):
        for l in range(8):
            at = pl.ds(pl.multiple_of(u * (8 * RESP) + RESP * l, RESP), RESP)
            resp[at, :] = response_of(l, *seeds).astype(jnp.bfloat16)

    def two_users(v, carry):
        prepare(2 * v + 1, second)
        respond(2 * v, first)
        prepare(jnp.minimum(2 * v + 2, USERS - 1), first)
        respond(2 * v + 1, second)
        return carry

    prepare(0, first)
    lax.fori_loop(0, USERS // 2, two_users, 0)
    keep.wait()
    to_right.wait()
    to_left.wait()

    def combine(u, carry):
        real = jnp.zeros((ANT, 128), jnp.float32)
        imag = jnp.zeros((ANT, 128), jnp.float32)
        for k in range(NEARBY_COUNT):
            sector = nearby[k, u] - me * CELL_SECTORS + REACH
            sector = jnp.clip(sector, 0, CELL_SECTORS + 2 * REACH - 1)
            tx = near[sector].astype(jnp.float32)
            at = pl.ds(pl.multiple_of(u * (8 * RESP) + RESP * k, RESP), RESP)
            ch = resp[at, :].astype(jnp.float32)
            real = real + (ch[:ANT] * tx[:ANT] - ch[ANT:] * tx[ANT:])
            imag = imag + (ch[:ANT] * tx[ANT:] + ch[ANT:] * tx[:ANT])
        part[u] = jnp.concatenate(
            [jnp.sum(real, axis=0, keepdims=True), jnp.sum(imag, axis=0, keepdims=True)], axis=0
        )
        return carry

    lax.fori_loop(0, USERS, combine, 0)
    swap = pltpu.make_async_remote_copy(
        src_ref=part,
        dst_ref=other,
        send_sem=sems.at[5],
        recv_sem=sems.at[6],
        device_id={"grp": 1 - grp},
        device_id_type=MESH,
    )
    swap.start()
    swap.wait()
    out[...] = (part[...] + other[...]) * (1.0 / math.sqrt(SECTOR_ANTENNAS))


VMEM = pl.BlockSpec(memory_space=pltpu.VMEM)
SMEM = pl.BlockSpec(memory_space=pltpu.SMEM)


def call(kernel, name, mib, out_shape, in_specs, scratch, remote=None):
    extra = {} if remote is None else {"collective_id": remote, "has_side_effects": True}
    many = isinstance(out_shape, (tuple, list))
    return pl.pallas_call(
        kernel,
        name=name,
        out_shape=out_shape,
        in_specs=in_specs,
        out_specs=[VMEM] * len(out_shape) if many else VMEM,
        scratch_shapes=scratch,
        compiler_params=pltpu.CompilerParams(vmem_limit_bytes=mib * MIB, **extra),
    )


def shards(
    path_delay,
    path_angle,
    path_gain,
    slot_counts,
    slot_offsets,
    ray_link,
    nearby_sectors,
    serving_slot,
    symbols,
):
    f32, bf16, i32 = jnp.float32, jnp.bfloat16, jnp.int32
    sent = call(
        pack_kernel,
        "pack",
        60,
        jax.ShapeDtypeStruct(((HALF + 1) * 8, 128), f32),
        [SMEM, SMEM, SMEM, VMEM, VMEM, VMEM],
        [pltpu.VMEM((8 * (PATH_ROWS + 1), 128), f32)],
    )(
        slot_counts,
        slot_offsets,
        ray_link,
        path_delay.reshape(PATH_ROWS, 128),
        path_angle.reshape(PATH_ROWS, 128),
        path_gain,
    )
    got = call(
        exchange_kernel,
        "exchange",
        16,
        jax.ShapeDtypeStruct((CELLS, 8, 128), f32),
        [VMEM],
        [pltpu.SemaphoreType.DMA((4,))],
        remote=0,
    )(sent.reshape(HALF + 1, 8, 128))
    rows, weights = call(
        transmit_kernel,
        "transmit",
        24,
        (
            jax.ShapeDtypeStruct((LINKS * 8, 128), f32),
            jax.ShapeDtypeStruct((CELL_SECTORS, RESP, 128), bf16),
        ),
        [SMEM, SMEM, VMEM, VMEM],
        [
            pltpu.VMEM((CELLS * 8, 128), f32),
            pltpu.VMEM((CELLS, 128), i32),
            pltpu.SMEM((CELLS, 128), i32),
            pltpu.SMEM((LINKS + 8,), i32),
            pltpu.VMEM((CELL_SECTORS * RESP, 128), f32),
            pltpu.VMEM((USERS * 8, 128), f32),
            *SEED_SCRATCH,
            pltpu.SemaphoreType.DMA,
        ],
    )(serving_slot, nearby_sectors, got.reshape(CELLS * 8, 128), symbols)
    return call(
        receive_kernel,
        "receive",
        24,
        jax.ShapeDtypeStruct((USERS, 2, FRAME_TONES), f32),
        [SMEM, VMEM, VMEM],
        [
            pltpu.VMEM((CELL_SECTORS + 2 * REACH, RESP, 128), bf16),
            pltpu.VMEM((LINKS * RESP, 128), bf16),
            pltpu.VMEM((USERS, 2, FRAME_TONES), f32),
            pltpu.VMEM((USERS, 2, FRAME_TONES), f32),
            *SEED_SCRATCH,
            *SEED_SCRATCH,
            pltpu.SemaphoreType.DMA((7,)),
        ],
        remote=1,
    )(nearby_sectors, rows, weights)


def solution(mesh):
    placed = (
        P("cell"),
        P("cell"),
        P(None, "cell"),
        P("cell"),
        P("cell"),
        P("cell"),
        P(None, "cell"),
        P("cell"),
        P("cell", None, None),
    )
    return jax.shard_map(
        shards, mesh=mesh, in_specs=placed, out_specs=P("cell", None, None), check_vma=False
    )
```

```python
import functools
import math

import jax
import jax.numpy as jnp
from jax import lax
from jax.experimental import pallas as pl
from jax.experimental.pallas import tpu as pltpu
from jax.sharding import PartitionSpec as P

SECTOR_ANTENNAS = 64
FRAME_TONES = 128
NEARBY_COUNT = 8
CELL_SECTORS = 32
REACH = 16
EPSILON = 1e-06

CELLS = 128
SLOTS = 256
USERS = 32
LINKS = USERS * NEARBY_COUNT
PATH_ROWS = 65
ANT = SECTOR_ANTENNAS // 2
RESP = 2 * ANT
TAG_LANE = 8
HALF = CELLS // 2
WIRE_ROWS = 5
MIB = 1024 * 1024
MESH = pl.DeviceIdType.MESH


def lanes(shape):
    return lax.broadcasted_iota(jnp.int32, shape, len(shape) - 1)


def rows_of(shape):
    return lax.broadcasted_iota(jnp.int32, shape, len(shape) - 2)


def sincos_turns(turns):
    r = turns - jnp.round(turns)
    r2 = r * r
    sin_c = [(-1) ** n * math.pi ** (2 * n + 1) / math.factorial(2 * n + 1) for n in range(7)]
    cos_c = [(-1) ** n * math.pi ** (2 * n) / math.factorial(2 * n) for n in range(7)]
    sh = jnp.full_like(r, sin_c[-1])
    ch = jnp.full_like(r, cos_c[-1])
    for n in range(5, -1, -1):
        sh = sh * r2 + sin_c[n]
        ch = ch * r2 + cos_c[n]
    sh = sh * r
    return 2.0 * sh * ch, 1.0 - 2.0 * sh * sh


def pack_kernel(counts, offsets, links, delay, angle, gain, out, store):
    for c in range(0, PATH_ROWS, 8):
        n = min(8, PATH_ROWS - c)
        for f, ref in ((0, delay), (1, angle)):
            value = ref[c : c + n, :]
            value = value * (1.0 / FRAME_TONES) if f == 0 else jnp.sin(value)
            store[pl.ds(8 * (c + 1) + f, n, stride=8), :] = value
            store[pl.ds(8 * c + 4 + f, n, stride=8), :] = value
    for q in range(PATH_ROWS):
        pair = gain[:, 128 * q : 128 * (q + 1)]
        store[8 * (q + 1) + 2 : 8 * (q + 1) + 4, :] = pair
        store[8 * q + 6 : 8 * q + 8, :] = pair

    def clear(i, carry):
        out[pl.ds(pl.multiple_of(64 * i, 64), 64), :] = jnp.zeros((64, 128), jnp.float32)
        return carry

    lax.fori_loop(0, HALF * 8 // 64, clear, 0)
    lane = lanes((8, 128))
    row = rows_of((8, 128))
    high = row >= 4
    place = lane + jnp.where(high, 128, 0)
    tag_place = jnp.where(row == 4, lane - TAG_LANE, -1000)
    half = my_half()

    def narrow(_, carry):
        low, top = carry
        mid = (low + top) >> 1
        below = (links[jnp.minimum(mid, SLOTS - 1)] >> 8) < HALF
        below = below & (low < top)
        return jnp.where(below, mid + 1, low), jnp.where(below, top, mid)

    split, _ = lax.fori_loop(0, 9, narrow, (jnp.int32(0), jnp.int32(SLOTS)))
    begin = jnp.where(half == 0, 0, split)
    end = jnp.where(half == 0, split, SLOTS)

    def one(r, carry):
        before, k, base, last = carry
        live = r < end
        r = jnp.minimum(r, SLOTS - 1)
        link = links[r]
        owner = jnp.where(live, (link >> 8) - half * HALF, HALF)
        same = owner == before
        k = jnp.where(same, k + 1, 0)
        base = jnp.where(same, base + last, 0)
        off = offsets[r]
        cnt = counts[r]
        q = off >> 7
        s = off & 127
        block = store[pl.ds(pl.multiple_of(8 * q + 8, 8), 8), :]
        turned = pltpu.roll(block, (base - s) & 127, 1)
        swapped = pltpu.roll(turned, 4, 0)
        j = place - base
        second = (j + s) >= 128
        value = jnp.where(second == high, turned, swapped)
        at = pl.ds(pl.multiple_of(8 * owner, 8), 8)
        new = jnp.where((j >= 0) & (j < cnt), value, out[at, :])
        new = jnp.where(tag_place == 2 * k, ((link & 255) + 1).astype(jnp.float32), new)
        new = jnp.where(tag_place == 2 * k + 1, cnt.astype(jnp.float32), new)
        out[at, :] = new
        return owner, k, base, cnt

    def eight(b, carry):
        for j in range(8):
            carry = one(begin + 8 * b + j, carry)
        return carry

    zero = jnp.int32(0)
    lax.fori_loop(0, (end - begin + 7) >> 3, eight, (jnp.int32(-1), zero, zero, zero))
    for c in range(0, HALF * 8, 64):
        extra = [out[pl.ds(c + 4 + f, 8, stride=8), :] for f in range(4)]
        total = extra[0]
        for f in range(1, 4):
            total = total + pltpu.roll(extra[f], 2 * f, 1)
        out[pl.ds(c + 4, 8, stride=8), :] = total


def my_half():
    return lax.rem(lax.axis_index("grp") + lax.axis_index("cell") // HALF, 2)


def exchange_kernel(sent, got, sems):
    me = lax.axis_index("cell")
    grp = lax.axis_index("grp")
    start = my_half() * HALF
    sibling = {"grp": 1 - grp}
    barrier = pltpu.get_barrier_semaphore()
    pl.semaphore_signal(barrier, inc=1, device_id=sibling, device_id_type=MESH)

    def greet(d, carry):
        other = start + lax.rem(me + d, HALF)
        pl.semaphore_signal(barrier, inc=1, device_id={"cell": other}, device_id_type=MESH)
        return carry

    lax.fori_loop(1 - grp, HALF, greet, 0)

    @pl.when(grp == 0)
    def _():
        got[me] = sent[lax.rem(me, HALF)]

    pl.semaphore_wait(barrier, HALF + grp)
    wire = pl.ds(0, WIRE_ROWS)

    def send(d, carry):
        near = lax.rem(me + d, HALF)
        pltpu.make_async_remote_copy(
            src_ref=sent.at[near, wire],
            dst_ref=got.at[me, wire],
            send_sem=sems.at[0],
            recv_sem=sems.at[1],
            device_id={"cell": start + near},
            device_id_type=MESH,
        ).start()
        return carry

    lax.fori_loop(1 - grp, HALF, send, 0)

    for g in range(2):

        @pl.when(grp == g)
        def _():
            whole = pltpu.make_async_remote_copy(
                src_ref=sent.at[pl.ds(0, HALF - 1 + g), wire],
                dst_ref=got.at[pl.ds(start, HALF - 1 + g), wire],
                send_sem=sems.at[0],
                recv_sem=sems.at[1],
                device_id=sibling,
                device_id_type=MESH,
            )
            whole.wait_recv()
            whole.wait_send()

    swap = pltpu.make_async_remote_copy(
        src_ref=got.at[pl.ds(start, HALF), wire],
        dst_ref=got.at[pl.ds(start, HALF), wire],
        send_sem=sems.at[2],
        recv_sem=sems.at[3],
        device_id=sibling,
        device_id_type=MESH,
    )
    swap.start()
    swap.wait()


def seeds_of(fields, grp, e_seed, s_seed, coef):
    turns, sine, real, imag = [v + pltpu.roll(v, 64, 1) for v in fields]
    hi = lanes((8, 128)) >= 64
    s1, c1 = sincos_turns(turns)
    e = jnp.where(hi, 0.0, 1.0)
    f = jnp.where(hi, 1.0, 0.0)
    e_seed[pl.ds(8, 8, stride=16), :] = e
    for j in range(1, 9):
        e, f = e * c1 - f * s1, f * c1 + e * s1
        if j < 8:
            e_seed[pl.ds(8 + j, 8, stride=16), :] = e
        e_seed[pl.ds(8 - j, 8, stride=16), :] = jnp.where(hi, -e, e)
    _, c8 = sincos_turns(8.0 * turns)
    coef[0:8, :] = 2.0 * c8
    sa, ca = sincos_turns(0.5 * sine)
    first = (grp * (ANT // 2)).astype(jnp.float32)
    s0, c0 = sincos_turns(first * sine)
    _, a8 = sincos_turns(4.0 * sine)
    coef[8:16, :] = 2.0 * a8
    g1 = jnp.where(hi, -imag, real)
    g2 = jnp.where(hi, real, imag)
    x = g1 * c0 + g2 * s0
    y = g2 * c0 - g1 * s0
    for a in range(16):
        s_seed[pl.ds(a, 8, stride=32), :] = x
        s_seed[pl.ds(16 + a, 8, stride=32), :] = y
        if a < 15:
            x, y = x * ca + y * sa, y * ca - x * sa


def response_of(l, e_seed, s_seed, coef):
    c = jnp.broadcast_to(coef[l : l + 1, :], (8, 128))
    low = e_seed[16 * l : 16 * l + 8, :]
    top = e_seed[16 * l + 8 : 16 * l + 16, :]
    down = [top, low]
    up = [low, top]
    for _ in range(7):
        down.append(c * down[-1] - down[-2])
        up.append(c * up[-1] - up[-2])
    table = jnp.concatenate(down[:0:-1] + up[1:], axis=0).astype(jnp.bfloat16)
    c = jnp.broadcast_to(coef[8 + l : 9 + l, :], (8, 128))
    parts = []
    for h in range(2):
        at = 32 * l + 16 * h
        run = [s_seed[at : at + 8, :], s_seed[at + 8 : at + 16, :]]
        for _ in range(2):
            run.append(c * run[-1] - run[-2])
        parts += run
    spread = jnp.concatenate(parts, axis=0).astype(jnp.bfloat16)
    return lax.dot_general(
        spread, table, (((1,), (1,)), ((), ())), preferred_element_type=jnp.float32
    )


SEED_SCRATCH = [
    pltpu.VMEM((8 * 16, 128), jnp.float32),
    pltpu.VMEM((8 * 32, 128), jnp.float32),
    pltpu.VMEM((16, 128), jnp.float32),
]


def unpacked(code, got, over):
    source = code >> 16
    base = (code >> 8) & 255
    cnt = code & 255
    lane = lanes((8, 128))
    value = jnp.where(lane < base + cnt - 128, over[source], got[source])
    return jnp.where(lane < cnt, pltpu.roll(value, (0 - base) & 127, 1), 0.0)


def transmit_kernel(
    slots, nearby, got, symbols, over, table, raw, table_s, serving, e_seed, s_seed, coef, sem
):
    me = lax.axis_index("cell")
    grp = lax.axis_index("grp")
    lane = lanes((8, 128))
    row = rows_of((8, 128))
    is_tag = (lane >= TAG_LANE) & (lane < TAG_LANE + 8) & (lax.rem(lane, 2) == 0)
    link = (lane + 1).astype(jnp.float32)
    found = [jnp.zeros((8, 128), jnp.float32) for _ in range(LINKS // 128)]
    for c in range(CELLS // 8):
        extra = got[8 * c : 8 * c + 8, 4, :]
        for f in range(4):
            over[8 * c : 8 * c + 8, f, :] = extra if f == 0 else pltpu.roll(extra, 128 - 2 * f, 1)
        cnt = jnp.where(is_tag, pltpu.roll(extra, 127, 1), 0.0)
        base = pltpu.roll(cnt, 2, 1) + pltpu.roll(cnt, 4, 1) + pltpu.roll(cnt, 6, 1)
        code = (8 * c + row).astype(jnp.float32) * 65536.0 + base * 256.0 + cnt
        for k in range(4):
            at = TAG_LANE + 2 * k
            tags = jnp.broadcast_to(extra[:, at : at + 1], (8, 128))
            codes = jnp.broadcast_to(code[:, at : at + 1], (8, 128))
            for h in range(LINKS // 128):
                found[h] = found[h] + jnp.where(tags == link + 128.0 * h, codes, 0.0)
    for h in range(LINKS // 128):
        table[h : h + 1, :] = jnp.sum(found[h], axis=0, keepdims=True).astype(jnp.int32)
    copy = pltpu.make_async_copy(table, table_s, sem)
    copy.start()

    def clear(i, carry):
        raw[i] = jnp.zeros((RESP, 128), jnp.float32)
        return carry

    lax.fori_loop(0, CELL_SECTORS, clear, 0, unroll=4)
    copy.wait()

    def serve(u, carry):
        g = u * NEARBY_COUNT + slots[u]
        code = table_s[g >> 7, g & 127]
        serving[pl.ds(pl.multiple_of(8 * u, 8), 8), :] = unpacked(code, got, over)
        return carry

    lax.fori_loop(0, USERS, serve, 0, unroll=8)

    def eight_users(c, carry):
        fields = [serving[pl.ds(64 * c + f, 8, stride=8), :] for f in range(4)]
        seeds_of(fields, grp, e_seed, s_seed, coef)
        for l in range(8):
            u = 8 * c + l
            resp = response_of(l, e_seed, s_seed, coef).astype(jnp.bfloat16).astype(jnp.float32)
            sym = symbols[u].astype(jnp.float32)
            sym_r, sym_i = sym[0:1, :], sym[1:2, :]
            real, imag = resp[:ANT, :], resp[ANT:, :]
            part = jnp.concatenate(
                [real * sym_r + imag * sym_i, real * sym_i - imag * sym_r], axis=0
            )
            sector = nearby[slots[u], u] - me * CELL_SECTORS
            raw[sector] = raw[sector] + part
        return carry

    lax.fori_loop(0, USERS // 8, eight_users, 0)


PIECE = 8
PIECES = (0, 16, 8, 24)


def receive_kernel(
    nearby, table, got, over, raw, out, near, resp, part, other,
    e_seed, s_seed, coef, e_seed2, s_seed2, coef2, rows, rows2, send_sems, recv_sems
):
    me = lax.axis_index("cell")
    grp = lax.axis_index("grp")
    right = lax.rem(me + 1, CELLS)
    left = lax.rem(me + CELLS - 1, CELLS)
    barrier = pltpu.get_barrier_semaphore()
    for target in ({"cell": left}, {"cell": right}, {"grp": 1 - grp}):
        pl.semaphore_signal(barrier, inc=1, device_id=target, device_id_type=MESH)

    halo = []
    for n, begin in enumerate(PIECES):

        def normalise(s, carry):
            real, imag = raw[s, :ANT, :], raw[s, ANT:, :]
            power = jnp.mean(real * real + imag * imag, axis=1, keepdims=True)
            scale = 1.0 / jnp.sqrt(power + EPSILON)
            near[REACH + s] = jnp.concatenate([real * scale, imag * scale], axis=0).astype(jnp.bfloat16)
            return carry

        lax.fori_loop(begin, begin + PIECE, normalise, 0, unroll=4)
        if n == 0:
            pl.semaphore_wait(barrier, 3)
        to_left = begin < CELL_SECTORS - REACH
        land = begin + REACH + CELL_SECTORS if to_left else begin + REACH - CELL_SECTORS
        halo.append(
            pltpu.make_async_remote_copy(
                src_ref=near.at[pl.ds(REACH + begin, PIECE)],
                dst_ref=near.at[pl.ds(land, PIECE)],
                send_sem=send_sems.at[n],
                recv_sem=recv_sems.at[n],
                device_id={"cell": left if to_left else right},
                device_id_type=MESH,
            )
        )
        halo[-1].start()

    first, second = (e_seed, s_seed, coef), (e_seed2, s_seed2, coef2)

    def unpack(u, rows):
        u = jnp.minimum(u, USERS - 1)
        for l in range(8):
            code = table[u // 16, lax.rem(u, 16) * 8 + l]
            rows[8 * l : 8 * l + 8, :] = unpacked(code, got, over)

    def prepare(rows, seeds):
        seeds_of([rows[pl.ds(f, 8, stride=8), :] for f in range(4)], grp, *seeds)

    def respond(u, seeds):
        for l in range(8):
            at = pl.ds(pl.multiple_of(u * (8 * RESP) + RESP * l, RESP), RESP)
            resp[at, :] = response_of(l, *seeds).astype(jnp.bfloat16)

    def two_users(v, carry):
        prepare(rows2, second)
        unpack(2 * v + 3, rows2)
        respond(2 * v, first)
        prepare(rows, first)
        unpack(2 * v + 4, rows)
        respond(2 * v + 1, second)
        return carry

    unpack(0, rows)
    prepare(rows, first)
    unpack(1, rows2)
    unpack(2, rows)
    lax.fori_loop(0, USERS // 2, two_users, 0)
    for copy in halo:
        copy.wait()

    def combine(u, carry):
        real = jnp.zeros((ANT, 128), jnp.float32)
        imag = jnp.zeros((ANT, 128), jnp.float32)
        for k in range(NEARBY_COUNT):
            sector = nearby[k, u] - me * CELL_SECTORS + REACH
            sector = jnp.clip(sector, 0, CELL_SECTORS + 2 * REACH - 1)
            tx = near[sector].astype(jnp.float32)
            at = pl.ds(pl.multiple_of(u * (8 * RESP) + RESP * k, RESP), RESP)
            ch = resp[at, :].astype(jnp.float32)
            real = real + (ch[:ANT] * tx[:ANT] - ch[ANT:] * tx[ANT:])
            imag = imag + (ch[:ANT] * tx[ANT:] + ch[ANT:] * tx[:ANT])
        part[u] = jnp.concatenate(
            [jnp.sum(real, axis=0, keepdims=True), jnp.sum(imag, axis=0, keepdims=True)], axis=0
        )
        return carry

    lax.fori_loop(0, USERS, combine, 0)
    swap = pltpu.make_async_remote_copy(
        src_ref=part,
        dst_ref=other,
        send_sem=send_sems.at[len(PIECES)],
        recv_sem=recv_sems.at[len(PIECES)],
        device_id={"grp": 1 - grp},
        device_id_type=MESH,
    )
    swap.start()
    swap.wait()
    out[...] = (part[...] + other[...]) * (1.0 / math.sqrt(SECTOR_ANTENNAS))


VMEM = pl.BlockSpec(memory_space=pltpu.VMEM)
SMEM = pl.BlockSpec(memory_space=pltpu.SMEM)


def call(kernel, name, mib, out_shape, in_specs, scratch, remote=None):
    extra = {} if remote is None else {"collective_id": remote, "has_side_effects": True}
    many = isinstance(out_shape, (tuple, list))
    return pl.pallas_call(
        kernel,
        name=name,
        out_shape=out_shape,
        in_specs=in_specs,
        out_specs=[VMEM] * len(out_shape) if many else VMEM,
        scratch_shapes=scratch,
        compiler_params=pltpu.CompilerParams(vmem_limit_bytes=mib * MIB, **extra),
    )


def shards(
    path_delay,
    path_angle,
    path_gain,
    slot_counts,
    slot_offsets,
    ray_link,
    nearby_sectors,
    serving_slot,
    symbols,
):
    f32, bf16, i32 = jnp.float32, jnp.bfloat16, jnp.int32
    sent = call(
        pack_kernel,
        "pack",
        60,
        jax.ShapeDtypeStruct(((HALF + 1) * 8, 128), f32),
        [SMEM, SMEM, SMEM, VMEM, VMEM, VMEM],
        [pltpu.VMEM((8 * (PATH_ROWS + 1), 128), f32)],
    )(
        slot_counts,
        slot_offsets,
        ray_link,
        path_delay.reshape(PATH_ROWS, 128),
        path_angle.reshape(PATH_ROWS, 128),
        path_gain,
    )
    got = call(
        exchange_kernel,
        "exchange",
        16,
        jax.ShapeDtypeStruct((CELLS, 8, 128), f32),
        [VMEM],
        [pltpu.SemaphoreType.DMA((4,))],
        remote=0,
    )(sent.reshape(HALF + 1, 8, 128))
    over, table, raw = call(
        transmit_kernel,
        "transmit",
        24,
        (
            jax.ShapeDtypeStruct((CELLS, 8, 128), f32),
            jax.ShapeDtypeStruct((LINKS // 128, 128), i32),
            jax.ShapeDtypeStruct((CELL_SECTORS, RESP, 128), f32),
        ),
        [SMEM, SMEM, VMEM, VMEM],
        [
            pltpu.SMEM((LINKS // 128, 128), i32),
            pltpu.VMEM((USERS * 8, 128), f32),
            *SEED_SCRATCH,
            pltpu.SemaphoreType.DMA,
        ],
    )(serving_slot, nearby_sectors, got, symbols)
    return call(
        receive_kernel,
        "receive",
        24,
        jax.ShapeDtypeStruct((USERS, 2, FRAME_TONES), f32),
        [SMEM, SMEM, VMEM, VMEM, VMEM],
        [
            pltpu.VMEM((CELL_SECTORS + 2 * REACH, RESP, 128), bf16),
            pltpu.VMEM((LINKS * RESP, 128), bf16),
            pltpu.VMEM((USERS, 2, FRAME_TONES), f32),
            pltpu.VMEM((USERS, 2, FRAME_TONES), f32),
            *SEED_SCRATCH,
            *SEED_SCRATCH,
            pltpu.VMEM((64, 128), f32),
            pltpu.VMEM((64, 128), f32),
            pltpu.SemaphoreType.DMA((len(PIECES) + 1,)),
            pltpu.SemaphoreType.DMA((len(PIECES) + 1,)),
        ],
        remote=1,
    )(nearby_sectors, table, got, over, raw)


def solution(mesh):
    placed = (
        P("cell"),
        P("cell"),
        P(None, "cell"),
        P("cell"),
        P("cell"),
        P("cell"),
        P(None, "cell"),
        P("cell"),
        P("cell", None, None),
    )
    return jax.shard_map(
        shards, mesh=mesh, in_specs=placed, out_specs=P("cell", None, None), check_vma=False
    )
```

```python
import functools
import math

import jax
import jax.numpy as jnp
from jax import lax
from jax.experimental import pallas as pl
from jax.experimental.pallas import tpu as pltpu
from jax.sharding import PartitionSpec as P

SECTOR_ANTENNAS = 64
FRAME_TONES = 128
NEARBY_COUNT = 8
CELL_SECTORS = 32
REACH = 16
EPSILON = 1e-06

CELLS = 128
SLOTS = 256
USERS = 32
LINKS = USERS * NEARBY_COUNT
PATH_ROWS = 65
ANT = SECTOR_ANTENNAS // 2
RESP = 2 * ANT
TAG_LANE = 8
HALF = CELLS // 2
WIRE_ROWS = 5
MIB = 1024 * 1024
MESH = pl.DeviceIdType.MESH


def lanes(shape):
    return lax.broadcasted_iota(jnp.int32, shape, len(shape) - 1)


def rows_of(shape):
    return lax.broadcasted_iota(jnp.int32, shape, len(shape) - 2)


def sincos_turns(turns):
    r = turns - jnp.round(turns)
    r2 = r * r
    sin_c = [(-1) ** n * math.pi ** (2 * n + 1) / math.factorial(2 * n + 1) for n in range(7)]
    cos_c = [(-1) ** n * math.pi ** (2 * n) / math.factorial(2 * n) for n in range(7)]
    sh = jnp.full_like(r, sin_c[-1])
    ch = jnp.full_like(r, cos_c[-1])
    for n in range(5, -1, -1):
        sh = sh * r2 + sin_c[n]
        ch = ch * r2 + cos_c[n]
    sh = sh * r
    return 2.0 * sh * ch, 1.0 - 2.0 * sh * sh


def my_half():
    return lax.rem(lax.axis_index("grp") + lax.axis_index("cell") // HALF, 2)


def deliver_kernel(
    counts, offsets, links, delay_in, angle_in, gain_in, got,
    delay, angle, gain, store, sent, begins, load_sems, sems
):
    me = lax.axis_index("cell")
    grp = lax.axis_index("grp")
    start = my_half() * HALF
    sibling = {"grp": 1 - grp}
    loads = [
        pltpu.make_async_copy(src, dst, load_sems.at[n])
        for n, (src, dst) in enumerate(((delay_in, delay), (angle_in, angle), (gain_in, gain)))
    ]
    for copy in loads:
        copy.start()
    barrier = pltpu.get_barrier_semaphore()
    pl.semaphore_signal(barrier, inc=1, device_id=sibling, device_id_type=MESH)

    def greet(d, carry):
        other = start + lax.rem(me + d, HALF)
        pl.semaphore_signal(barrier, inc=1, device_id={"cell": other}, device_id_type=MESH)
        return carry

    lax.fori_loop(1 - grp, HALF, greet, 0)

    def narrow(_, carry):
        low, top = carry
        mid = (low + top) >> 1
        below = (links[jnp.minimum(mid, SLOTS - 1)] >> 8) < start
        below = below & (low < top)
        return jnp.where(below, mid + 1, low), jnp.where(below, top, mid)

    at, _ = lax.fori_loop(0, 9, narrow, (jnp.int32(0), jnp.int32(SLOTS)))

    def count(o, at):
        begins[o] = at
        total = at
        for k in range(4):
            slot = at + k
            mine = (links[jnp.minimum(slot, SLOTS - 1)] >> 8) == start + o
            total = total + jnp.where(mine & (slot < SLOTS), 1, 0)
        return total

    begins[HALF] = lax.fori_loop(0, HALF, count, at, unroll=4)

    for copy in loads:
        copy.wait()
    for c in range(0, PATH_ROWS, 8):
        n = min(8, PATH_ROWS - c)
        for f, ref in ((0, delay), (1, angle)):
            value = ref[c : c + n, :]
            value = value * (1.0 / FRAME_TONES) if f == 0 else jnp.sin(value)
            store[c : c + n, f, :] = value
            store[c : c + n, 4 + f, :] = value
    for q in range(PATH_ROWS):
        pair = gain[:, 128 * q : 128 * (q + 1)]
        store[q, 2:4, :] = pair
        store[q, 6:8, :] = pair
    store[PATH_ROWS] = jnp.zeros((8, 128), jnp.float32)

    lane = lanes((8, 128))
    row = rows_of((8, 128))
    place = lane + jnp.where(row >= 4, 128, 0)
    tag_place = jnp.where(row == 4, lane - TAG_LANE, -1000)

    def pack(o, carry):
        first = begins[o]
        number = begins[o + 1] - first
        base = jnp.int32(0)
        message = jnp.zeros((8, 128), jnp.float32)
        for k in range(4):
            r = jnp.minimum(first + k, SLOTS - 1)
            cnt = jnp.where(k < number, counts[r], 0)
            tag = jnp.where(k < number, (links[r] & 255) + 1, 0)
            off = offsets[r]
            q = off >> 7
            s = off & 127
            value = jnp.where(lane < s + cnt - 128, store[q + 1], store[q])
            value = pltpu.roll(value, (base - s) & 127, 1)
            j = place - base
            message = jnp.where((j >= 0) & (j < cnt), value, message)
            message = jnp.where(tag_place == 2 * k, tag.astype(jnp.float32), message)
            message = jnp.where(tag_place == 2 * k + 1, cnt.astype(jnp.float32), message)
            base = base + cnt
        sent[o] = message
        return carry

    lax.fori_loop(0, HALF, pack, 0, unroll=4)
    for c in range(0, HALF, 8):
        total = sent[c : c + 8, 4, :]
        for f in range(1, 4):
            total = total + pltpu.roll(sent[c : c + 8, 4 + f, :], 2 * f, 1)
        sent[c : c + 8, 4, :] = total

    @pl.when(grp == 0)
    def _():
        got[me] = sent[lax.rem(me, HALF)]

    pl.semaphore_wait(barrier, HALF + grp)
    wire = pl.ds(0, WIRE_ROWS)

    def send(d, carry):
        near = lax.rem(me + d, HALF)
        pltpu.make_async_remote_copy(
            src_ref=sent.at[near, wire],
            dst_ref=got.at[me, wire],
            send_sem=sems.at[0],
            recv_sem=sems.at[1],
            device_id={"cell": start + near},
            device_id_type=MESH,
        ).start()
        return carry

    lax.fori_loop(1 - grp, HALF, send, 0)

    for g in range(2):

        @pl.when(grp == g)
        def _():
            whole = pltpu.make_async_remote_copy(
                src_ref=sent.at[pl.ds(0, HALF - 1 + g), wire],
                dst_ref=got.at[pl.ds(start, HALF - 1 + g), wire],
                send_sem=sems.at[0],
                recv_sem=sems.at[1],
                device_id=sibling,
                device_id_type=MESH,
            )
            whole.wait_recv()
            whole.wait_send()

    swap = pltpu.make_async_remote_copy(
        src_ref=got.at[pl.ds(start, HALF), wire],
        dst_ref=got.at[pl.ds(start, HALF), wire],
        send_sem=sems.at[2],
        recv_sem=sems.at[3],
        device_id=sibling,
        device_id_type=MESH,
    )
    swap.start()
    swap.wait()


def seeds_of(fields, grp, e_seed, s_seed, coef):
    turns, sine, real, imag = [v + pltpu.roll(v, 64, 1) for v in fields]
    hi = lanes((8, 128)) >= 64
    s1, c1 = sincos_turns(turns)
    e = jnp.where(hi, 0.0, 1.0)
    f = jnp.where(hi, 1.0, 0.0)
    e_seed[pl.ds(8, 8, stride=16), :] = e
    for j in range(1, 9):
        e, f = e * c1 - f * s1, f * c1 + e * s1
        if j < 8:
            e_seed[pl.ds(8 + j, 8, stride=16), :] = e
        e_seed[pl.ds(8 - j, 8, stride=16), :] = jnp.where(hi, -e, e)
    _, c8 = sincos_turns(8.0 * turns)
    coef[0:8, :] = 2.0 * c8
    sa, ca = sincos_turns(0.5 * sine)
    first = (grp * (ANT // 2)).astype(jnp.float32)
    s0, c0 = sincos_turns(first * sine)
    _, a8 = sincos_turns(4.0 * sine)
    coef[8:16, :] = 2.0 * a8
    g1 = jnp.where(hi, -imag, real)
    g2 = jnp.where(hi, real, imag)
    x = g1 * c0 + g2 * s0
    y = g2 * c0 - g1 * s0
    for a in range(16):
        s_seed[pl.ds(a, 8, stride=32), :] = x
        s_seed[pl.ds(16 + a, 8, stride=32), :] = y
        if a < 15:
            x, y = x * ca + y * sa, y * ca - x * sa


def response_of(l, e_seed, s_seed, coef):
    c = jnp.broadcast_to(coef[l : l + 1, :], (8, 128))
    low = e_seed[16 * l : 16 * l + 8, :]
    top = e_seed[16 * l + 8 : 16 * l + 16, :]
    down = [top, low]
    up = [low, top]
    for _ in range(7):
        down.append(c * down[-1] - down[-2])
        up.append(c * up[-1] - up[-2])
    table = jnp.concatenate(down[:0:-1] + up[1:], axis=0).astype(jnp.bfloat16)
    c = jnp.broadcast_to(coef[8 + l : 9 + l, :], (8, 128))
    parts = []
    for h in range(2):
        at = 32 * l + 16 * h
        run = [s_seed[at : at + 8, :], s_seed[at + 8 : at + 16, :]]
        for _ in range(2):
            run.append(c * run[-1] - run[-2])
        parts += run
    spread = jnp.concatenate(parts, axis=0).astype(jnp.bfloat16)
    return lax.dot_general(
        spread, table, (((1,), (1,)), ((), ())), preferred_element_type=jnp.float32
    )


SEED_SCRATCH = [
    pltpu.VMEM((8 * 16, 128), jnp.float32),
    pltpu.VMEM((8 * 32, 128), jnp.float32),
    pltpu.VMEM((16, 128), jnp.float32),
]


def unpacked(code, got, over):
    source = code >> 16
    base = (code >> 8) & 255
    cnt = code & 255
    lane = lanes((8, 128))
    value = jnp.where(lane < base + cnt - 128, over[source], got[source])
    return jnp.where(lane < cnt, pltpu.roll(value, (0 - base) & 127, 1), 0.0)


def transmit_kernel(
    slots, nearby, got, symbols, over, table, raw, table_s, serving, e_seed, s_seed, coef, sem
):
    me = lax.axis_index("cell")
    grp = lax.axis_index("grp")
    lane = lanes((8, 128))
    row = rows_of((8, 128))
    is_tag = (lane >= TAG_LANE) & (lane < TAG_LANE + 8) & (lax.rem(lane, 2) == 0)
    link = (lane + 1).astype(jnp.float32)
    found = [jnp.zeros((8, 128), jnp.float32) for _ in range(LINKS // 128)]
    for c in range(CELLS // 8):
        extra = got[8 * c : 8 * c + 8, 4, :]
        for f in range(4):
            over[8 * c : 8 * c + 8, f, :] = extra if f == 0 else pltpu.roll(extra, 128 - 2 * f, 1)
        cnt = jnp.where(is_tag, pltpu.roll(extra, 127, 1), 0.0)
        base = pltpu.roll(cnt, 2, 1) + pltpu.roll(cnt, 4, 1) + pltpu.roll(cnt, 6, 1)
        code = (8 * c + row).astype(jnp.float32) * 65536.0 + base * 256.0 + cnt
        for k in range(4):
            at = TAG_LANE + 2 * k
            tags = jnp.broadcast_to(extra[:, at : at + 1], (8, 128))
            codes = jnp.broadcast_to(code[:, at : at + 1], (8, 128))
            for h in range(LINKS // 128):
                found[h] = found[h] + jnp.where(tags == link + 128.0 * h, codes, 0.0)
    for h in range(LINKS // 128):
        table[h : h + 1, :] = jnp.sum(found[h], axis=0, keepdims=True).astype(jnp.int32)
    copy = pltpu.make_async_copy(table, table_s, sem)
    copy.start()

    def clear(i, carry):
        raw[i] = jnp.zeros((RESP, 128), jnp.float32)
        return carry

    lax.fori_loop(0, CELL_SECTORS, clear, 0, unroll=4)
    copy.wait()

    def serve(u, carry):
        g = u * NEARBY_COUNT + slots[u]
        code = table_s[g >> 7, g & 127]
        serving[pl.ds(pl.multiple_of(8 * u, 8), 8), :] = unpacked(code, got, over)
        return carry

    lax.fori_loop(0, USERS, serve, 0, unroll=8)

    def eight_users(c, carry):
        fields = [serving[pl.ds(64 * c + f, 8, stride=8), :] for f in range(4)]
        seeds_of(fields, grp, e_seed, s_seed, coef)
        for l in range(8):
            u = 8 * c + l
            resp = response_of(l, e_seed, s_seed, coef).astype(jnp.bfloat16).astype(jnp.float32)
            sym = symbols[u].astype(jnp.float32)
            sym_r, sym_i = sym[0:1, :], sym[1:2, :]
            real, imag = resp[:ANT, :], resp[ANT:, :]
            part = jnp.concatenate(
                [real * sym_r + imag * sym_i, real * sym_i - imag * sym_r], axis=0
            )
            sector = nearby[slots[u], u] - me * CELL_SECTORS
            raw[sector] = raw[sector] + part
        return carry

    lax.fori_loop(0, USERS // 8, eight_users, 0)


PIECE = 8
PIECES = (0, 16, 8, 24)


def receive_kernel(
    nearby, table, got, over, raw, out, near, resp, part, other,
    e_seed, s_seed, coef, e_seed2, s_seed2, coef2, rows, rows2, send_sems, recv_sems
):
    me = lax.axis_index("cell")
    grp = lax.axis_index("grp")
    right = lax.rem(me + 1, CELLS)
    left = lax.rem(me + CELLS - 1, CELLS)
    barrier = pltpu.get_barrier_semaphore()
    for target in ({"cell": left}, {"cell": right}, {"grp": 1 - grp}):
        pl.semaphore_signal(barrier, inc=1, device_id=target, device_id_type=MESH)

    halo = []
    for n, begin in enumerate(PIECES):

        def normalise(s, carry):
            real, imag = raw[s, :ANT, :], raw[s, ANT:, :]
            power = jnp.mean(real * real + imag * imag, axis=1, keepdims=True)
            scale = 1.0 / jnp.sqrt(power + EPSILON)
            near[REACH + s] = jnp.concatenate([real * scale, imag * scale], axis=0).astype(jnp.bfloat16)
            return carry

        lax.fori_loop(begin, begin + PIECE, normalise, 0, unroll=4)
        if n == 0:
            pl.semaphore_wait(barrier, 3)
        to_left = begin < CELL_SECTORS - REACH
        land = begin + REACH + CELL_SECTORS if to_left else begin + REACH - CELL_SECTORS
        halo.append(
            pltpu.make_async_remote_copy(
                src_ref=near.at[pl.ds(REACH + begin, PIECE)],
                dst_ref=near.at[pl.ds(land, PIECE)],
                send_sem=send_sems.at[n],
                recv_sem=recv_sems.at[n],
                device_id={"cell": left if to_left else right},
                device_id_type=MESH,
            )
        )
        halo[-1].start()

    first, second = (e_seed, s_seed, coef), (e_seed2, s_seed2, coef2)

    def unpack(u, rows):
        u = jnp.minimum(u, USERS - 1)
        for l in range(8):
            code = table[u // 16, lax.rem(u, 16) * 8 + l]
            rows[8 * l : 8 * l + 8, :] = unpacked(code, got, over)

    def prepare(rows, seeds):
        seeds_of([rows[pl.ds(f, 8, stride=8), :] for f in range(4)], grp, *seeds)

    def respond(u, seeds):
        for l in range(8):
            at = pl.ds(pl.multiple_of(u * (8 * RESP) + RESP * l, RESP), RESP)
            resp[at, :] = response_of(l, *seeds).astype(jnp.bfloat16)

    def two_users(v, carry):
        prepare(rows2, second)
        unpack(2 * v + 3, rows2)
        respond(2 * v, first)
        prepare(rows, first)
        unpack(2 * v + 4, rows)
        respond(2 * v + 1, second)
        return carry

    unpack(0, rows)
    prepare(rows, first)
    unpack(1, rows2)
    unpack(2, rows)
    lax.fori_loop(0, USERS // 2, two_users, 0)
    for copy in halo:
        copy.wait()

    def combine(u, carry):
        real = jnp.zeros((ANT, 128), jnp.float32)
        imag = jnp.zeros((ANT, 128), jnp.float32)
        for k in range(NEARBY_COUNT):
            sector = nearby[k, u] - me * CELL_SECTORS + REACH
            sector = jnp.clip(sector, 0, CELL_SECTORS + 2 * REACH - 1)
            tx = near[sector].astype(jnp.float32)
            at = pl.ds(pl.multiple_of(u * (8 * RESP) + RESP * k, RESP), RESP)
            ch = resp[at, :].astype(jnp.float32)
            real = real + (ch[:ANT] * tx[:ANT] - ch[ANT:] * tx[ANT:])
            imag = imag + (ch[:ANT] * tx[ANT:] + ch[ANT:] * tx[:ANT])
        part[u] = jnp.concatenate(
            [jnp.sum(real, axis=0, keepdims=True), jnp.sum(imag, axis=0, keepdims=True)], axis=0
        )
        return carry

    lax.fori_loop(0, USERS, combine, 0)
    swap = pltpu.make_async_remote_copy(
        src_ref=part,
        dst_ref=other,
        send_sem=send_sems.at[len(PIECES)],
        recv_sem=recv_sems.at[len(PIECES)],
        device_id={"grp": 1 - grp},
        device_id_type=MESH,
    )
    swap.start()
    swap.wait()
    out[...] = (part[...] + other[...]) * (1.0 / math.sqrt(SECTOR_ANTENNAS))


VMEM = pl.BlockSpec(memory_space=pltpu.VMEM)
SMEM = pl.BlockSpec(memory_space=pltpu.SMEM)
HBM = pl.BlockSpec(memory_space=pltpu.HBM)


def call(kernel, name, mib, out_shape, in_specs, scratch, remote=None):
    extra = {} if remote is None else {"collective_id": remote, "has_side_effects": True}
    many = isinstance(out_shape, (tuple, list))
    return pl.pallas_call(
        kernel,
        name=name,
        out_shape=out_shape,
        in_specs=in_specs,
        out_specs=[VMEM] * len(out_shape) if many else VMEM,
        scratch_shapes=scratch,
        compiler_params=pltpu.CompilerParams(vmem_limit_bytes=mib * MIB, **extra),
    )


def shards(
    path_delay,
    path_angle,
    path_gain,
    slot_counts,
    slot_offsets,
    ray_link,
    nearby_sectors,
    serving_slot,
    symbols,
):
    f32, bf16, i32 = jnp.float32, jnp.bfloat16, jnp.int32
    got = call(
        deliver_kernel,
        "deliver",
        60,
        jax.ShapeDtypeStruct((CELLS, 8, 128), f32),
        [SMEM, SMEM, SMEM, HBM, HBM, HBM],
        [
            pltpu.VMEM((PATH_ROWS, 128), f32),
            pltpu.VMEM((PATH_ROWS, 128), f32),
            pltpu.VMEM((2, PATH_ROWS * 128), f32),
            pltpu.VMEM((PATH_ROWS + 1, 8, 128), f32),
            pltpu.VMEM((HALF, 8, 128), f32),
            pltpu.SMEM((HALF + 1,), i32),
            pltpu.SemaphoreType.DMA((3,)),
            pltpu.SemaphoreType.DMA((4,)),
        ],
        remote=0,
    )(
        slot_counts,
        slot_offsets,
        ray_link,
        path_delay.reshape(PATH_ROWS, 128),
        path_angle.reshape(PATH_ROWS, 128),
        path_gain,
    )
    over, table, raw = call(
        transmit_kernel,
        "transmit",
        24,
        (
            jax.ShapeDtypeStruct((CELLS, 8, 128), f32),
            jax.ShapeDtypeStruct((LINKS // 128, 128), i32),
            jax.ShapeDtypeStruct((CELL_SECTORS, RESP, 128), f32),
        ),
        [SMEM, SMEM, VMEM, VMEM],
        [
            pltpu.SMEM((LINKS // 128, 128), i32),
            pltpu.VMEM((USERS * 8, 128), f32),
            *SEED_SCRATCH,
            pltpu.SemaphoreType.DMA,
        ],
    )(serving_slot, nearby_sectors, got, symbols)
    return call(
        receive_kernel,
        "receive",
        24,
        jax.ShapeDtypeStruct((USERS, 2, FRAME_TONES), f32),
        [SMEM, SMEM, VMEM, VMEM, VMEM],
        [
            pltpu.VMEM((CELL_SECTORS + 2 * REACH, RESP, 128), bf16),
            pltpu.VMEM((LINKS * RESP, 128), bf16),
            pltpu.VMEM((USERS, 2, FRAME_TONES), f32),
            pltpu.VMEM((USERS, 2, FRAME_TONES), f32),
            *SEED_SCRATCH,
            *SEED_SCRATCH,
            pltpu.VMEM((64, 128), f32),
            pltpu.VMEM((64, 128), f32),
            pltpu.SemaphoreType.DMA((len(PIECES) + 1,)),
            pltpu.SemaphoreType.DMA((len(PIECES) + 1,)),
        ],
        remote=1,
    )(nearby_sectors, table, got, over, raw)


def solution(mesh):
    placed = (
        P("cell"),
        P("cell"),
        P(None, "cell"),
        P("cell"),
        P("cell"),
        P("cell"),
        P(None, "cell"),
        P("cell"),
        P("cell", None, None),
    )
    return jax.shard_map(
        shards, mesh=mesh, in_specs=placed, out_specs=P("cell", None, None), check_vma=False
    )
```

```python
import functools
import math

import jax
import jax.numpy as jnp
from jax import lax
from jax.experimental import pallas as pl
from jax.experimental.pallas import tpu as pltpu
from jax.sharding import PartitionSpec as P

SECTOR_ANTENNAS = 64
FRAME_TONES = 128
NEARBY_COUNT = 8
CELL_SECTORS = 32
REACH = 16
EPSILON = 1e-06

CELLS = 128
SLOTS = 256
USERS = 32
LINKS = USERS * NEARBY_COUNT
PATH_ROWS = 65
ANT = SECTOR_ANTENNAS // 2
RESP = 2 * ANT
TAG_LANE = 8
HALF = CELLS // 2
WIRE_ROWS = 5
MIB = 1024 * 1024
MESH = pl.DeviceIdType.MESH


def lanes(shape):
    return lax.broadcasted_iota(jnp.int32, shape, len(shape) - 1)


def rows_of(shape):
    return lax.broadcasted_iota(jnp.int32, shape, len(shape) - 2)


def sincos_turns(turns):
    r = turns - jnp.round(turns)
    r2 = r * r
    sin_c = [(-1) ** n * math.pi ** (2 * n + 1) / math.factorial(2 * n + 1) for n in range(7)]
    cos_c = [(-1) ** n * math.pi ** (2 * n) / math.factorial(2 * n) for n in range(7)]
    sh = jnp.full_like(r, sin_c[-1])
    ch = jnp.full_like(r, cos_c[-1])
    for n in range(5, -1, -1):
        sh = sh * r2 + sin_c[n]
        ch = ch * r2 + cos_c[n]
    sh = sh * r
    return 2.0 * sh * ch, 1.0 - 2.0 * sh * sh


def my_half():
    return lax.rem(lax.axis_index("grp") + lax.axis_index("cell") // HALF, 2)


def deliver_kernel(
    counts, offsets, links, fields, got, store, sent, begins, sems
):
    me = lax.axis_index("cell")
    grp = lax.axis_index("grp")
    start = my_half() * HALF
    sibling = {"grp": 1 - grp}
    barrier = pltpu.get_barrier_semaphore()
    pl.semaphore_signal(barrier, inc=1, device_id=sibling, device_id_type=MESH)

    def greet(d, carry):
        other = start + lax.rem(me + d, HALF)
        pl.semaphore_signal(barrier, inc=1, device_id={"cell": other}, device_id_type=MESH)
        return carry

    lax.fori_loop(1 - grp, HALF, greet, 0)

    def narrow(_, carry):
        low, top = carry
        mid = (low + top) >> 1
        below = (links[jnp.minimum(mid, SLOTS - 1)] >> 8) < start
        below = below & (low < top)
        return jnp.where(below, mid + 1, low), jnp.where(below, top, mid)

    at, _ = lax.fori_loop(0, 9, narrow, (jnp.int32(0), jnp.int32(SLOTS)))

    def count(o, at):
        begins[o] = at
        total = at
        for k in range(4):
            slot = at + k
            mine = (links[jnp.minimum(slot, SLOTS - 1)] >> 8) == start + o
            total = total + jnp.where(mine & (slot < SLOTS), 1, 0)
        return total

    begins[HALF] = lax.fori_loop(0, HALF, count, at, unroll=4)

    for c in range(0, PATH_ROWS, 8):
        n = min(8, PATH_ROWS - c)
        for f in range(4):
            value = fields[f, c : c + n, :]
            if f < 2:
                value = value * (1.0 / FRAME_TONES) if f == 0 else jnp.sin(value)
            store[c : c + n, f, :] = value
            store[c : c + n, 4 + f, :] = value
    store[PATH_ROWS] = jnp.zeros((8, 128), jnp.float32)

    lane = lanes((8, 128))
    row = rows_of((8, 128))
    place = lane + jnp.where(row >= 4, 128, 0)
    tag_place = jnp.where(row == 4, lane - TAG_LANE, -1000)

    def pack(o, carry):
        first = begins[o]
        number = begins[o + 1] - first
        base = jnp.int32(0)
        message = jnp.zeros((8, 128), jnp.float32)
        for k in range(4):
            r = jnp.minimum(first + k, SLOTS - 1)
            cnt = jnp.where(k < number, counts[r], 0)
            tag = jnp.where(k < number, (links[r] & 255) + 1, 0)
            off = offsets[r]
            q = off >> 7
            s = off & 127
            value = jnp.where(lane < s + cnt - 128, store[q + 1], store[q])
            value = pltpu.roll(value, (base - s) & 127, 1)
            j = place - base
            message = jnp.where((j >= 0) & (j < cnt), value, message)
            message = jnp.where(tag_place == 2 * k, tag.astype(jnp.float32), message)
            message = jnp.where(tag_place == 2 * k + 1, cnt.astype(jnp.float32), message)
            base = base + cnt
        sent[o] = message
        return carry

    lax.fori_loop(0, HALF, pack, 0, unroll=4)
    for c in range(0, HALF, 8):
        total = sent[c : c + 8, 4, :]
        for f in range(1, 4):
            total = total + pltpu.roll(sent[c : c + 8, 4 + f, :], 2 * f, 1)
        sent[c : c + 8, 4, :] = total

    @pl.when(grp == 0)
    def _():
        got[me] = sent[lax.rem(me, HALF)]

    pl.semaphore_wait(barrier, HALF + grp)
    wire = pl.ds(0, WIRE_ROWS)

    def send(d, carry):
        near = lax.rem(me + d, HALF)
        pltpu.make_async_remote_copy(
            src_ref=sent.at[near, wire],
            dst_ref=got.at[me, wire],
            send_sem=sems.at[0],
            recv_sem=sems.at[1],
            device_id={"cell": start + near},
            device_id_type=MESH,
        ).start()
        return carry

    lax.fori_loop(1 - grp, HALF, send, 0)

    for g in range(2):

        @pl.when(grp == g)
        def _():
            whole = pltpu.make_async_remote_copy(
                src_ref=sent.at[pl.ds(0, HALF - 1 + g), wire],
                dst_ref=got.at[pl.ds(start, HALF - 1 + g), wire],
                send_sem=sems.at[0],
                recv_sem=sems.at[1],
                device_id=sibling,
                device_id_type=MESH,
            )
            whole.wait_recv()
            whole.wait_send()

    swap = pltpu.make_async_remote_copy(
        src_ref=got.at[pl.ds(start, HALF), wire],
        dst_ref=got.at[pl.ds(start, HALF), wire],
        send_sem=sems.at[2],
        recv_sem=sems.at[3],
        device_id=sibling,
        device_id_type=MESH,
    )
    swap.start()
    swap.wait()


def seeds_of(fields, grp, e_seed, s_seed, coef):
    turns, sine, real, imag = [v + pltpu.roll(v, 64, 1) for v in fields]
    hi = lanes((8, 128)) >= 64
    s1, c1 = sincos_turns(turns)
    e = jnp.where(hi, 0.0, 1.0)
    f = jnp.where(hi, 1.0, 0.0)
    e_seed[pl.ds(8, 8, stride=16), :] = e
    for j in range(1, 9):
        e, f = e * c1 - f * s1, f * c1 + e * s1
        if j < 8:
            e_seed[pl.ds(8 + j, 8, stride=16), :] = e
        e_seed[pl.ds(8 - j, 8, stride=16), :] = jnp.where(hi, -e, e)
    _, c8 = sincos_turns(8.0 * turns)
    coef[0:8, :] = 2.0 * c8
    sa, ca = sincos_turns(0.5 * sine)
    first = (grp * (ANT // 2)).astype(jnp.float32)
    s0, c0 = sincos_turns(first * sine)
    _, a8 = sincos_turns(4.0 * sine)
    coef[8:16, :] = 2.0 * a8
    g1 = jnp.where(hi, -imag, real)
    g2 = jnp.where(hi, real, imag)
    x = g1 * c0 + g2 * s0
    y = g2 * c0 - g1 * s0
    for a in range(16):
        s_seed[pl.ds(a, 8, stride=32), :] = x
        s_seed[pl.ds(16 + a, 8, stride=32), :] = y
        if a < 15:
            x, y = x * ca + y * sa, y * ca - x * sa


def response_of(l, e_seed, s_seed, coef):
    c = jnp.broadcast_to(coef[l : l + 1, :], (8, 128))
    low = e_seed[16 * l : 16 * l + 8, :]
    top = e_seed[16 * l + 8 : 16 * l + 16, :]
    down = [top, low]
    up = [low, top]
    for _ in range(7):
        down.append(c * down[-1] - down[-2])
        up.append(c * up[-1] - up[-2])
    table = jnp.concatenate(down[:0:-1] + up[1:], axis=0).astype(jnp.bfloat16)
    c = jnp.broadcast_to(coef[8 + l : 9 + l, :], (8, 128))
    parts = []
    for h in range(2):
        at = 32 * l + 16 * h
        run = [s_seed[at : at + 8, :], s_seed[at + 8 : at + 16, :]]
        for _ in range(2):
            run.append(c * run[-1] - run[-2])
        parts += run
    spread = jnp.concatenate(parts, axis=0).astype(jnp.bfloat16)
    return lax.dot_general(
        spread, table, (((1,), (1,)), ((), ())), preferred_element_type=jnp.float32
    )


SEED_SCRATCH = [
    pltpu.VMEM((8 * 16, 128), jnp.float32),
    pltpu.VMEM((8 * 32, 128), jnp.float32),
    pltpu.VMEM((16, 128), jnp.float32),
]


def unpacked(code, got, over):
    source = code >> 16
    base = (code >> 8) & 255
    cnt = code & 255
    lane = lanes((8, 128))
    value = jnp.where(lane < base + cnt - 128, over[source], got[source])
    return jnp.where(lane < cnt, pltpu.roll(value, (0 - base) & 127, 1), 0.0)


def transmit_kernel(
    slots, nearby, got, symbols, over, table, raw, table_s, serving,
    e_seed, s_seed, coef, e_seed2, s_seed2, coef2, sem
):
    me = lax.axis_index("cell")
    grp = lax.axis_index("grp")
    lane = lanes((8, 128))
    row = rows_of((8, 128))
    is_tag = (lane >= TAG_LANE) & (lane < TAG_LANE + 8) & (lax.rem(lane, 2) == 0)
    link = (lane + 1).astype(jnp.float32)
    found = [jnp.zeros((8, 128), jnp.float32) for _ in range(LINKS // 128)]
    for c in range(CELLS // 8):
        extra = got[8 * c : 8 * c + 8, 4, :]
        for f in range(4):
            over[8 * c : 8 * c + 8, f, :] = extra if f == 0 else pltpu.roll(extra, 128 - 2 * f, 1)
        cnt = jnp.where(is_tag, pltpu.roll(extra, 127, 1), 0.0)
        base = pltpu.roll(cnt, 2, 1) + pltpu.roll(cnt, 4, 1) + pltpu.roll(cnt, 6, 1)
        code = (8 * c + row).astype(jnp.float32) * 65536.0 + base * 256.0 + cnt
        for k in range(4):
            at = TAG_LANE + 2 * k
            tags = jnp.broadcast_to(extra[:, at : at + 1], (8, 128))
            codes = jnp.broadcast_to(code[:, at : at + 1], (8, 128))
            for h in range(LINKS // 128):
                found[h] = found[h] + jnp.where(tags == link + 128.0 * h, codes, 0.0)
    for h in range(LINKS // 128):
        table[h : h + 1, :] = jnp.sum(found[h], axis=0, keepdims=True).astype(jnp.int32)
    copy = pltpu.make_async_copy(table, table_s, sem)
    copy.start()

    def clear(i, carry):
        raw[i] = jnp.zeros((RESP, 128), jnp.float32)
        return carry

    lax.fori_loop(0, CELL_SECTORS, clear, 0, unroll=4)
    copy.wait()

    def serve(u, carry):
        g = u * NEARBY_COUNT + slots[u]
        code = table_s[g >> 7, g & 127]
        serving[pl.ds(pl.multiple_of(8 * u, 8), 8), :] = unpacked(code, got, over)
        return carry

    lax.fori_loop(0, USERS, serve, 0, unroll=8)

    seeds = (e_seed, s_seed, coef), (e_seed2, s_seed2, coef2)

    def prepare(c):
        fields = [serving[pl.ds(64 * c + f, 8, stride=8), :] for f in range(4)]
        seeds_of(fields, grp, *seeds[c % 2])

    prepare(0)
    for c in range(USERS // 8):
        if c + 1 < USERS // 8:
            prepare(c + 1)
        for l in range(8):
            u = 8 * c + l
            resp = response_of(l, *seeds[c % 2]).astype(jnp.bfloat16).astype(jnp.float32)
            sym = symbols[u].astype(jnp.float32)
            sym_r, sym_i = sym[0:1, :], sym[1:2, :]
            real, imag = resp[:ANT, :], resp[ANT:, :]
            part = jnp.concatenate(
                [real * sym_r + imag * sym_i, real * sym_i - imag * sym_r], axis=0
            )
            sector = nearby[slots[u], u] - me * CELL_SECTORS
            raw[sector] = raw[sector] + part


PIECE = 8
PIECES = (0, 16, 8, 24)


def receive_kernel(
    nearby, table, got, over, raw, out, near, resp, part, other,
    e_seed, s_seed, coef, e_seed2, s_seed2, coef2, rows, rows2, send_sems, recv_sems
):
    me = lax.axis_index("cell")
    grp = lax.axis_index("grp")
    right = lax.rem(me + 1, CELLS)
    left = lax.rem(me + CELLS - 1, CELLS)
    barrier = pltpu.get_barrier_semaphore()
    for target in ({"cell": left}, {"cell": right}, {"grp": 1 - grp}):
        pl.semaphore_signal(barrier, inc=1, device_id=target, device_id_type=MESH)

    halo = []
    for n, begin in enumerate(PIECES):

        def normalise(s, carry):
            real, imag = raw[s, :ANT, :], raw[s, ANT:, :]
            power = jnp.mean(real * real + imag * imag, axis=1, keepdims=True)
            scale = 1.0 / jnp.sqrt(power + EPSILON)
            near[REACH + s] = jnp.concatenate([real * scale, imag * scale], axis=0).astype(jnp.bfloat16)
            return carry

        lax.fori_loop(begin, begin + PIECE, normalise, 0, unroll=4)
        if n == 0:
            pl.semaphore_wait(barrier, 3)
        to_left = begin < CELL_SECTORS - REACH
        land = begin + REACH + CELL_SECTORS if to_left else begin + REACH - CELL_SECTORS
        halo.append(
            pltpu.make_async_remote_copy(
                src_ref=near.at[pl.ds(REACH + begin, PIECE)],
                dst_ref=near.at[pl.ds(land, PIECE)],
                send_sem=send_sems.at[n],
                recv_sem=recv_sems.at[n],
                device_id={"cell": left if to_left else right},
                device_id_type=MESH,
            )
        )
        halo[-1].start()

    first, second = (e_seed, s_seed, coef), (e_seed2, s_seed2, coef2)

    def unpack(u, rows):
        u = jnp.minimum(u, USERS - 1)
        for l in range(8):
            code = table[u // 16, lax.rem(u, 16) * 8 + l]
            rows[8 * l : 8 * l + 8, :] = unpacked(code, got, over)

    def prepare(rows, seeds):
        seeds_of([rows[pl.ds(f, 8, stride=8), :] for f in range(4)], grp, *seeds)

    def respond(u, seeds):
        for l in range(8):
            at = pl.ds(pl.multiple_of(u * (8 * RESP) + RESP * l, RESP), RESP)
            resp[at, :] = response_of(l, *seeds).astype(jnp.bfloat16)

    def two_users(v, carry):
        prepare(rows2, second)
        unpack(2 * v + 3, rows2)
        respond(2 * v, first)
        prepare(rows, first)
        unpack(2 * v + 4, rows)
        respond(2 * v + 1, second)
        return carry

    unpack(0, rows)
    prepare(rows, first)
    unpack(1, rows2)
    unpack(2, rows)
    lax.fori_loop(0, USERS // 2, two_users, 0)
    for copy in halo:
        copy.wait()

    def combine(u, carry):
        real = jnp.zeros((ANT, 128), jnp.float32)
        imag = jnp.zeros((ANT, 128), jnp.float32)
        for k in range(NEARBY_COUNT):
            sector = nearby[k, u] - me * CELL_SECTORS + REACH
            sector = jnp.clip(sector, 0, CELL_SECTORS + 2 * REACH - 1)
            tx = near[sector].astype(jnp.float32)
            at = pl.ds(pl.multiple_of(u * (8 * RESP) + RESP * k, RESP), RESP)
            ch = resp[at, :].astype(jnp.float32)
            real = real + (ch[:ANT] * tx[:ANT] - ch[ANT:] * tx[ANT:])
            imag = imag + (ch[:ANT] * tx[ANT:] + ch[ANT:] * tx[:ANT])
        part[u] = jnp.concatenate(
            [jnp.sum(real, axis=0, keepdims=True), jnp.sum(imag, axis=0, keepdims=True)], axis=0
        )
        return carry

    lax.fori_loop(0, USERS, combine, 0)
    swap = pltpu.make_async_remote_copy(
        src_ref=part,
        dst_ref=other,
        send_sem=send_sems.at[len(PIECES)],
        recv_sem=recv_sems.at[len(PIECES)],
        device_id={"grp": 1 - grp},
        device_id_type=MESH,
    )
    swap.start()
    swap.wait()
    out[...] = (part[...] + other[...]) * (1.0 / math.sqrt(SECTOR_ANTENNAS))


VMEM = pl.BlockSpec(memory_space=pltpu.VMEM)
SMEM = pl.BlockSpec(memory_space=pltpu.SMEM)


def call(kernel, name, mib, out_shape, in_specs, scratch, remote=None):
    extra = {} if remote is None else {"collective_id": remote, "has_side_effects": True}
    many = isinstance(out_shape, (tuple, list))
    return pl.pallas_call(
        kernel,
        name=name,
        out_shape=out_shape,
        in_specs=in_specs,
        out_specs=[VMEM] * len(out_shape) if many else VMEM,
        scratch_shapes=scratch,
        compiler_params=pltpu.CompilerParams(vmem_limit_bytes=mib * MIB, **extra),
    )


def shards(
    path_delay,
    path_angle,
    path_gain,
    slot_counts,
    slot_offsets,
    ray_link,
    nearby_sectors,
    serving_slot,
    symbols,
):
    f32, bf16, i32 = jnp.float32, jnp.bfloat16, jnp.int32
    got = call(
        deliver_kernel,
        "deliver",
        16,
        jax.ShapeDtypeStruct((CELLS, 8, 128), f32),
        [SMEM, SMEM, SMEM, VMEM],
        [
            pltpu.VMEM((PATH_ROWS + 1, 8, 128), f32),
            pltpu.VMEM((HALF, 8, 128), f32),
            pltpu.SMEM((HALF + 1,), i32),
            pltpu.SemaphoreType.DMA((4,)),
        ],
        remote=0,
    )(
        slot_counts,
        slot_offsets,
        ray_link,
        jnp.stack((path_delay, path_angle, path_gain[0], path_gain[1])).reshape(4, PATH_ROWS, 128),
    )
    over, table, raw = call(
        transmit_kernel,
        "transmit",
        24,
        (
            jax.ShapeDtypeStruct((CELLS, 8, 128), f32),
            jax.ShapeDtypeStruct((LINKS // 128, 128), i32),
            jax.ShapeDtypeStruct((CELL_SECTORS, RESP, 128), f32),
        ),
        [SMEM, SMEM, VMEM, VMEM],
        [
            pltpu.SMEM((LINKS // 128, 128), i32),
            pltpu.VMEM((USERS * 8, 128), f32),
            *SEED_SCRATCH,
            *SEED_SCRATCH,
            pltpu.SemaphoreType.DMA,
        ],
    )(serving_slot, nearby_sectors, got, symbols)
    return call(
        receive_kernel,
        "receive",
        24,
        jax.ShapeDtypeStruct((USERS, 2, FRAME_TONES), f32),
        [SMEM, SMEM, VMEM, VMEM, VMEM],
        [
            pltpu.VMEM((CELL_SECTORS + 2 * REACH, RESP, 128), bf16),
            pltpu.VMEM((LINKS * RESP, 128), bf16),
            pltpu.VMEM((USERS, 2, FRAME_TONES), f32),
            pltpu.VMEM((USERS, 2, FRAME_TONES), f32),
            *SEED_SCRATCH,
            *SEED_SCRATCH,
            pltpu.VMEM((64, 128), f32),
            pltpu.VMEM((64, 128), f32),
            pltpu.SemaphoreType.DMA((len(PIECES) + 1,)),
            pltpu.SemaphoreType.DMA((len(PIECES) + 1,)),
        ],
        remote=1,
    )(nearby_sectors, table, got, over, raw)


def solution(mesh):
    placed = (
        P("cell"),
        P("cell"),
        P(None, "cell"),
        P("cell"),
        P("cell"),
        P("cell"),
        P(None, "cell"),
        P("cell"),
        P("cell", None, None),
    )
    return jax.shard_map(
        shards, mesh=mesh, in_specs=placed, out_specs=P("cell", None, None), check_vma=False
    )
```

```python
import functools
import math

import jax
import jax.numpy as jnp
from jax import lax
from jax.experimental import pallas as pl
from jax.experimental.pallas import tpu as pltpu
from jax.sharding import PartitionSpec as P

SECTOR_ANTENNAS = 64
FRAME_TONES = 128
NEARBY_COUNT = 8
CELL_SECTORS = 32
REACH = 16
EPSILON = 1e-06

CELLS = 128
SLOTS = 256
USERS = 32
LINKS = USERS * NEARBY_COUNT
PATH_ROWS = 65
ANT = SECTOR_ANTENNAS // 2
RESP = 2 * ANT
TAG_LANE = 8
HALF = CELLS // 2
WIRE_ROWS = 5
MIB = 1024 * 1024
MESH = pl.DeviceIdType.MESH


def lanes(shape):
    return lax.broadcasted_iota(jnp.int32, shape, len(shape) - 1)


def rows_of(shape):
    return lax.broadcasted_iota(jnp.int32, shape, len(shape) - 2)


def sincos_turns(turns):
    r = turns - jnp.round(turns)
    r2 = r * r
    sin_c = [(-1) ** n * math.pi ** (2 * n + 1) / math.factorial(2 * n + 1) for n in range(7)]
    cos_c = [(-1) ** n * math.pi ** (2 * n) / math.factorial(2 * n) for n in range(7)]
    sh = jnp.full_like(r, sin_c[-1])
    ch = jnp.full_like(r, cos_c[-1])
    for n in range(5, -1, -1):
        sh = sh * r2 + sin_c[n]
        ch = ch * r2 + cos_c[n]
    sh = sh * r
    return 2.0 * sh * ch, 1.0 - 2.0 * sh * sh


def my_half():
    return lax.rem(lax.axis_index("grp") + lax.axis_index("cell") // HALF, 2)


def deliver_kernel(
    counts, offsets, links, fields, got, store, sent, begins, sems
):
    me = lax.axis_index("cell")
    grp = lax.axis_index("grp")
    start = my_half() * HALF
    sibling = {"grp": 1 - grp}
    barrier = pltpu.get_barrier_semaphore()
    pl.semaphore_signal(barrier, inc=1, device_id=sibling, device_id_type=MESH)

    def greet(d, carry):
        other = start + lax.rem(me + d, HALF)
        pl.semaphore_signal(barrier, inc=1, device_id={"cell": other}, device_id_type=MESH)
        return carry

    lax.fori_loop(1 - grp, HALF, greet, 0)

    def narrow(_, carry):
        low, top = carry
        mid = (low + top) >> 1
        below = (links[jnp.minimum(mid, SLOTS - 1)] >> 8) < start
        below = below & (low < top)
        return jnp.where(below, mid + 1, low), jnp.where(below, top, mid)

    at, _ = lax.fori_loop(0, 9, narrow, (jnp.int32(0), jnp.int32(SLOTS)))

    def count(o, at):
        begins[o] = at
        total = at
        for k in range(4):
            slot = at + k
            mine = (links[jnp.minimum(slot, SLOTS - 1)] >> 8) == start + o
            total = total + jnp.where(mine & (slot < SLOTS), 1, 0)
        return total

    begins[HALF] = lax.fori_loop(0, HALF, count, at, unroll=4)

    for c in range(0, PATH_ROWS, 8):
        n = min(8, PATH_ROWS - c)
        for f in range(4):
            value = fields[f, c : c + n, :]
            if f < 2:
                value = value * (1.0 / FRAME_TONES) if f == 0 else jnp.sin(value)
            store[c : c + n, f, :] = value
            store[c : c + n, 4 + f, :] = value
    store[PATH_ROWS] = jnp.zeros((8, 128), jnp.float32)

    lane = lanes((8, 128))
    row = rows_of((8, 128))
    place = lane + jnp.where(row >= 4, 128, 0)
    tag_place = jnp.where(row == 4, lane - TAG_LANE, -1000)

    def pack(o, carry):
        first = begins[o]
        number = begins[o + 1] - first
        base = jnp.int32(0)
        message = jnp.zeros((8, 128), jnp.float32)
        for k in range(4):
            r = jnp.minimum(first + k, SLOTS - 1)
            cnt = jnp.where(k < number, counts[r], 0)
            tag = jnp.where(k < number, (links[r] & 255) + 1, 0)
            off = offsets[r]
            q = off >> 7
            s = off & 127
            value = jnp.where(lane < s + cnt - 128, store[q + 1], store[q])
            value = pltpu.roll(value, (base - s) & 127, 1)
            j = place - base
            message = jnp.where((j >= 0) & (j < cnt), value, message)
            for n, number_sent in enumerate((tag, cnt, base)):
                message = jnp.where(tag_place == 3 * k + n, number_sent.astype(jnp.float32), message)
            base = base + cnt
        sent[o] = message
        return carry

    lax.fori_loop(0, HALF, pack, 0, unroll=4)
    for c in range(0, HALF, 8):
        total = sent[c : c + 8, 4, :]
        for f in range(1, 4):
            total = total + pltpu.roll(sent[c : c + 8, 4 + f, :], 2 * f, 1)
        sent[c : c + 8, 4, :] = total

    @pl.when(grp == 0)
    def _():
        got[me] = sent[lax.rem(me, HALF)]

    pl.semaphore_wait(barrier, HALF + grp)
    wire = pl.ds(0, WIRE_ROWS)

    def send(d, carry):
        near = lax.rem(me + d, HALF)
        pltpu.make_async_remote_copy(
            src_ref=sent.at[near, wire],
            dst_ref=got.at[me, wire],
            send_sem=sems.at[0],
            recv_sem=sems.at[1],
            device_id={"cell": start + near},
            device_id_type=MESH,
        ).start()
        return carry

    lax.fori_loop(1 - grp, HALF, send, 0)

    for g in range(2):

        @pl.when(grp == g)
        def _():
            whole = pltpu.make_async_remote_copy(
                src_ref=sent.at[pl.ds(0, HALF - 1 + g), wire],
                dst_ref=got.at[pl.ds(start, HALF - 1 + g), wire],
                send_sem=sems.at[0],
                recv_sem=sems.at[1],
                device_id=sibling,
                device_id_type=MESH,
            )
            whole.wait_recv()
            whole.wait_send()

    swap = pltpu.make_async_remote_copy(
        src_ref=got.at[pl.ds(start, HALF), wire],
        dst_ref=got.at[pl.ds(start, HALF), wire],
        send_sem=sems.at[2],
        recv_sem=sems.at[3],
        device_id=sibling,
        device_id_type=MESH,
    )
    swap.start()
    swap.wait()


def seeds_of(fields, grp, e_seed, s_seed, coef):
    turns, sine, real, imag = [v + pltpu.roll(v, 64, 1) for v in fields]
    hi = lanes((8, 128)) >= 64
    s1, c1 = sincos_turns(turns)
    e = jnp.where(hi, 0.0, 1.0)
    f = jnp.where(hi, 1.0, 0.0)
    e_seed[pl.ds(8, 8, stride=16), :] = e
    for j in range(1, 9):
        e, f = e * c1 - f * s1, f * c1 + e * s1
        if j < 8:
            e_seed[pl.ds(8 + j, 8, stride=16), :] = e
        e_seed[pl.ds(8 - j, 8, stride=16), :] = jnp.where(hi, -e, e)
    _, c8 = sincos_turns(8.0 * turns)
    coef[0:8, :] = 2.0 * c8
    sa, ca = sincos_turns(0.5 * sine)
    first = (grp * (ANT // 2)).astype(jnp.float32)
    s0, c0 = sincos_turns(first * sine)
    _, a8 = sincos_turns(4.0 * sine)
    coef[8:16, :] = 2.0 * a8
    g1 = jnp.where(hi, -imag, real)
    g2 = jnp.where(hi, real, imag)
    x = g1 * c0 + g2 * s0
    y = g2 * c0 - g1 * s0
    for a in range(16):
        s_seed[pl.ds(a, 8, stride=32), :] = x
        s_seed[pl.ds(16 + a, 8, stride=32), :] = y
        if a < 15:
            x, y = x * ca + y * sa, y * ca - x * sa


def response_of(l, e_seed, s_seed, coef):
    c = jnp.broadcast_to(coef[l : l + 1, :], (8, 128))
    low = e_seed[16 * l : 16 * l + 8, :]
    top = e_seed[16 * l + 8 : 16 * l + 16, :]
    down = [top, low]
    up = [low, top]
    for _ in range(7):
        down.append(c * down[-1] - down[-2])
        up.append(c * up[-1] - up[-2])
    table = jnp.concatenate(down[:0:-1] + up[1:], axis=0).astype(jnp.bfloat16)
    c = jnp.broadcast_to(coef[8 + l : 9 + l, :], (8, 128))
    parts = []
    for h in range(2):
        at = 32 * l + 16 * h
        run = [s_seed[at : at + 8, :], s_seed[at + 8 : at + 16, :]]
        for _ in range(2):
            run.append(c * run[-1] - run[-2])
        parts += run
    spread = jnp.concatenate(parts, axis=0).astype(jnp.bfloat16)
    return lax.dot_general(
        spread, table, (((1,), (1,)), ((), ())), preferred_element_type=jnp.float32
    )


SEED_SCRATCH = [
    pltpu.VMEM((8 * 16, 128), jnp.float32),
    pltpu.VMEM((8 * 32, 128), jnp.float32),
    pltpu.VMEM((16, 128), jnp.float32),
]


def unpacked(code, load):
    base = code & 255
    cnt = (code >> 8) & 255
    lane = lanes((8, 128))
    message, overflow = load(code >> 16)
    value = jnp.where(lane < base + cnt - 128, overflow, message)
    return jnp.where(lane < cnt, pltpu.roll(value, (0 - base) & 127, 1), 0.0)


def transmit_kernel(
    slots, nearby, got, symbols, over, table, raw, table_s, serving,
    e_seed, s_seed, coef, e_seed2, s_seed2, coef2, sem
):
    me = lax.axis_index("cell")
    grp = lax.axis_index("grp")
    lane = lanes((8, 128))
    row = rows_of((8, 128))
    is_tag = (lane >= TAG_LANE) & (lane < TAG_LANE + 12)
    link = lane + 1
    found = [jnp.zeros((8, 128), jnp.int32) for _ in range(LINKS // 128)]
    for c in range(CELLS // 8):
        extra = got[pl.ds(64 * c + 4, 8, stride=8), :]
        number = jnp.where(is_tag, extra, 0.0).astype(jnp.int32)
        number = number + (pltpu.roll(number, 126, 1) << 9) + (pltpu.roll(number, 127, 1) << 17)
        for k in range(4):
            at = TAG_LANE + 3 * k
            value = jnp.broadcast_to(number[:, at : at + 1], (8, 128))
            code = (value >> 9) + ((8 * c + row) << 16)
            for h in range(LINKS // 128):
                found[h] = found[h] + jnp.where((value & 511) == link + 128 * h, code, 0)
    for h in range(LINKS // 128):
        table[h : h + 1, :] = jnp.sum(found[h], axis=0, keepdims=True)
    copy = pltpu.make_async_copy(table, table_s, sem)
    copy.start()

    def clear(i, carry):
        raw[i] = jnp.zeros((RESP, 128), jnp.float32)
        return carry

    lax.fori_loop(0, CELL_SECTORS, clear, 0, unroll=4)
    for c in range(CELLS // 8):
        extra = got[pl.ds(64 * c + 4, 8, stride=8), :]
        for f in range(4):
            over[pl.ds(64 * c + f, 8, stride=8), :] = extra if f == 0 else pltpu.roll(extra, 128 - 2 * f, 1)
    copy.wait()

    def load(source):
        at = pl.ds(pl.multiple_of(8 * source, 8), 8)
        return got[at, :], over[at, :]

    def serve(u, carry):
        g = u * NEARBY_COUNT + slots[u]
        code = table_s[g >> 7, g & 127]
        serving[pl.ds(pl.multiple_of(8 * u, 8), 8), :] = unpacked(code, load)
        return carry

    lax.fori_loop(0, USERS, serve, 0, unroll=8)

    seeds = (e_seed, s_seed, coef), (e_seed2, s_seed2, coef2)

    def prepare(c):
        fields = [serving[pl.ds(64 * c + f, 8, stride=8), :] for f in range(4)]
        seeds_of(fields, grp, *seeds[c % 2])

    prepare(0)
    for c in range(USERS // 8):
        if c + 1 < USERS // 8:
            prepare(c + 1)
        for l in range(8):
            u = 8 * c + l
            resp = response_of(l, *seeds[c % 2]).astype(jnp.bfloat16).astype(jnp.float32)
            sym = symbols[u].astype(jnp.float32)
            sym_r, sym_i = sym[0:1, :], sym[1:2, :]
            real, imag = resp[:ANT, :], resp[ANT:, :]
            part = jnp.concatenate(
                [real * sym_r + imag * sym_i, real * sym_i - imag * sym_r], axis=0
            )
            sector = nearby[slots[u], u] - me * CELL_SECTORS
            raw[sector] = raw[sector] + part


PIECE = 8
PIECES = (0, 16, 8, 24)


def receive_kernel(
    nearby, table, got, over, raw, out, near, resp, part, other,
    e_seed, s_seed, coef, e_seed2, s_seed2, coef2, rows, rows2, send_sems, recv_sems
):
    me = lax.axis_index("cell")
    grp = lax.axis_index("grp")
    right = lax.rem(me + 1, CELLS)
    left = lax.rem(me + CELLS - 1, CELLS)
    barrier = pltpu.get_barrier_semaphore()
    for target in ({"cell": left}, {"cell": right}, {"grp": 1 - grp}):
        pl.semaphore_signal(barrier, inc=1, device_id=target, device_id_type=MESH)

    halo = []
    for n, begin in enumerate(PIECES):

        def normalise(s, carry):
            real, imag = raw[s, :ANT, :], raw[s, ANT:, :]
            power = jnp.mean(real * real + imag * imag, axis=1, keepdims=True)
            scale = 1.0 / jnp.sqrt(power + EPSILON)
            near[REACH + s] = jnp.concatenate([real * scale, imag * scale], axis=0).astype(jnp.bfloat16)
            return carry

        lax.fori_loop(begin, begin + PIECE, normalise, 0, unroll=4)
        if n == 0:
            pl.semaphore_wait(barrier, 3)
        to_left = begin < CELL_SECTORS - REACH
        land = begin + REACH + CELL_SECTORS if to_left else begin + REACH - CELL_SECTORS
        halo.append(
            pltpu.make_async_remote_copy(
                src_ref=near.at[pl.ds(REACH + begin, PIECE)],
                dst_ref=near.at[pl.ds(land, PIECE)],
                send_sem=send_sems.at[n],
                recv_sem=recv_sems.at[n],
                device_id={"cell": left if to_left else right},
                device_id_type=MESH,
            )
        )
        halo[-1].start()

    first, second = (e_seed, s_seed, coef), (e_seed2, s_seed2, coef2)

    def unpack(u, rows):
        u = jnp.minimum(u, USERS - 1)
        for l in range(8):
            code = table[u // 16, lax.rem(u, 16) * 8 + l]
            rows[8 * l : 8 * l + 8, :] = unpacked(code, lambda i: (got[i], over[i]))

    def prepare(rows, seeds):
        seeds_of([rows[pl.ds(f, 8, stride=8), :] for f in range(4)], grp, *seeds)

    def respond(u, seeds):
        for l in range(8):
            at = pl.ds(pl.multiple_of(u * (8 * RESP) + RESP * l, RESP), RESP)
            resp[at, :] = response_of(l, *seeds).astype(jnp.bfloat16)

    def two_users(v, carry):
        prepare(rows2, second)
        unpack(2 * v + 3, rows2)
        respond(2 * v, first)
        prepare(rows, first)
        unpack(2 * v + 4, rows)
        respond(2 * v + 1, second)
        return carry

    unpack(0, rows)
    prepare(rows, first)
    unpack(1, rows2)
    unpack(2, rows)
    lax.fori_loop(0, USERS // 2, two_users, 0)
    for copy in halo:
        copy.wait()

    def combine(u, carry):
        real = jnp.zeros((ANT, 128), jnp.float32)
        imag = jnp.zeros((ANT, 128), jnp.float32)
        for k in range(NEARBY_COUNT):
            sector = nearby[k, u] - me * CELL_SECTORS + REACH
            sector = jnp.clip(sector, 0, CELL_SECTORS + 2 * REACH - 1)
            tx = near[sector].astype(jnp.float32)
            at = pl.ds(pl.multiple_of(u * (8 * RESP) + RESP * k, RESP), RESP)
            ch = resp[at, :].astype(jnp.float32)
            real = real + (ch[:ANT] * tx[:ANT] - ch[ANT:] * tx[ANT:])
            imag = imag + (ch[:ANT] * tx[ANT:] + ch[ANT:] * tx[:ANT])
        part[u] = jnp.concatenate(
            [jnp.sum(real, axis=0, keepdims=True), jnp.sum(imag, axis=0, keepdims=True)], axis=0
        )
        return carry

    lax.fori_loop(0, USERS, combine, 0)
    swap = pltpu.make_async_remote_copy(
        src_ref=part,
        dst_ref=other,
        send_sem=send_sems.at[len(PIECES)],
        recv_sem=recv_sems.at[len(PIECES)],
        device_id={"grp": 1 - grp},
        device_id_type=MESH,
    )
    swap.start()
    swap.wait()
    out[...] = (part[...] + other[...]) * (1.0 / math.sqrt(SECTOR_ANTENNAS))


VMEM = pl.BlockSpec(memory_space=pltpu.VMEM)
SMEM = pl.BlockSpec(memory_space=pltpu.SMEM)


def call(kernel, name, mib, out_shape, in_specs, scratch, remote=None):
    extra = {} if remote is None else {"collective_id": remote, "has_side_effects": True}
    many = isinstance(out_shape, (tuple, list))
    return pl.pallas_call(
        kernel,
        name=name,
        out_shape=out_shape,
        in_specs=in_specs,
        out_specs=[VMEM] * len(out_shape) if many else VMEM,
        scratch_shapes=scratch,
        compiler_params=pltpu.CompilerParams(vmem_limit_bytes=mib * MIB, **extra),
    )


def shards(
    path_delay,
    path_angle,
    path_gain,
    slot_counts,
    slot_offsets,
    ray_link,
    nearby_sectors,
    serving_slot,
    symbols,
):
    f32, bf16, i32 = jnp.float32, jnp.bfloat16, jnp.int32
    got = call(
        deliver_kernel,
        "deliver",
        16,
        jax.ShapeDtypeStruct((CELLS, 8, 128), f32),
        [SMEM, SMEM, SMEM, VMEM],
        [
            pltpu.VMEM((PATH_ROWS + 1, 8, 128), f32),
            pltpu.VMEM((HALF, 8, 128), f32),
            pltpu.SMEM((HALF + 1,), i32),
            pltpu.SemaphoreType.DMA((4,)),
        ],
        remote=0,
    )(
        slot_counts,
        slot_offsets,
        ray_link,
        jnp.stack((path_delay, path_angle, path_gain[0], path_gain[1])).reshape(4, PATH_ROWS, 128),
    )
    over, table, raw = call(
        transmit_kernel,
        "transmit",
        24,
        (
            jax.ShapeDtypeStruct((CELLS * 8, 128), f32),
            jax.ShapeDtypeStruct((LINKS // 128, 128), i32),
            jax.ShapeDtypeStruct((CELL_SECTORS, RESP, 128), f32),
        ),
        [SMEM, SMEM, VMEM, VMEM],
        [
            pltpu.SMEM((LINKS // 128, 128), i32),
            pltpu.VMEM((USERS * 8, 128), f32),
            *SEED_SCRATCH,
            *SEED_SCRATCH,
            pltpu.SemaphoreType.DMA,
        ],
    )(serving_slot, nearby_sectors, got.reshape(CELLS * 8, 128), symbols)
    return call(
        receive_kernel,
        "receive",
        24,
        jax.ShapeDtypeStruct((USERS, 2, FRAME_TONES), f32),
        [SMEM, SMEM, VMEM, VMEM, VMEM],
        [
            pltpu.VMEM((CELL_SECTORS + 2 * REACH, RESP, 128), bf16),
            pltpu.VMEM((LINKS * RESP, 128), bf16),
            pltpu.VMEM((USERS, 2, FRAME_TONES), f32),
            pltpu.VMEM((USERS, 2, FRAME_TONES), f32),
            *SEED_SCRATCH,
            *SEED_SCRATCH,
            pltpu.VMEM((64, 128), f32),
            pltpu.VMEM((64, 128), f32),
            pltpu.SemaphoreType.DMA((len(PIECES) + 1,)),
            pltpu.SemaphoreType.DMA((len(PIECES) + 1,)),
        ],
        remote=1,
    )(nearby_sectors, table, got, over.reshape(CELLS, 8, 128), raw)


def solution(mesh):
    placed = (
        P("cell"),
        P("cell"),
        P(None, "cell"),
        P("cell"),
        P("cell"),
        P("cell"),
        P(None, "cell"),
        P("cell"),
        P("cell", None, None),
    )
    return jax.shard_map(
        shards, mesh=mesh, in_specs=placed, out_specs=P("cell", None, None), check_vma=False
    )
```

```python
import functools
import math

import jax
import jax.numpy as jnp
from jax import lax
from jax.experimental import pallas as pl
from jax.experimental.pallas import tpu as pltpu
from jax.sharding import PartitionSpec as P

SECTOR_ANTENNAS = 64
FRAME_TONES = 128
NEARBY_COUNT = 8
CELL_SECTORS = 32
REACH = 16
EPSILON = 1e-06

CELLS = 128
SLOTS = 256
USERS = 32
LINKS = USERS * NEARBY_COUNT
PATH_ROWS = 65
ANT = SECTOR_ANTENNAS // 2
RESP = 2 * ANT
TAG_LANE = 8
HALF = CELLS // 2
WIRE_ROWS = 5
MIB = 1024 * 1024
MESH = pl.DeviceIdType.MESH


def lanes(shape):
    return lax.broadcasted_iota(jnp.int32, shape, len(shape) - 1)


def rows_of(shape):
    return lax.broadcasted_iota(jnp.int32, shape, len(shape) - 2)


def sincos_turns(turns):
    r = turns - jnp.round(turns)
    r2 = r * r
    sin_c = [(-1) ** n * math.pi ** (2 * n + 1) / math.factorial(2 * n + 1) for n in range(7)]
    cos_c = [(-1) ** n * math.pi ** (2 * n) / math.factorial(2 * n) for n in range(7)]
    sh = jnp.full_like(r, sin_c[-1])
    ch = jnp.full_like(r, cos_c[-1])
    for n in range(5, -1, -1):
        sh = sh * r2 + sin_c[n]
        ch = ch * r2 + cos_c[n]
    sh = sh * r
    return 2.0 * sh * ch, 1.0 - 2.0 * sh * sh


def my_half():
    return lax.rem(lax.axis_index("grp") + lax.axis_index("cell") // HALF, 2)


def deliver_kernel(
    counts, offsets, links, _slots, fields, got, store, sent, begins, sems
):
    me = lax.axis_index("cell")
    grp = lax.axis_index("grp")
    start = my_half() * HALF
    sibling = {"grp": 1 - grp}
    barrier = pltpu.get_barrier_semaphore()
    pl.semaphore_signal(barrier, inc=1, device_id=sibling, device_id_type=MESH)

    def greet(d, carry):
        other = start + lax.rem(me + d, HALF)
        pl.semaphore_signal(barrier, inc=1, device_id={"cell": other}, device_id_type=MESH)
        return carry

    @pl.when(grp == 1)
    def _():
        greet(0, 0)

    lax.fori_loop(1, HALF, greet, 0, unroll=9)

    def narrow(_, carry):
        low, top = carry
        mid = (low + top) >> 1
        below = (links[jnp.minimum(mid, SLOTS - 1)] >> 8) < start
        below = below & (low < top)
        return jnp.where(below, mid + 1, low), jnp.where(below, top, mid)

    at, _ = lax.fori_loop(0, 9, narrow, (jnp.int32(0), jnp.int32(SLOTS)))

    def count(o, at):
        begins[o] = at
        total = at
        for k in range(4):
            slot = at + k
            mine = (links[jnp.minimum(slot, SLOTS - 1)] >> 8) == start + o
            total = total + jnp.where(mine & (slot < SLOTS), 1, 0)
        return total

    begins[HALF] = lax.fori_loop(0, HALF, count, at, unroll=4)

    for c in range(0, PATH_ROWS, 8):
        n = min(8, PATH_ROWS - c)
        for f in range(4):
            value = fields[f, c : c + n, :]
            if f < 2:
                value = value * (1.0 / FRAME_TONES) if f == 0 else jnp.sin(value)
            store[c : c + n, f, :] = value
            store[c : c + n, 4 + f, :] = value
    store[PATH_ROWS] = jnp.zeros((8, 128), jnp.float32)

    lane = lanes((8, 128))
    row = rows_of((8, 128))
    place = lane + jnp.where(row >= 4, 128, 0)
    tag_place = jnp.where(row == 4, lane - TAG_LANE, -1000)

    def pack(o, carry):
        first = begins[o]
        number = begins[o + 1] - first
        base = jnp.int32(0)
        message = jnp.zeros((8, 128), jnp.float32)
        for k in range(4):
            r = jnp.minimum(first + k, SLOTS - 1)
            cnt = jnp.where(k < number, counts[r], 0)
            tag = jnp.where(k < number, (links[r] & 255) + 1, 0)
            off = offsets[r]
            q = off >> 7
            s = off & 127
            value = jnp.where(lane < s + cnt - 128, store[q + 1], store[q])
            value = pltpu.roll(value, (base - s) & 127, 1)
            j = place - base
            message = jnp.where((j >= 0) & (j < cnt), value, message)
            for n, number_sent in enumerate((tag, cnt, base)):
                message = jnp.where(tag_place == 3 * k + n, number_sent.astype(jnp.float32), message)
            base = base + cnt
        sent[o] = message
        return carry

    lax.fori_loop(0, HALF, pack, 0, unroll=4)
    for c in range(0, HALF, 8):
        total = sent[c : c + 8, 4, :]
        for f in range(1, 4):
            total = total + pltpu.roll(sent[c : c + 8, 4 + f, :], 2 * f, 1)
        sent[c : c + 8, 4, :] = total

    @pl.when(grp == 0)
    def _():
        got[me] = sent[lax.rem(me, HALF)]

    pl.semaphore_wait(barrier, HALF + grp)
    wire = pl.ds(0, WIRE_ROWS)

    def send(d, carry):
        near = lax.rem(me + d, HALF)
        pltpu.make_async_remote_copy(
            src_ref=sent.at[near, wire],
            dst_ref=got.at[me, wire],
            send_sem=sems.at[0],
            recv_sem=sems.at[1],
            device_id={"cell": start + near},
            device_id_type=MESH,
        ).start()
        return carry

    lax.fori_loop(1 - grp, HALF, send, 0)

    for g in range(2):

        @pl.when(grp == g)
        def _():
            whole = pltpu.make_async_remote_copy(
                src_ref=sent.at[pl.ds(0, HALF - 1 + g), wire],
                dst_ref=got.at[pl.ds(start, HALF - 1 + g), wire],
                send_sem=sems.at[0],
                recv_sem=sems.at[1],
                device_id=sibling,
                device_id_type=MESH,
            )
            whole.wait_recv()
            whole.wait_send()

    swap = pltpu.make_async_remote_copy(
        src_ref=got.at[pl.ds(start, HALF), wire],
        dst_ref=got.at[pl.ds(start, HALF), wire],
        send_sem=sems.at[2],
        recv_sem=sems.at[3],
        device_id=sibling,
        device_id_type=MESH,
    )
    swap.start()
    swap.wait()


def seeds_of(fields, grp, e_seed, s_seed, coef):
    turns, sine, real, imag = [v + pltpu.roll(v, 64, 1) for v in fields]
    hi = lanes((8, 128)) >= 64
    s1, c1 = sincos_turns(turns)
    e = jnp.where(hi, 0.0, 1.0)
    f = jnp.where(hi, 1.0, 0.0)
    e_seed[pl.ds(8, 8, stride=16), :] = e
    for j in range(1, 9):
        e, f = e * c1 - f * s1, f * c1 + e * s1
        if j < 8:
            e_seed[pl.ds(8 + j, 8, stride=16), :] = e
        e_seed[pl.ds(8 - j, 8, stride=16), :] = jnp.where(hi, -e, e)
    _, c8 = sincos_turns(8.0 * turns)
    coef[0:8, :] = 2.0 * c8
    sa, ca = sincos_turns(0.5 * sine)
    first = (grp * (ANT // 2)).astype(jnp.float32)
    s0, c0 = sincos_turns(first * sine)
    _, a8 = sincos_turns(4.0 * sine)
    coef[8:16, :] = 2.0 * a8
    g1 = jnp.where(hi, -imag, real)
    g2 = jnp.where(hi, real, imag)
    x = g1 * c0 + g2 * s0
    y = g2 * c0 - g1 * s0
    for a in range(16):
        s_seed[pl.ds(a, 8, stride=32), :] = x
        s_seed[pl.ds(16 + a, 8, stride=32), :] = y
        if a < 15:
            x, y = x * ca + y * sa, y * ca - x * sa


def response_of(l, e_seed, s_seed, coef):
    c = jnp.broadcast_to(coef[l : l + 1, :], (8, 128))
    low = e_seed[16 * l : 16 * l + 8, :]
    top = e_seed[16 * l + 8 : 16 * l + 16, :]
    down = [top, low]
    up = [low, top]
    for _ in range(7):
        down.append(c * down[-1] - down[-2])
        up.append(c * up[-1] - up[-2])
    table = jnp.concatenate(down[:0:-1] + up[1:], axis=0).astype(jnp.bfloat16)
    c = jnp.broadcast_to(coef[8 + l : 9 + l, :], (8, 128))
    parts = []
    for h in range(2):
        at = 32 * l + 16 * h
        run = [s_seed[at : at + 8, :], s_seed[at + 8 : at + 16, :]]
        for _ in range(2):
            run.append(c * run[-1] - run[-2])
        parts += run
    spread = jnp.concatenate(parts, axis=0).astype(jnp.bfloat16)
    return lax.dot_general(
        spread, table, (((1,), (1,)), ((), ())), preferred_element_type=jnp.float32
    )


SEED_SCRATCH = [
    pltpu.VMEM((8 * 16, 128), jnp.float32),
    pltpu.VMEM((8 * 32, 128), jnp.float32),
    pltpu.VMEM((16, 128), jnp.float32),
]


def unpacked(code, load):
    base = code & 255
    cnt = (code >> 8) & 255
    lane = lanes((8, 128))
    message, overflow = load(code >> 16)
    value = jnp.where(lane < base + cnt - 128, overflow, message)
    return jnp.where(lane < cnt, pltpu.roll(value, (0 - base) & 127, 1), 0.0)


def transmit_kernel(
    slots, nearby, got, symbols, over, table, raw, table_s, serving,
    e_seed, s_seed, coef, e_seed2, s_seed2, coef2, sem
):
    me = lax.axis_index("cell")
    grp = lax.axis_index("grp")
    lane = lanes((8, 128))
    row = rows_of((8, 128))
    is_tag = (lane >= TAG_LANE) & (lane < TAG_LANE + 12)
    link = lane + 1
    found = [jnp.zeros((8, 128), jnp.int32) for _ in range(LINKS // 128)]
    for c in range(CELLS // 8):
        extra = got[pl.ds(64 * c + 4, 8, stride=8), :]
        number = jnp.where(is_tag, extra, 0.0).astype(jnp.int32)
        number = number + (pltpu.roll(number, 126, 1) << 9) + (pltpu.roll(number, 127, 1) << 17)
        for k in range(4):
            at = TAG_LANE + 3 * k
            value = jnp.broadcast_to(number[:, at : at + 1], (8, 128))
            code = (value >> 9) + ((8 * c + row) << 16)
            for h in range(LINKS // 128):
                found[h] = found[h] + jnp.where((value & 511) == link + 128 * h, code, 0)
    for h in range(LINKS // 128):
        table[h : h + 1, :] = jnp.sum(found[h], axis=0, keepdims=True)
    copy = pltpu.make_async_copy(table, table_s, sem)
    copy.start()

    def clear(i, carry):
        raw[i] = jnp.zeros((RESP, 128), jnp.float32)
        return carry

    lax.fori_loop(0, CELL_SECTORS, clear, 0, unroll=4)
    for c in range(CELLS // 8):
        extra = got[pl.ds(64 * c + 4, 8, stride=8), :]
        for f in range(4):
            over[pl.ds(64 * c + f, 8, stride=8), :] = extra if f == 0 else pltpu.roll(extra, 128 - 2 * f, 1)
    copy.wait()

    def load(source):
        at = pl.ds(pl.multiple_of(8 * source, 8), 8)
        return got[at, :], over[at, :]

    def serve(u, carry):
        g = u * NEARBY_COUNT + slots[u]
        code = table_s[g >> 7, g & 127]
        serving[pl.ds(pl.multiple_of(8 * u, 8), 8), :] = unpacked(code, load)
        return carry

    lax.fori_loop(0, USERS, serve, 0, unroll=8)

    seeds = (e_seed, s_seed, coef), (e_seed2, s_seed2, coef2)

    def prepare(c):
        fields = [serving[pl.ds(64 * c + f, 8, stride=8), :] for f in range(4)]
        seeds_of(fields, grp, *seeds[c % 2])

    prepare(0)
    for c in range(USERS // 8):
        if c + 1 < USERS // 8:
            prepare(c + 1)
        for l in range(8):
            u = 8 * c + l
            resp = response_of(l, *seeds[c % 2]).astype(jnp.bfloat16).astype(jnp.float32)
            sym = symbols[u].astype(jnp.float32)
            sym_r, sym_i = sym[0:1, :], sym[1:2, :]
            real, imag = resp[:ANT, :], resp[ANT:, :]
            part = jnp.concatenate(
                [real * sym_r + imag * sym_i, real * sym_i - imag * sym_r], axis=0
            )
            sector = nearby[slots[u], u] - me * CELL_SECTORS
            raw[sector] = raw[sector] + part


PIECE = 8
PIECES = (0, 16, 8, 24)


def receive_kernel(
    nearby, table, got, over, raw, out, near, resp, part, other,
    e_seed, s_seed, coef, e_seed2, s_seed2, coef2, rows, rows2, send_sems, recv_sems
):
    me = lax.axis_index("cell")
    grp = lax.axis_index("grp")
    right = lax.rem(me + 1, CELLS)
    left = lax.rem(me + CELLS - 1, CELLS)
    barrier = pltpu.get_barrier_semaphore()
    for target in ({"cell": left}, {"cell": right}, {"grp": 1 - grp}):
        pl.semaphore_signal(barrier, inc=1, device_id=target, device_id_type=MESH)

    halo = []
    for n, begin in enumerate(PIECES):

        def normalise(s, carry):
            real, imag = raw[s, :ANT, :], raw[s, ANT:, :]
            power = jnp.mean(real * real + imag * imag, axis=1, keepdims=True)
            scale = 1.0 / jnp.sqrt(power + EPSILON)
            near[REACH + s] = jnp.concatenate([real * scale, imag * scale], axis=0).astype(jnp.bfloat16)
            return carry

        lax.fori_loop(begin, begin + PIECE, normalise, 0, unroll=8)
        if n == 0:
            pl.semaphore_wait(barrier, 3)
        to_left = begin < CELL_SECTORS - REACH
        land = begin + REACH + CELL_SECTORS if to_left else begin + REACH - CELL_SECTORS
        halo.append(
            pltpu.make_async_remote_copy(
                src_ref=near.at[pl.ds(REACH + begin, PIECE)],
                dst_ref=near.at[pl.ds(land, PIECE)],
                send_sem=send_sems.at[n],
                recv_sem=recv_sems.at[n],
                device_id={"cell": left if to_left else right},
                device_id_type=MESH,
            )
        )
        halo[-1].start()

    first, second = (e_seed, s_seed, coef), (e_seed2, s_seed2, coef2)

    def unpack(u, rows):
        u = jnp.minimum(u, USERS - 1)
        for l in range(8):
            code = table[u // 16, lax.rem(u, 16) * 8 + l]
            rows[8 * l : 8 * l + 8, :] = unpacked(code, lambda i: (got[i], over[i]))

    def prepare(rows, seeds):
        seeds_of([rows[pl.ds(f, 8, stride=8), :] for f in range(4)], grp, *seeds)

    def respond(u, seeds):
        for l in range(8):
            at = pl.ds(pl.multiple_of(u * (8 * RESP) + RESP * l, RESP), RESP)
            resp[at, :] = response_of(l, *seeds).astype(jnp.bfloat16)

    def two_users(v, carry):
        prepare(rows2, second)
        unpack(2 * v + 3, rows2)
        respond(2 * v, first)
        prepare(rows, first)
        unpack(2 * v + 4, rows)
        respond(2 * v + 1, second)
        return carry

    unpack(0, rows)
    prepare(rows, first)
    unpack(1, rows2)
    unpack(2, rows)
    lax.fori_loop(0, USERS // 2, two_users, 0)
    for copy in halo:
        copy.wait()

    def combine(u, carry):
        real = jnp.zeros((ANT, 128), jnp.float32)
        imag = jnp.zeros((ANT, 128), jnp.float32)
        for k in range(NEARBY_COUNT):
            sector = nearby[k, u] - me * CELL_SECTORS + REACH
            sector = jnp.clip(sector, 0, CELL_SECTORS + 2 * REACH - 1)
            tx = near[sector].astype(jnp.float32)
            at = pl.ds(pl.multiple_of(u * (8 * RESP) + RESP * k, RESP), RESP)
            ch = resp[at, :].astype(jnp.float32)
            real = real + (ch[:ANT] * tx[:ANT] - ch[ANT:] * tx[ANT:])
            imag = imag + (ch[:ANT] * tx[ANT:] + ch[ANT:] * tx[:ANT])
        part[u] = jnp.concatenate(
            [jnp.sum(real, axis=0, keepdims=True), jnp.sum(imag, axis=0, keepdims=True)], axis=0
        )
        return carry

    lax.fori_loop(0, USERS, combine, 0, unroll=4)
    swap = pltpu.make_async_remote_copy(
        src_ref=part,
        dst_ref=other,
        send_sem=send_sems.at[len(PIECES)],
        recv_sem=recv_sems.at[len(PIECES)],
        device_id={"grp": 1 - grp},
        device_id_type=MESH,
    )
    swap.start()
    swap.wait()
    out[...] = (part[...] + other[...]) * (1.0 / math.sqrt(SECTOR_ANTENNAS))


VMEM = pl.BlockSpec(memory_space=pltpu.VMEM)
SMEM = pl.BlockSpec(memory_space=pltpu.SMEM)


def call(kernel, name, mib, out_shape, in_specs, scratch, remote=None):
    extra = {} if remote is None else {"collective_id": remote, "has_side_effects": True}
    many = isinstance(out_shape, (tuple, list))
    return pl.pallas_call(
        kernel,
        name=name,
        out_shape=out_shape,
        in_specs=in_specs,
        out_specs=[VMEM] * len(out_shape) if many else VMEM,
        scratch_shapes=scratch,
        compiler_params=pltpu.CompilerParams(vmem_limit_bytes=mib * MIB, **extra),
    )


def shards(
    path_delay,
    path_angle,
    path_gain,
    slot_counts,
    slot_offsets,
    ray_link,
    nearby_sectors,
    serving_slot,
    symbols,
):
    f32, bf16, i32 = jnp.float32, jnp.bfloat16, jnp.int32
    got = call(
        deliver_kernel,
        "deliver",
        16,
        jax.ShapeDtypeStruct((CELLS, 8, 128), f32),
        [SMEM, SMEM, SMEM, SMEM, VMEM],
        [
            pltpu.VMEM((PATH_ROWS + 1, 8, 128), f32),
            pltpu.VMEM((HALF, 8, 128), f32),
            pltpu.SMEM((HALF + 1,), i32),
            pltpu.SemaphoreType.DMA((4,)),
        ],
        remote=0,
    )(
        slot_counts,
        slot_offsets,
        ray_link,
        serving_slot,
        jnp.stack((path_delay, path_angle, path_gain[0], path_gain[1])).reshape(4, PATH_ROWS, 128),
    )
    over, table, raw = call(
        transmit_kernel,
        "transmit",
        24,
        (
            jax.ShapeDtypeStruct((CELLS * 8, 128), f32),
            jax.ShapeDtypeStruct((LINKS // 128, 128), i32),
            jax.ShapeDtypeStruct((CELL_SECTORS, RESP, 128), f32),
        ),
        [SMEM, SMEM, VMEM, VMEM],
        [
            pltpu.SMEM((LINKS // 128, 128), i32),
            pltpu.VMEM((USERS * 8, 128), f32),
            *SEED_SCRATCH,
            *SEED_SCRATCH,
            pltpu.SemaphoreType.DMA,
        ],
    )(serving_slot, nearby_sectors, got.reshape(CELLS * 8, 128), symbols)
    return call(
        receive_kernel,
        "receive",
        24,
        jax.ShapeDtypeStruct((USERS, 2, FRAME_TONES), f32),
        [SMEM, SMEM, VMEM, VMEM, VMEM],
        [
            pltpu.VMEM((CELL_SECTORS + 2 * REACH, RESP, 128), bf16),
            pltpu.VMEM((LINKS * RESP, 128), bf16),
            pltpu.VMEM((USERS, 2, FRAME_TONES), f32),
            pltpu.VMEM((USERS, 2, FRAME_TONES), f32),
            *SEED_SCRATCH,
            *SEED_SCRATCH,
            pltpu.VMEM((64, 128), f32),
            pltpu.VMEM((64, 128), f32),
            pltpu.SemaphoreType.DMA((len(PIECES) + 1,)),
            pltpu.SemaphoreType.DMA((len(PIECES) + 1,)),
        ],
        remote=1,
    )(nearby_sectors, table, got, over.reshape(CELLS, 8, 128), raw)


def solution(mesh):
    placed = (
        P("cell"),
        P("cell"),
        P(None, "cell"),
        P("cell"),
        P("cell"),
        P("cell"),
        P(None, "cell"),
        P("cell"),
        P("cell", None, None),
    )
    return jax.shard_map(
        shards, mesh=mesh, in_specs=placed, out_specs=P("cell", None, None), check_vma=False
    )
```

```python
import functools
import math

import jax
import jax.numpy as jnp
from jax import lax
from jax.experimental import pallas as pl
from jax.experimental.pallas import tpu as pltpu
from jax.sharding import PartitionSpec as P

SECTOR_ANTENNAS = 64
FRAME_TONES = 128
NEARBY_COUNT = 8
CELL_SECTORS = 32
REACH = 16
EPSILON = 1e-06

CELLS = 128
SLOTS = 256
USERS = 32
LINKS = USERS * NEARBY_COUNT
PATH_ROWS = 65
ANT = SECTOR_ANTENNAS // 2
RESP = 2 * ANT
TAG_LANE = 8
HALF = CELLS // 2
WIRE_ROWS = 5
MIB = 1024 * 1024
MESH = pl.DeviceIdType.MESH


def lanes(shape):
    return lax.broadcasted_iota(jnp.int32, shape, len(shape) - 1)


def rows_of(shape):
    return lax.broadcasted_iota(jnp.int32, shape, len(shape) - 2)


def sincos_turns(turns):
    r = turns - jnp.round(turns)
    r2 = r * r
    sin_c = [(-1) ** n * math.pi ** (2 * n + 1) / math.factorial(2 * n + 1) for n in range(7)]
    cos_c = [(-1) ** n * math.pi ** (2 * n) / math.factorial(2 * n) for n in range(7)]
    sh = jnp.full_like(r, sin_c[-1])
    ch = jnp.full_like(r, cos_c[-1])
    for n in range(5, -1, -1):
        sh = sh * r2 + sin_c[n]
        ch = ch * r2 + cos_c[n]
    sh = sh * r
    return 2.0 * sh * ch, 1.0 - 2.0 * sh * sh


def my_half():
    return lax.rem(lax.axis_index("grp") + lax.axis_index("cell") // HALF, 2)


def deliver_kernel(
    counts_in, offsets_in, links_in, _slots, fields, got,
    counts, offsets, links, store, sent, begins, load_sems, sems
):
    me = lax.axis_index("cell")
    grp = lax.axis_index("grp")
    start = my_half() * HALF
    sibling = {"grp": 1 - grp}
    loads = [
        pltpu.make_async_copy(src, dst, load_sems.at[n])
        for n, (src, dst) in enumerate(((counts_in, counts), (offsets_in, offsets), (links_in, links)))
    ]
    for copy in loads:
        copy.start()
    barrier = pltpu.get_barrier_semaphore()
    pl.semaphore_signal(barrier, inc=1, device_id=sibling, device_id_type=MESH)

    def greet(d, carry):
        other = start + lax.rem(me + d, HALF)
        pl.semaphore_signal(barrier, inc=1, device_id={"cell": other}, device_id_type=MESH)
        return carry

    @pl.when(grp == 1)
    def _():
        greet(0, 0)

    lax.fori_loop(1, HALF, greet, 0, unroll=9)

    for copy in loads:
        copy.wait()

    def narrow(_, carry):
        low, top = carry
        mid = (low + top) >> 1
        below = (links[jnp.minimum(mid, SLOTS - 1)] >> 8) < start
        below = below & (low < top)
        return jnp.where(below, mid + 1, low), jnp.where(below, top, mid)

    at, _ = lax.fori_loop(0, 9, narrow, (jnp.int32(0), jnp.int32(SLOTS)))

    def count(o, at):
        begins[o] = at
        total = at
        for k in range(4):
            slot = at + k
            mine = (links[jnp.minimum(slot, SLOTS - 1)] >> 8) == start + o
            total = total + jnp.where(mine & (slot < SLOTS), 1, 0)
        return total

    begins[HALF] = lax.fori_loop(0, HALF, count, at, unroll=4)

    for c in range(0, PATH_ROWS, 8):
        n = min(8, PATH_ROWS - c)
        for f in range(4):
            value = fields[f, c : c + n, :]
            if f < 2:
                value = value * (1.0 / FRAME_TONES) if f == 0 else jnp.sin(value)
            store[c : c + n, f, :] = value
            store[c : c + n, 4 + f, :] = value
    store[PATH_ROWS] = jnp.zeros((8, 128), jnp.float32)

    lane = lanes((8, 128))
    row = rows_of((8, 128))
    place = lane + jnp.where(row >= 4, 128, 0)
    tag_place = jnp.where(row == 4, lane - TAG_LANE, -1000)

    def pack(o, carry):
        first = begins[o]
        number = begins[o + 1] - first
        base = jnp.int32(0)
        message = jnp.zeros((8, 128), jnp.float32)
        for k in range(4):
            r = jnp.minimum(first + k, SLOTS - 1)
            cnt = jnp.where(k < number, counts[r], 0)
            tag = jnp.where(k < number, (links[r] & 255) + 1, 0)
            off = offsets[r]
            q = off >> 7
            s = off & 127
            value = jnp.where(lane < s + cnt - 128, store[q + 1], store[q])
            value = pltpu.roll(value, (base - s) & 127, 1)
            j = place - base
            message = jnp.where((j >= 0) & (j < cnt), value, message)
            for n, number_sent in enumerate((tag, cnt, base)):
                message = jnp.where(tag_place == 3 * k + n, number_sent.astype(jnp.float32), message)
            base = base + cnt
        sent[o] = message
        return carry

    lax.fori_loop(0, HALF, pack, 0, unroll=4)
    for c in range(0, HALF, 8):
        total = sent[c : c + 8, 4, :]
        for f in range(1, 4):
            total = total + pltpu.roll(sent[c : c + 8, 4 + f, :], 2 * f, 1)
        sent[c : c + 8, 4, :] = total

    @pl.when(grp == 0)
    def _():
        got[me] = sent[lax.rem(me, HALF)]

    pl.semaphore_wait(barrier, HALF + grp)
    wire = pl.ds(0, WIRE_ROWS)

    def send(hops, q, carry):
        near = lax.rem(me + 8 * q + hops, HALF)
        pltpu.make_async_remote_copy(
            src_ref=sent.at[near, wire],
            dst_ref=got.at[me, wire],
            send_sem=sems.at[0],
            recv_sem=sems.at[1],
            device_id={"cell": start + near},
            device_id_type=MESH,
        ).start()
        return carry

    for hops in (4, 3, 5, 2, 6, 1, 7):
        lax.fori_loop(0, HALF // 8, functools.partial(send, hops), 0, unroll=4)
    lax.fori_loop(1 - grp, HALF // 8, functools.partial(send, 0), 0)

    for g in range(2):

        @pl.when(grp == g)
        def _():
            whole = pltpu.make_async_remote_copy(
                src_ref=sent.at[pl.ds(0, HALF - 1 + g), wire],
                dst_ref=got.at[pl.ds(start, HALF - 1 + g), wire],
                send_sem=sems.at[0],
                recv_sem=sems.at[1],
                device_id=sibling,
                device_id_type=MESH,
            )
            whole.wait_recv()
            whole.wait_send()

    swap = pltpu.make_async_remote_copy(
        src_ref=got.at[pl.ds(start, HALF), wire],
        dst_ref=got.at[pl.ds(start, HALF), wire],
        send_sem=sems.at[2],
        recv_sem=sems.at[3],
        device_id=sibling,
        device_id_type=MESH,
    )
    swap.start()
    swap.wait()


def seeds_of(fields, grp, e_seed, s_seed, coef):
    turns, sine, real, imag = [v + pltpu.roll(v, 64, 1) for v in fields]
    hi = lanes((8, 128)) >= 64
    s1, c1 = sincos_turns(turns)
    e = jnp.where(hi, 0.0, 1.0)
    f = jnp.where(hi, 1.0, 0.0)
    e_seed[pl.ds(8, 8, stride=16), :] = e
    for j in range(1, 9):
        e, f = e * c1 - f * s1, f * c1 + e * s1
        if j < 8:
            e_seed[pl.ds(8 + j, 8, stride=16), :] = e
        e_seed[pl.ds(8 - j, 8, stride=16), :] = jnp.where(hi, -e, e)
    _, c8 = sincos_turns(8.0 * turns)
    coef[0:8, :] = 2.0 * c8
    sa, ca = sincos_turns(0.5 * sine)
    first = (grp * (ANT // 2)).astype(jnp.float32)
    s0, c0 = sincos_turns(first * sine)
    _, a8 = sincos_turns(4.0 * sine)
    coef[8:16, :] = 2.0 * a8
    g1 = jnp.where(hi, -imag, real)
    g2 = jnp.where(hi, real, imag)
    x = g1 * c0 + g2 * s0
    y = g2 * c0 - g1 * s0
    for a in range(16):
        s_seed[pl.ds(a, 8, stride=32), :] = x
        s_seed[pl.ds(16 + a, 8, stride=32), :] = y
        if a < 15:
            x, y = x * ca + y * sa, y * ca - x * sa


def response_of(l, e_seed, s_seed, coef):
    c = jnp.broadcast_to(coef[l : l + 1, :], (8, 128))
    low = e_seed[16 * l : 16 * l + 8, :]
    top = e_seed[16 * l + 8 : 16 * l + 16, :]
    down = [top, low]
    up = [low, top]
    for _ in range(7):
        down.append(c * down[-1] - down[-2])
        up.append(c * up[-1] - up[-2])
    table = jnp.concatenate(down[:0:-1] + up[1:], axis=0).astype(jnp.bfloat16)
    c = jnp.broadcast_to(coef[8 + l : 9 + l, :], (8, 128))
    parts = []
    for h in range(2):
        at = 32 * l + 16 * h
        run = [s_seed[at : at + 8, :], s_seed[at + 8 : at + 16, :]]
        for _ in range(2):
            run.append(c * run[-1] - run[-2])
        parts += run
    spread = jnp.concatenate(parts, axis=0).astype(jnp.bfloat16)
    return lax.dot_general(
        spread, table, (((1,), (1,)), ((), ())), preferred_element_type=jnp.float32
    )


SEED_SCRATCH = [
    pltpu.VMEM((8 * 16, 128), jnp.float32),
    pltpu.VMEM((8 * 32, 128), jnp.float32),
    pltpu.VMEM((16, 128), jnp.float32),
]


def unpacked(code, load):
    base = code & 255
    cnt = (code >> 8) & 255
    lane = lanes((8, 128))
    message, overflow = load(code >> 16)
    value = jnp.where(lane < base + cnt - 128, overflow, message)
    return jnp.where(lane < cnt, pltpu.roll(value, (0 - base) & 127, 1), 0.0)


def transmit_kernel(
    slots, nearby, got, symbols, over, table, raw, table_s, serving,
    e_seed, s_seed, coef, e_seed2, s_seed2, coef2, sem
):
    me = lax.axis_index("cell")
    grp = lax.axis_index("grp")
    lane = lanes((8, 128))
    row = rows_of((8, 128))
    is_tag = (lane >= TAG_LANE) & (lane < TAG_LANE + 12)
    link = lane + 1
    found = [jnp.zeros((8, 128), jnp.int32) for _ in range(LINKS // 128)]
    for c in range(CELLS // 8):
        extra = got[pl.ds(64 * c + 4, 8, stride=8), :]
        number = jnp.where(is_tag, extra, 0.0).astype(jnp.int32)
        number = number + (pltpu.roll(number, 126, 1) << 9) + (pltpu.roll(number, 127, 1) << 17)
        for k in range(4):
            at = TAG_LANE + 3 * k
            value = jnp.broadcast_to(number[:, at : at + 1], (8, 128))
            code = (value >> 9) + ((8 * c + row) << 16)
            for h in range(LINKS // 128):
                found[h] = found[h] + jnp.where((value & 511) == link + 128 * h, code, 0)
    for h in range(LINKS // 128):
        table[h : h + 1, :] = jnp.sum(found[h], axis=0, keepdims=True)
    copy = pltpu.make_async_copy(table, table_s, sem)
    copy.start()

    def clear(i, carry):
        raw[i] = jnp.zeros((RESP, 128), jnp.float32)
        return carry

    lax.fori_loop(0, CELL_SECTORS, clear, 0, unroll=4)
    for c in range(CELLS // 8):
        extra = got[pl.ds(64 * c + 4, 8, stride=8), :]
        for f in range(4):
            over[pl.ds(64 * c + f, 8, stride=8), :] = extra if f == 0 else pltpu.roll(extra, 128 - 2 * f, 1)
    copy.wait()

    def load(source):
        at = pl.ds(pl.multiple_of(8 * source, 8), 8)
        return got[at, :], over[at, :]

    def serve(u, carry):
        g = u * NEARBY_COUNT + slots[u]
        code = table_s[g >> 7, g & 127]
        serving[pl.ds(pl.multiple_of(8 * u, 8), 8), :] = unpacked(code, load)
        return carry

    lax.fori_loop(0, USERS, serve, 0, unroll=8)

    seeds = (e_seed, s_seed, coef), (e_seed2, s_seed2, coef2)

    def prepare(c):
        fields = [serving[pl.ds(64 * c + f, 8, stride=8), :] for f in range(4)]
        seeds_of(fields, grp, *seeds[c % 2])

    prepare(0)
    for c in range(USERS // 8):
        if c + 1 < USERS // 8:
            prepare(c + 1)
        for l in range(8):
            u = 8 * c + l
            resp = response_of(l, *seeds[c % 2]).astype(jnp.bfloat16).astype(jnp.float32)
            sym = symbols[u].astype(jnp.float32)
            sym_r, sym_i = sym[0:1, :], sym[1:2, :]
            real, imag = resp[:ANT, :], resp[ANT:, :]
            part = jnp.concatenate(
                [real * sym_r + imag * sym_i, real * sym_i - imag * sym_r], axis=0
            )
            sector = nearby[slots[u], u] - me * CELL_SECTORS
            raw[sector] = raw[sector] + part


PIECE = 8
PIECES = (0, 16, 8, 24)


def receive_kernel(
    nearby, table, got, over, raw, out, near, resp, part, other,
    e_seed, s_seed, coef, e_seed2, s_seed2, coef2, rows, rows2, send_sems, recv_sems
):
    me = lax.axis_index("cell")
    grp = lax.axis_index("grp")
    right = lax.rem(me + 1, CELLS)
    left = lax.rem(me + CELLS - 1, CELLS)
    barrier = pltpu.get_barrier_semaphore()
    for target in ({"cell": left}, {"cell": right}, {"grp": 1 - grp}):
        pl.semaphore_signal(barrier, inc=1, device_id=target, device_id_type=MESH)

    halo = []
    for n, begin in enumerate(PIECES):

        def normalise(s, carry):
            real, imag = raw[s, :ANT, :], raw[s, ANT:, :]
            power = jnp.mean(real * real + imag * imag, axis=1, keepdims=True)
            scale = 1.0 / jnp.sqrt(power + EPSILON)
            near[REACH + s] = jnp.concatenate([real * scale, imag * scale], axis=0).astype(jnp.bfloat16)
            return carry

        lax.fori_loop(begin, begin + PIECE, normalise, 0, unroll=8)
        if n == 0:
            pl.semaphore_wait(barrier, 3)
        to_left = begin < CELL_SECTORS - REACH
        land = begin + REACH + CELL_SECTORS if to_left else begin + REACH - CELL_SECTORS
        halo.append(
            pltpu.make_async_remote_copy(
                src_ref=near.at[pl.ds(REACH + begin, PIECE)],
                dst_ref=near.at[pl.ds(land, PIECE)],
                send_sem=send_sems.at[n],
                recv_sem=recv_sems.at[n],
                device_id={"cell": left if to_left else right},
                device_id_type=MESH,
            )
        )
        halo[-1].start()

    first, second = (e_seed, s_seed, coef), (e_seed2, s_seed2, coef2)

    def unpack(u, rows):
        u = jnp.minimum(u, USERS - 1)
        for l in range(8):
            code = table[u // 16, lax.rem(u, 16) * 8 + l]
            rows[8 * l : 8 * l + 8, :] = unpacked(code, lambda i: (got[i], over[i]))

    def prepare(rows, seeds):
        seeds_of([rows[pl.ds(f, 8, stride=8), :] for f in range(4)], grp, *seeds)

    def respond(u, seeds):
        for l in range(8):
            at = pl.ds(pl.multiple_of(u * (8 * RESP) + RESP * l, RESP), RESP)
            resp[at, :] = response_of(l, *seeds).astype(jnp.bfloat16)

    def two_users(v, carry):
        prepare(rows2, second)
        unpack(2 * v + 3, rows2)
        respond(2 * v, first)
        prepare(rows, first)
        unpack(2 * v + 4, rows)
        respond(2 * v + 1, second)
        return carry

    unpack(0, rows)
    prepare(rows, first)
    unpack(1, rows2)
    unpack(2, rows)
    lax.fori_loop(0, USERS // 2, two_users, 0)
    for copy in halo:
        copy.wait()

    def combine(u, carry):
        real = jnp.zeros((ANT, 128), jnp.float32)
        imag = jnp.zeros((ANT, 128), jnp.float32)
        for k in range(NEARBY_COUNT):
            sector = nearby[k, u] - me * CELL_SECTORS + REACH
            sector = jnp.clip(sector, 0, CELL_SECTORS + 2 * REACH - 1)
            tx = near[sector].astype(jnp.float32)
            at = pl.ds(pl.multiple_of(u * (8 * RESP) + RESP * k, RESP), RESP)
            ch = resp[at, :].astype(jnp.float32)
            real = real + (ch[:ANT] * tx[:ANT] - ch[ANT:] * tx[ANT:])
            imag = imag + (ch[:ANT] * tx[ANT:] + ch[ANT:] * tx[:ANT])
        part[u] = jnp.concatenate(
            [jnp.sum(real, axis=0, keepdims=True), jnp.sum(imag, axis=0, keepdims=True)], axis=0
        )
        return carry

    lax.fori_loop(0, USERS, combine, 0, unroll=4)
    swap = pltpu.make_async_remote_copy(
        src_ref=part,
        dst_ref=other,
        send_sem=send_sems.at[len(PIECES)],
        recv_sem=recv_sems.at[len(PIECES)],
        device_id={"grp": 1 - grp},
        device_id_type=MESH,
    )
    swap.start()
    swap.wait()
    out[...] = (part[...] + other[...]) * (1.0 / math.sqrt(SECTOR_ANTENNAS))


VMEM = pl.BlockSpec(memory_space=pltpu.VMEM)
SMEM = pl.BlockSpec(memory_space=pltpu.SMEM)
ANY = pl.BlockSpec(memory_space=pl.ANY)


def call(kernel, name, mib, out_shape, in_specs, scratch, remote=None):
    extra = {} if remote is None else {"collective_id": remote, "has_side_effects": True}
    many = isinstance(out_shape, (tuple, list))
    return pl.pallas_call(
        kernel,
        name=name,
        out_shape=out_shape,
        in_specs=in_specs,
        out_specs=[VMEM] * len(out_shape) if many else VMEM,
        scratch_shapes=scratch,
        compiler_params=pltpu.CompilerParams(vmem_limit_bytes=mib * MIB, **extra),
    )


def shards(
    path_delay,
    path_angle,
    path_gain,
    slot_counts,
    slot_offsets,
    ray_link,
    nearby_sectors,
    serving_slot,
    symbols,
):
    f32, bf16, i32 = jnp.float32, jnp.bfloat16, jnp.int32
    got = call(
        deliver_kernel,
        "deliver",
        16,
        jax.ShapeDtypeStruct((CELLS, 8, 128), f32),
        [ANY, ANY, ANY, ANY, VMEM],
        [
            pltpu.SMEM((SLOTS,), i32),
            pltpu.SMEM((SLOTS,), i32),
            pltpu.SMEM((SLOTS,), i32),
            pltpu.VMEM((PATH_ROWS + 1, 8, 128), f32),
            pltpu.VMEM((HALF, 8, 128), f32),
            pltpu.SMEM((HALF + 1,), i32),
            pltpu.SemaphoreType.DMA((3,)),
            pltpu.SemaphoreType.DMA((4,)),
        ],
        remote=0,
    )(
        slot_counts,
        slot_offsets,
        ray_link,
        serving_slot,
        jnp.stack((path_delay, path_angle, path_gain[0], path_gain[1])).reshape(4, PATH_ROWS, 128),
    )
    over, table, raw = call(
        transmit_kernel,
        "transmit",
        24,
        (
            jax.ShapeDtypeStruct((CELLS * 8, 128), f32),
            jax.ShapeDtypeStruct((LINKS // 128, 128), i32),
            jax.ShapeDtypeStruct((CELL_SECTORS, RESP, 128), f32),
        ),
        [SMEM, SMEM, VMEM, VMEM],
        [
            pltpu.SMEM((LINKS // 128, 128), i32),
            pltpu.VMEM((USERS * 8, 128), f32),
            *SEED_SCRATCH,
            *SEED_SCRATCH,
            pltpu.SemaphoreType.DMA,
        ],
    )(serving_slot, nearby_sectors, got.reshape(CELLS * 8, 128), symbols)
    return call(
        receive_kernel,
        "receive",
        24,
        jax.ShapeDtypeStruct((USERS, 2, FRAME_TONES), f32),
        [SMEM, SMEM, VMEM, VMEM, VMEM],
        [
            pltpu.VMEM((CELL_SECTORS + 2 * REACH, RESP, 128), bf16),
            pltpu.VMEM((LINKS * RESP, 128), bf16),
            pltpu.VMEM((USERS, 2, FRAME_TONES), f32),
            pltpu.VMEM((USERS, 2, FRAME_TONES), f32),
            *SEED_SCRATCH,
            *SEED_SCRATCH,
            pltpu.VMEM((64, 128), f32),
            pltpu.VMEM((64, 128), f32),
            pltpu.SemaphoreType.DMA((len(PIECES) + 1,)),
            pltpu.SemaphoreType.DMA((len(PIECES) + 1,)),
        ],
        remote=1,
    )(nearby_sectors, table, got, over.reshape(CELLS, 8, 128), raw)


def solution(mesh):
    placed = (
        P("cell"),
        P("cell"),
        P(None, "cell"),
        P("cell"),
        P("cell"),
        P("cell"),
        P(None, "cell"),
        P("cell"),
        P("cell", None, None),
    )
    return jax.shard_map(
        shards, mesh=mesh, in_specs=placed, out_specs=P("cell", None, None), check_vma=False
    )
```

```python
import functools
import math

import jax
import jax.numpy as jnp
from jax import lax
from jax.experimental import pallas as pl
from jax.experimental.pallas import tpu as pltpu
from jax.sharding import PartitionSpec as P

SECTOR_ANTENNAS = 64
FRAME_TONES = 128
NEARBY_COUNT = 8
CELL_SECTORS = 32
REACH = 16
EPSILON = 1e-06

CELLS = 128
SLOTS = 256
USERS = 32
LINKS = USERS * NEARBY_COUNT
PATH_ROWS = 65
ANT = SECTOR_ANTENNAS // 2
RESP = 2 * ANT
TAG_LANE = 8
HALF = CELLS // 2
WIRE_ROWS = 5
MIB = 1024 * 1024
MESH = pl.DeviceIdType.MESH


def lanes(shape):
    return lax.broadcasted_iota(jnp.int32, shape, len(shape) - 1)


def rows_of(shape):
    return lax.broadcasted_iota(jnp.int32, shape, len(shape) - 2)


def sincos_turns(turns):
    r = turns - jnp.round(turns)
    r2 = r * r
    sin_c = [(-1) ** n * math.pi ** (2 * n + 1) / math.factorial(2 * n + 1) for n in range(7)]
    cos_c = [(-1) ** n * math.pi ** (2 * n) / math.factorial(2 * n) for n in range(7)]
    sh = jnp.full_like(r, sin_c[-1])
    ch = jnp.full_like(r, cos_c[-1])
    for n in range(5, -1, -1):
        sh = sh * r2 + sin_c[n]
        ch = ch * r2 + cos_c[n]
    sh = sh * r
    return 2.0 * sh * ch, 1.0 - 2.0 * sh * sh


def my_half():
    return lax.rem(lax.axis_index("grp") + lax.axis_index("cell") // HALF, 2)


def deliver_kernel(
    counts_in, offsets_in, links_in, _slots, fields, got,
    counts, offsets, links, store, sent, begins, load_sems, sems
):
    me = lax.axis_index("cell")
    grp = lax.axis_index("grp")
    start = my_half() * HALF
    sibling = {"grp": 1 - grp}
    loads = [
        pltpu.make_async_copy(src, dst, load_sems.at[n])
        for n, (src, dst) in enumerate(((counts_in, counts), (offsets_in, offsets), (links_in, links)))
    ]
    for copy in loads:
        copy.start()
    barrier = pltpu.get_barrier_semaphore()
    pl.semaphore_signal(barrier, inc=1, device_id=sibling, device_id_type=MESH)

    def greet(d, carry):
        other = start + lax.rem(me + d, HALF)
        pl.semaphore_signal(barrier, inc=1, device_id={"cell": other}, device_id_type=MESH)
        return carry

    @pl.when(grp == 1)
    def _():
        greet(0, 0)

    lax.fori_loop(1, HALF, greet, 0, unroll=9)

    for copy in loads:
        copy.wait()

    def narrow(_, carry):
        low, top = carry
        mid = (low + top) >> 1
        below = (links[jnp.minimum(mid, SLOTS - 1)] >> 8) < start
        below = below & (low < top)
        return jnp.where(below, mid + 1, low), jnp.where(below, top, mid)

    at, _ = lax.fori_loop(0, 9, narrow, (jnp.int32(0), jnp.int32(SLOTS)))

    def count(o, at):
        begins[o] = at
        total = at
        for k in range(4):
            slot = at + k
            mine = (links[jnp.minimum(slot, SLOTS - 1)] >> 8) == start + o
            total = total + jnp.where(mine & (slot < SLOTS), 1, 0)
        return total

    begins[HALF] = lax.fori_loop(0, HALF, count, at, unroll=4)

    for c in range(0, PATH_ROWS, 8):
        n = min(8, PATH_ROWS - c)
        for f in range(4):
            value = fields[f, c : c + n, :]
            if f < 2:
                value = value * (1.0 / FRAME_TONES) if f == 0 else jnp.sin(value)
            store[c : c + n, f, :] = value
            store[c : c + n, 4 + f, :] = value
    store[PATH_ROWS] = jnp.zeros((8, 128), jnp.float32)

    lane = lanes((8, 128))
    row = rows_of((8, 128))
    place = lane + jnp.where(row >= 4, 128, 0)
    tag_place = jnp.where(row == 4, lane - TAG_LANE, -1000)

    def pack(o, carry):
        first = begins[o]
        number = begins[o + 1] - first
        base = jnp.int32(0)
        message = jnp.zeros((8, 128), jnp.float32)
        for k in range(4):
            r = jnp.minimum(first + k, SLOTS - 1)
            cnt = jnp.where(k < number, counts[r], 0)
            tag = jnp.where(k < number, (links[r] & 255) + 1, 0)
            off = offsets[r]
            q = off >> 7
            s = off & 127
            value = jnp.where(lane < s + cnt - 128, store[q + 1], store[q])
            value = pltpu.roll(value, (base - s) & 127, 1)
            j = place - base
            message = jnp.where((j >= 0) & (j < cnt), value, message)
            for n, number_sent in enumerate((tag, cnt, base)):
                message = jnp.where(tag_place == 3 * k + n, number_sent.astype(jnp.float32), message)
            base = base + cnt
        sent[o] = message
        return carry

    lax.fori_loop(0, HALF, pack, 0, unroll=4)
    for c in range(0, HALF, 8):
        total = sent[c : c + 8, 4, :]
        for f in range(1, 4):
            total = total + pltpu.roll(sent[c : c + 8, 4 + f, :], 2 * f, 1)
        sent[c : c + 8, 4, :] = total

    @pl.when(grp == 0)
    def _():
        got[me] = sent[lax.rem(me, HALF)]

    pl.semaphore_wait(barrier, HALF + grp)
    wire = pl.ds(0, WIRE_ROWS)

    def send(hops, q, carry):
        near = lax.rem(me + 8 * q + hops, HALF)
        pltpu.make_async_remote_copy(
            src_ref=sent.at[near, wire],
            dst_ref=got.at[me, wire],
            send_sem=sems.at[0],
            recv_sem=sems.at[1],
            device_id={"cell": start + near},
            device_id_type=MESH,
        ).start()
        return carry

    for hops in (4, 3, 5, 2, 6, 1, 7):
        lax.fori_loop(0, HALF // 8, functools.partial(send, hops), 0, unroll=4)
    lax.fori_loop(1 - grp, HALF // 8, functools.partial(send, 0), 0)

    for g in range(2):

        @pl.when(grp == g)
        def _():
            whole = pltpu.make_async_remote_copy(
                src_ref=sent.at[pl.ds(0, HALF - 1 + g), wire],
                dst_ref=got.at[pl.ds(start, HALF - 1 + g), wire],
                send_sem=sems.at[0],
                recv_sem=sems.at[1],
                device_id=sibling,
                device_id_type=MESH,
            )
            whole.wait_recv()
            whole.wait_send()

    swap = pltpu.make_async_remote_copy(
        src_ref=got.at[pl.ds(start, HALF), wire],
        dst_ref=got.at[pl.ds(start, HALF), wire],
        send_sem=sems.at[2],
        recv_sem=sems.at[3],
        device_id=sibling,
        device_id_type=MESH,
    )
    swap.start()
    swap.wait()


def seeds_of(fields, grp, e_seed, s_seed, coef):
    turns, sine, real, imag = [v + pltpu.roll(v, 64, 1) for v in fields]
    hi = lanes((8, 128)) >= 64
    s1, c1 = sincos_turns(turns)
    e = jnp.where(hi, 0.0, 1.0)
    f = jnp.where(hi, 1.0, 0.0)
    e_seed[pl.ds(8, 8, stride=16), :] = e
    for j in range(1, 9):
        e, f = e * c1 - f * s1, f * c1 + e * s1
        if j < 8:
            e_seed[pl.ds(8 + j, 8, stride=16), :] = e
        e_seed[pl.ds(8 - j, 8, stride=16), :] = jnp.where(hi, -e, e)
    _, c8 = sincos_turns(8.0 * turns)
    coef[0:8, :] = 2.0 * c8
    sa, ca = sincos_turns(0.5 * sine)
    first = (grp * (ANT // 2)).astype(jnp.float32)
    s0, c0 = sincos_turns(first * sine)
    _, a8 = sincos_turns(4.0 * sine)
    coef[8:16, :] = 2.0 * a8
    g1 = jnp.where(hi, -imag, real)
    g2 = jnp.where(hi, real, imag)
    x = g1 * c0 + g2 * s0
    y = g2 * c0 - g1 * s0
    for a in range(16):
        s_seed[pl.ds(a, 8, stride=32), :] = x
        s_seed[pl.ds(16 + a, 8, stride=32), :] = y
        if a < 15:
            x, y = x * ca + y * sa, y * ca - x * sa


def response_of(l, e_seed, s_seed, coef):
    c = jnp.broadcast_to(coef[l : l + 1, :], (8, 128))
    low = e_seed[16 * l : 16 * l + 8, :]
    top = e_seed[16 * l + 8 : 16 * l + 16, :]
    down = [top, low]
    up = [low, top]
    for _ in range(7):
        down.append(c * down[-1] - down[-2])
        up.append(c * up[-1] - up[-2])
    table = jnp.concatenate(down[:0:-1] + up[1:], axis=0).astype(jnp.bfloat16)
    c = jnp.broadcast_to(coef[8 + l : 9 + l, :], (8, 128))
    parts = []
    for h in range(2):
        at = 32 * l + 16 * h
        run = [s_seed[at : at + 8, :], s_seed[at + 8 : at + 16, :]]
        for _ in range(2):
            run.append(c * run[-1] - run[-2])
        parts += run
    spread = jnp.concatenate(parts, axis=0).astype(jnp.bfloat16)
    return lax.dot_general(
        spread, table, (((1,), (1,)), ((), ())), preferred_element_type=jnp.float32
    )


SEED_SCRATCH = [
    pltpu.VMEM((8 * 16, 128), jnp.float32),
    pltpu.VMEM((8 * 32, 128), jnp.float32),
    pltpu.VMEM((16, 128), jnp.float32),
]


def unpacked(code, load):
    base = code & 255
    cnt = (code >> 8) & 255
    lane = lanes((8, 128))
    message, overflow = load(code >> 16)
    value = jnp.where(lane < base + cnt - 128, overflow, message)
    return jnp.where(lane < cnt, pltpu.roll(value, (0 - base) & 127, 1), 0.0)


def transmit_kernel(
    slots, nearby, got, symbols, over, table, raw, table_s, serving,
    e_seed, s_seed, coef, e_seed2, s_seed2, coef2, sem
):
    me = lax.axis_index("cell")
    grp = lax.axis_index("grp")
    lane = lanes((8, 128))
    row = rows_of((8, 128))
    is_tag = (lane >= TAG_LANE) & (lane < TAG_LANE + 12)
    link = lane + 1
    found = [jnp.zeros((8, 128), jnp.int32) for _ in range(LINKS // 128)]
    for c in range(CELLS // 8):
        extra = got[pl.ds(64 * c + 4, 8, stride=8), :]
        number = jnp.where(is_tag, extra, 0.0).astype(jnp.int32)
        number = number + (pltpu.roll(number, 126, 1) << 9) + (pltpu.roll(number, 127, 1) << 17)
        for k in range(4):
            at = TAG_LANE + 3 * k
            value = jnp.broadcast_to(number[:, at : at + 1], (8, 128))
            code = (value >> 9) + ((8 * c + row) << 16)
            for h in range(LINKS // 128):
                found[h] = found[h] + jnp.where((value & 511) == link + 128 * h, code, 0)
    for h in range(LINKS // 128):
        table[h : h + 1, :] = jnp.sum(found[h], axis=0, keepdims=True)
    copy = pltpu.make_async_copy(table, table_s, sem)
    copy.start()

    def clear(i, carry):
        raw[i] = jnp.zeros((RESP, 128), jnp.float32)
        return carry

    lax.fori_loop(0, CELL_SECTORS, clear, 0, unroll=4)
    for c in range(CELLS // 8):
        extra = got[pl.ds(64 * c + 4, 8, stride=8), :]
        for f in range(4):
            over[pl.ds(64 * c + f, 8, stride=8), :] = extra if f == 0 else pltpu.roll(extra, 128 - 2 * f, 1)
    copy.wait()

    def load(source):
        at = pl.ds(pl.multiple_of(8 * source, 8), 8)
        return got[at, :], over[at, :]

    def serve(u, carry):
        g = u * NEARBY_COUNT + slots[u]
        code = table_s[g >> 7, g & 127]
        serving[pl.ds(pl.multiple_of(8 * u, 8), 8), :] = unpacked(code, load)
        return carry

    lax.fori_loop(0, USERS, serve, 0, unroll=8)

    seeds = (e_seed, s_seed, coef), (e_seed2, s_seed2, coef2)

    def prepare(c):
        fields = [serving[pl.ds(64 * c + f, 8, stride=8), :] for f in range(4)]
        seeds_of(fields, grp, *seeds[c % 2])

    prepare(0)
    for c in range(USERS // 8):
        if c + 1 < USERS // 8:
            prepare(c + 1)
        for l in range(8):
            u = 8 * c + l
            resp = response_of(l, *seeds[c % 2]).astype(jnp.bfloat16).astype(jnp.float32)
            sym = symbols[u].astype(jnp.float32)
            sym_r, sym_i = sym[0:1, :], sym[1:2, :]
            real, imag = resp[:ANT, :], resp[ANT:, :]
            part = jnp.concatenate(
                [real * sym_r + imag * sym_i, real * sym_i - imag * sym_r], axis=0
            )
            sector = nearby[slots[u], u] - me * CELL_SECTORS
            raw[sector] = raw[sector] + part


PIECE = REACH
PIECES = (0, 16)


def receive_kernel(
    nearby, table, got, over, raw, out, near, resp, part, other,
    e_seed, s_seed, coef, e_seed2, s_seed2, coef2, rows, rows2, send_sems, recv_sems
):
    me = lax.axis_index("cell")
    grp = lax.axis_index("grp")
    right = lax.rem(me + 1, CELLS)
    left = lax.rem(me + CELLS - 1, CELLS)
    barrier = pltpu.get_barrier_semaphore()
    for target in ({"cell": left}, {"cell": right}, {"grp": 1 - grp}):
        pl.semaphore_signal(barrier, inc=1, device_id=target, device_id_type=MESH)

    halo = []
    for n, begin in enumerate(PIECES):

        def normalise(s, carry):
            real, imag = raw[s, :ANT, :], raw[s, ANT:, :]
            power = jnp.mean(real * real + imag * imag, axis=1, keepdims=True)
            scale = 1.0 / jnp.sqrt(power + EPSILON)
            near[REACH + s] = jnp.concatenate([real * scale, imag * scale], axis=0).astype(jnp.bfloat16)
            return carry

        lax.fori_loop(begin, begin + PIECE, normalise, 0, unroll=8)
        if n == 0:
            pl.semaphore_wait(barrier, 3)
        to_left = begin < CELL_SECTORS - REACH
        land = begin + REACH + CELL_SECTORS if to_left else begin + REACH - CELL_SECTORS
        halo.append(
            pltpu.make_async_remote_copy(
                src_ref=near.at[pl.ds(REACH + begin, PIECE)],
                dst_ref=near.at[pl.ds(land, PIECE)],
                send_sem=send_sems.at[n],
                recv_sem=recv_sems.at[n],
                device_id={"cell": left if to_left else right},
                device_id_type=MESH,
            )
        )
        halo[-1].start()

    first, second = (e_seed, s_seed, coef), (e_seed2, s_seed2, coef2)

    def unpack(u, rows):
        u = jnp.minimum(u, USERS - 1)
        for l in range(8):
            code = table[u // 16, lax.rem(u, 16) * 8 + l]
            rows[8 * l : 8 * l + 8, :] = unpacked(code, lambda i: (got[i], over[i]))

    def prepare(rows, seeds):
        seeds_of([rows[pl.ds(f, 8, stride=8), :] for f in range(4)], grp, *seeds)

    def respond(u, seeds):
        for l in range(8):
            at = pl.ds(pl.multiple_of(u * (8 * RESP) + RESP * l, RESP), RESP)
            resp[at, :] = response_of(l, *seeds).astype(jnp.bfloat16)

    def two_users(v, carry):
        prepare(rows2, second)
        unpack(2 * v + 3, rows2)
        respond(2 * v, first)
        prepare(rows, first)
        unpack(2 * v + 4, rows)
        respond(2 * v + 1, second)
        return carry

    unpack(0, rows)
    prepare(rows, first)
    unpack(1, rows2)
    unpack(2, rows)
    lax.fori_loop(0, USERS // 2, two_users, 0)
    for copy in halo:
        copy.wait()

    def combine(u, carry):
        real = jnp.zeros((ANT, 128), jnp.float32)
        imag = jnp.zeros((ANT, 128), jnp.float32)
        for k in range(NEARBY_COUNT):
            sector = nearby[k, u] - me * CELL_SECTORS + REACH
            sector = jnp.clip(sector, 0, CELL_SECTORS + 2 * REACH - 1)
            tx = near[sector].astype(jnp.float32)
            at = pl.ds(pl.multiple_of(u * (8 * RESP) + RESP * k, RESP), RESP)
            ch = resp[at, :].astype(jnp.float32)
            real = real + (ch[:ANT] * tx[:ANT] - ch[ANT:] * tx[ANT:])
            imag = imag + (ch[:ANT] * tx[ANT:] + ch[ANT:] * tx[:ANT])
        part[u] = jnp.concatenate(
            [jnp.sum(real, axis=0, keepdims=True), jnp.sum(imag, axis=0, keepdims=True)], axis=0
        )
        return carry

    lax.fori_loop(0, USERS, combine, 0, unroll=4)
    swap = pltpu.make_async_remote_copy(
        src_ref=part,
        dst_ref=other,
        send_sem=send_sems.at[len(PIECES)],
        recv_sem=recv_sems.at[len(PIECES)],
        device_id={"grp": 1 - grp},
        device_id_type=MESH,
    )
    swap.start()
    swap.wait()
    out[...] = (part[...] + other[...]) * (1.0 / math.sqrt(SECTOR_ANTENNAS))


VMEM = pl.BlockSpec(memory_space=pltpu.VMEM)
SMEM = pl.BlockSpec(memory_space=pltpu.SMEM)
ANY = pl.BlockSpec(memory_space=pl.ANY)


def call(kernel, name, mib, out_shape, in_specs, scratch, remote=None):
    extra = {} if remote is None else {"collective_id": remote, "has_side_effects": True}
    many = isinstance(out_shape, (tuple, list))
    return pl.pallas_call(
        kernel,
        name=name,
        out_shape=out_shape,
        in_specs=in_specs,
        out_specs=[VMEM] * len(out_shape) if many else VMEM,
        scratch_shapes=scratch,
        compiler_params=pltpu.CompilerParams(vmem_limit_bytes=mib * MIB, **extra),
    )


def shards(
    path_delay,
    path_angle,
    path_gain,
    slot_counts,
    slot_offsets,
    ray_link,
    nearby_sectors,
    serving_slot,
    symbols,
):
    f32, bf16, i32 = jnp.float32, jnp.bfloat16, jnp.int32
    got = call(
        deliver_kernel,
        "deliver",
        16,
        jax.ShapeDtypeStruct((CELLS, 8, 128), f32),
        [ANY, ANY, ANY, ANY, VMEM],
        [
            pltpu.SMEM((SLOTS,), i32),
            pltpu.SMEM((SLOTS,), i32),
            pltpu.SMEM((SLOTS,), i32),
            pltpu.VMEM((PATH_ROWS + 1, 8, 128), f32),
            pltpu.VMEM((HALF, 8, 128), f32),
            pltpu.SMEM((HALF + 1,), i32),
            pltpu.SemaphoreType.DMA((3,)),
            pltpu.SemaphoreType.DMA((4,)),
        ],
        remote=0,
    )(
        slot_counts,
        slot_offsets,
        ray_link,
        serving_slot,
        jnp.stack((path_delay, path_angle, path_gain[0], path_gain[1])).reshape(4, PATH_ROWS, 128),
    )
    over, table, raw = call(
        transmit_kernel,
        "transmit",
        24,
        (
            jax.ShapeDtypeStruct((CELLS * 8, 128), f32),
            jax.ShapeDtypeStruct((LINKS // 128, 128), i32),
            jax.ShapeDtypeStruct((CELL_SECTORS, RESP, 128), f32),
        ),
        [SMEM, SMEM, VMEM, VMEM],
        [
            pltpu.SMEM((LINKS // 128, 128), i32),
            pltpu.VMEM((USERS * 8, 128), f32),
            *SEED_SCRATCH,
            *SEED_SCRATCH,
            pltpu.SemaphoreType.DMA,
        ],
    )(serving_slot, nearby_sectors, got.reshape(CELLS * 8, 128), symbols)
    return call(
        receive_kernel,
        "receive",
        24,
        jax.ShapeDtypeStruct((USERS, 2, FRAME_TONES), f32),
        [SMEM, SMEM, VMEM, VMEM, VMEM],
        [
            pltpu.VMEM((CELL_SECTORS + 2 * REACH, RESP, 128), bf16),
            pltpu.VMEM((LINKS * RESP, 128), bf16),
            pltpu.VMEM((USERS, 2, FRAME_TONES), f32),
            pltpu.VMEM((USERS, 2, FRAME_TONES), f32),
            *SEED_SCRATCH,
            *SEED_SCRATCH,
            pltpu.VMEM((64, 128), f32),
            pltpu.VMEM((64, 128), f32),
            pltpu.SemaphoreType.DMA((len(PIECES) + 1,)),
            pltpu.SemaphoreType.DMA((len(PIECES) + 1,)),
        ],
        remote=1,
    )(nearby_sectors, table, got, over.reshape(CELLS, 8, 128), raw)


def solution(mesh):
    placed = (
        P("cell"),
        P("cell"),
        P(None, "cell"),
        P("cell"),
        P("cell"),
        P("cell"),
        P(None, "cell"),
        P("cell"),
        P("cell", None, None),
    )
    return jax.shard_map(
        shards, mesh=mesh, in_specs=placed, out_specs=P("cell", None, None), check_vma=False
    )
```

```python
import functools
import math

import jax
import jax.numpy as jnp
from jax import lax
from jax.experimental import pallas as pl
from jax.experimental.pallas import tpu as pltpu
from jax.sharding import PartitionSpec as P

SECTOR_ANTENNAS = 64
FRAME_TONES = 128
NEARBY_COUNT = 8
CELL_SECTORS = 32
REACH = 16
EPSILON = 1e-06

CELLS = 128
SLOTS = 256
USERS = 32
LINKS = USERS * NEARBY_COUNT
PATH_ROWS = 65
ANT = SECTOR_ANTENNAS // 2
RESP = 2 * ANT
TAG_LANE = 8
HALF = CELLS // 2
WIRE_ROWS = 5
MIB = 1024 * 1024
MESH = pl.DeviceIdType.MESH


def lanes(shape):
    return lax.broadcasted_iota(jnp.int32, shape, len(shape) - 1)


def rows_of(shape):
    return lax.broadcasted_iota(jnp.int32, shape, len(shape) - 2)


def sincos_turns(turns):
    r = turns - jnp.round(turns)
    r2 = r * r
    sin_c = [(-1) ** n * math.pi ** (2 * n + 1) / math.factorial(2 * n + 1) for n in range(7)]
    cos_c = [(-1) ** n * math.pi ** (2 * n) / math.factorial(2 * n) for n in range(7)]
    sh = jnp.full_like(r, sin_c[-1])
    ch = jnp.full_like(r, cos_c[-1])
    for n in range(5, -1, -1):
        sh = sh * r2 + sin_c[n]
        ch = ch * r2 + cos_c[n]
    sh = sh * r
    return 2.0 * sh * ch, 1.0 - 2.0 * sh * sh


def my_half():
    return lax.rem(lax.axis_index("grp") + lax.axis_index("cell") // HALF, 2)


def deliver_kernel(
    counts_in, offsets_in, links_in, _slots, fields, got,
    counts, offsets, links, store, sent, begins, load_sems, sems
):
    me = lax.axis_index("cell")
    grp = lax.axis_index("grp")
    start = my_half() * HALF
    sibling = {"grp": 1 - grp}
    loads = [
        pltpu.make_async_copy(src, dst, load_sems.at[n])
        for n, (src, dst) in enumerate(((counts_in, counts), (offsets_in, offsets), (links_in, links)))
    ]
    for copy in loads:
        copy.start()
    barrier = pltpu.get_barrier_semaphore()
    pl.semaphore_signal(barrier, inc=1, device_id=sibling, device_id_type=MESH)

    def greet(d, carry):
        other = start + lax.rem(me + d, HALF)
        pl.semaphore_signal(barrier, inc=1, device_id={"cell": other}, device_id_type=MESH)
        return carry

    @pl.when(grp == 1)
    def _():
        greet(0, 0)

    lax.fori_loop(1, HALF, greet, 0, unroll=9)

    for copy in loads:
        copy.wait()

    def narrow(_, carry):
        low, top = carry
        mid = (low + top) >> 1
        below = (links[jnp.minimum(mid, SLOTS - 1)] >> 8) < start
        below = below & (low < top)
        return jnp.where(below, mid + 1, low), jnp.where(below, top, mid)

    at, _ = lax.fori_loop(0, 9, narrow, (jnp.int32(0), jnp.int32(SLOTS)))

    def count(o, at):
        begins[o] = at
        total = at
        for k in range(4):
            slot = at + k
            mine = (links[jnp.minimum(slot, SLOTS - 1)] >> 8) == start + o
            total = total + jnp.where(mine & (slot < SLOTS), 1, 0)
        return total

    begins[HALF] = lax.fori_loop(0, HALF, count, at, unroll=4)

    for c in range(0, PATH_ROWS, 8):
        n = min(8, PATH_ROWS - c)
        for f in range(4):
            value = fields[f, c : c + n, :]
            if f < 2:
                value = value * (1.0 / FRAME_TONES) if f == 0 else jnp.sin(value)
            store[c : c + n, f, :] = value
            store[c : c + n, 4 + f, :] = value
    store[PATH_ROWS] = jnp.zeros((8, 128), jnp.float32)

    lane = lanes((8, 128))
    row = rows_of((8, 128))
    place = lane + jnp.where(row >= 4, 128, 0)
    tag_place = jnp.where(row == 4, lane - TAG_LANE, -1000)

    def pack(o, carry):
        first = begins[o]
        number = begins[o + 1] - first
        base = jnp.int32(0)
        message = jnp.zeros((8, 128), jnp.float32)
        for k in range(4):
            r = jnp.minimum(first + k, SLOTS - 1)
            cnt = jnp.where(k < number, counts[r], 0)
            tag = jnp.where(k < number, (links[r] & 255) + 1, 0)
            off = offsets[r]
            q = off >> 7
            s = off & 127
            value = jnp.where(lane < s + cnt - 128, store[q + 1], store[q])
            value = pltpu.roll(value, (base - s) & 127, 1)
            j = place - base
            message = jnp.where((j >= 0) & (j < cnt), value, message)
            for n, number_sent in enumerate((tag, cnt, base)):
                message = jnp.where(tag_place == 3 * k + n, number_sent.astype(jnp.float32), message)
            base = base + cnt
        sent[o] = message
        return carry

    lax.fori_loop(0, HALF, pack, 0, unroll=4)
    for c in range(0, HALF, 8):
        total = sent[c : c + 8, 4, :]
        for f in range(1, 4):
            total = total + pltpu.roll(sent[c : c + 8, 4 + f, :], 2 * f, 1)
        sent[c : c + 8, 4, :] = total

    @pl.when(grp == 0)
    def _():
        got[me] = sent[lax.rem(me, HALF)]

    pl.semaphore_wait(barrier, HALF + grp)
    wire = pl.ds(0, WIRE_ROWS)

    def send(hops, q, carry):
        near = lax.rem(me + 8 * q + hops, HALF)
        pltpu.make_async_remote_copy(
            src_ref=sent.at[near, wire],
            dst_ref=got.at[me, wire],
            send_sem=sems.at[0],
            recv_sem=sems.at[1],
            device_id={"cell": start + near},
            device_id_type=MESH,
        ).start()
        return carry

    for hops in (4, 3, 5, 2, 6, 1, 7):
        lax.fori_loop(0, HALF // 8, functools.partial(send, hops), 0, unroll=4)
    lax.fori_loop(1 - grp, HALF // 8, functools.partial(send, 0), 0)

    def messages(number):
        return pltpu.make_async_remote_copy(
            src_ref=sent.at[pl.ds(0, number), wire],
            dst_ref=got.at[pl.ds(start, number), wire],
            send_sem=sems.at[0],
            recv_sem=sems.at[1],
            device_id=sibling,
            device_id_type=MESH,
        )

    for g in range(2):
        pl.when(grp == g)(messages(HALF - 1 + g).wait_recv)
    swap = pltpu.make_async_remote_copy(
        src_ref=got.at[pl.ds(start, HALF), wire],
        dst_ref=got.at[pl.ds(start, HALF), wire],
        send_sem=sems.at[2],
        recv_sem=sems.at[3],
        device_id=sibling,
        device_id_type=MESH,
    )
    swap.start()
    for g in range(2):
        pl.when(grp == g)(messages(HALF - 1 + g).wait_send)
    swap.wait()


def seeds_of(fields, grp, e_seed, s_seed, coef):
    turns, sine, real, imag = [v + pltpu.roll(v, 64, 1) for v in fields]
    hi = lanes((8, 128)) >= 64
    s1, c1 = sincos_turns(turns)
    e = jnp.where(hi, 0.0, 1.0)
    f = jnp.where(hi, 1.0, 0.0)
    e_seed[pl.ds(8, 8, stride=16), :] = e
    for j in range(1, 9):
        e, f = e * c1 - f * s1, f * c1 + e * s1
        if j < 8:
            e_seed[pl.ds(8 + j, 8, stride=16), :] = e
        e_seed[pl.ds(8 - j, 8, stride=16), :] = jnp.where(hi, -e, e)
    _, c8 = sincos_turns(8.0 * turns)
    coef[0:8, :] = 2.0 * c8
    sa, ca = sincos_turns(0.5 * sine)
    first = (grp * (ANT // 2)).astype(jnp.float32)
    s0, c0 = sincos_turns(first * sine)
    _, a8 = sincos_turns(4.0 * sine)
    coef[8:16, :] = 2.0 * a8
    g1 = jnp.where(hi, -imag, real)
    g2 = jnp.where(hi, real, imag)
    x = g1 * c0 + g2 * s0
    y = g2 * c0 - g1 * s0
    for a in range(16):
        s_seed[pl.ds(a, 8, stride=32), :] = x
        s_seed[pl.ds(16 + a, 8, stride=32), :] = y
        if a < 15:
            x, y = x * ca + y * sa, y * ca - x * sa


def response_of(l, e_seed, s_seed, coef):
    c = jnp.broadcast_to(coef[l : l + 1, :], (8, 128))
    low = e_seed[16 * l : 16 * l + 8, :]
    top = e_seed[16 * l + 8 : 16 * l + 16, :]
    down = [top, low]
    up = [low, top]
    for _ in range(7):
        down.append(c * down[-1] - down[-2])
        up.append(c * up[-1] - up[-2])
    table = jnp.concatenate(down[:0:-1] + up[1:], axis=0).astype(jnp.bfloat16)
    c = jnp.broadcast_to(coef[8 + l : 9 + l, :], (8, 128))
    parts = []
    for h in range(2):
        at = 32 * l + 16 * h
        run = [s_seed[at : at + 8, :], s_seed[at + 8 : at + 16, :]]
        for _ in range(2):
            run.append(c * run[-1] - run[-2])
        parts += run
    spread = jnp.concatenate(parts, axis=0).astype(jnp.bfloat16)
    return lax.dot_general(
        spread, table, (((1,), (1,)), ((), ())), preferred_element_type=jnp.float32
    )


SEED_SCRATCH = [
    pltpu.VMEM((8 * 16, 128), jnp.float32),
    pltpu.VMEM((8 * 32, 128), jnp.float32),
    pltpu.VMEM((16, 128), jnp.float32),
]


def unpacked(code, load):
    base = code & 255
    cnt = (code >> 8) & 255
    lane = lanes((8, 128))
    message, overflow = load(code >> 16)
    value = jnp.where(lane < base + cnt - 128, overflow, message)
    return jnp.where(lane < cnt, pltpu.roll(value, (0 - base) & 127, 1), 0.0)


def transmit_kernel(
    slots, nearby, got, symbols, over, table, raw, table_s, serving,
    e_seed, s_seed, coef, e_seed2, s_seed2, coef2, sem
):
    me = lax.axis_index("cell")
    grp = lax.axis_index("grp")
    lane = lanes((8, 128))
    row = rows_of((8, 128))
    is_tag = (lane >= TAG_LANE) & (lane < TAG_LANE + 12)
    link = lane + 1
    found = [jnp.zeros((8, 128), jnp.int32) for _ in range(LINKS // 128)]
    for c in range(CELLS // 8):
        extra = got[pl.ds(64 * c + 4, 8, stride=8), :]
        number = jnp.where(is_tag, extra, 0.0).astype(jnp.int32)
        number = number + (pltpu.roll(number, 126, 1) << 9) + (pltpu.roll(number, 127, 1) << 17)
        for k in range(4):
            at = TAG_LANE + 3 * k
            value = jnp.broadcast_to(number[:, at : at + 1], (8, 128))
            code = (value >> 9) + ((8 * c + row) << 16)
            for h in range(LINKS // 128):
                found[h] = found[h] + jnp.where((value & 511) == link + 128 * h, code, 0)
    for h in range(LINKS // 128):
        table[h : h + 1, :] = jnp.sum(found[h], axis=0, keepdims=True)
    copy = pltpu.make_async_copy(table, table_s, sem)
    copy.start()

    def clear(i, carry):
        raw[i] = jnp.zeros((RESP, 128), jnp.float32)
        return carry

    lax.fori_loop(0, CELL_SECTORS, clear, 0, unroll=4)
    for c in range(CELLS // 8):
        extra = got[pl.ds(64 * c + 4, 8, stride=8), :]
        for f in range(4):
            over[pl.ds(64 * c + f, 8, stride=8), :] = extra if f == 0 else pltpu.roll(extra, 128 - 2 * f, 1)
    copy.wait()

    def load(source):
        at = pl.ds(pl.multiple_of(8 * source, 8), 8)
        return got[at, :], over[at, :]

    def serve(u, carry):
        g = u * NEARBY_COUNT + slots[u]
        code = table_s[g >> 7, g & 127]
        serving[pl.ds(pl.multiple_of(8 * u, 8), 8), :] = unpacked(code, load)
        return carry

    lax.fori_loop(0, USERS, serve, 0, unroll=8)

    seeds = (e_seed, s_seed, coef), (e_seed2, s_seed2, coef2)

    def prepare(c):
        fields = [serving[pl.ds(64 * c + f, 8, stride=8), :] for f in range(4)]
        seeds_of(fields, grp, *seeds[c % 2])

    prepare(0)
    for c in range(USERS // 8):
        if c + 1 < USERS // 8:
            prepare(c + 1)
        for l in range(8):
            u = 8 * c + l
            resp = response_of(l, *seeds[c % 2]).astype(jnp.bfloat16).astype(jnp.float32)
            sym = symbols[u].astype(jnp.float32)
            sym_r, sym_i = sym[0:1, :], sym[1:2, :]
            real, imag = resp[:ANT, :], resp[ANT:, :]
            part = jnp.concatenate(
                [real * sym_r + imag * sym_i, real * sym_i - imag * sym_r], axis=0
            )
            sector = nearby[slots[u], u] - me * CELL_SECTORS
            raw[sector] = raw[sector] + part


PIECE = REACH
PIECES = (0, 16)


def receive_kernel(
    nearby, table, got, over, raw, out, near, resp, part, other,
    e_seed, s_seed, coef, e_seed2, s_seed2, coef2, rows, rows2, send_sems, recv_sems
):
    me = lax.axis_index("cell")
    grp = lax.axis_index("grp")
    right = lax.rem(me + 1, CELLS)
    left = lax.rem(me + CELLS - 1, CELLS)
    barrier = pltpu.get_barrier_semaphore()
    for target in ({"cell": left}, {"cell": right}, {"grp": 1 - grp}):
        pl.semaphore_signal(barrier, inc=1, device_id=target, device_id_type=MESH)

    halo = []
    for n, begin in enumerate(PIECES):

        def normalise(s, carry):
            real, imag = raw[s, :ANT, :], raw[s, ANT:, :]
            power = jnp.mean(real * real + imag * imag, axis=1, keepdims=True)
            scale = 1.0 / jnp.sqrt(power + EPSILON)
            near[REACH + s] = jnp.concatenate([real * scale, imag * scale], axis=0).astype(jnp.bfloat16)
            return carry

        lax.fori_loop(begin, begin + PIECE, normalise, 0, unroll=8)
        if n == 0:
            pl.semaphore_wait(barrier, 3)
        to_left = begin < CELL_SECTORS - REACH
        land = begin + REACH + CELL_SECTORS if to_left else begin + REACH - CELL_SECTORS
        halo.append(
            pltpu.make_async_remote_copy(
                src_ref=near.at[pl.ds(REACH + begin, PIECE)],
                dst_ref=near.at[pl.ds(land, PIECE)],
                send_sem=send_sems.at[n],
                recv_sem=recv_sems.at[n],
                device_id={"cell": left if to_left else right},
                device_id_type=MESH,
            )
        )
        halo[-1].start()

    first, second = (e_seed, s_seed, coef), (e_seed2, s_seed2, coef2)

    def unpack(u, rows):
        u = jnp.minimum(u, USERS - 1)
        for l in range(8):
            code = table[u // 16, lax.rem(u, 16) * 8 + l]
            rows[8 * l : 8 * l + 8, :] = unpacked(code, lambda i: (got[i], over[i]))

    def prepare(rows, seeds):
        seeds_of([rows[pl.ds(f, 8, stride=8), :] for f in range(4)], grp, *seeds)

    def respond(u, seeds):
        for l in range(8):
            at = pl.ds(pl.multiple_of(u * (8 * RESP) + RESP * l, RESP), RESP)
            resp[at, :] = response_of(l, *seeds).astype(jnp.bfloat16)

    def two_users(v, carry):
        prepare(rows2, second)
        unpack(2 * v + 3, rows2)
        respond(2 * v, first)
        prepare(rows, first)
        unpack(2 * v + 4, rows)
        respond(2 * v + 1, second)
        return carry

    unpack(0, rows)
    prepare(rows, first)
    unpack(1, rows2)
    unpack(2, rows)
    lax.fori_loop(0, USERS // 2, two_users, 0)
    for copy in halo:
        copy.wait()

    def combine(u, carry):
        real = jnp.zeros((ANT, 128), jnp.float32)
        imag = jnp.zeros((ANT, 128), jnp.float32)
        for k in range(NEARBY_COUNT):
            sector = nearby[k, u] - me * CELL_SECTORS + REACH
            sector = jnp.clip(sector, 0, CELL_SECTORS + 2 * REACH - 1)
            tx = near[sector].astype(jnp.float32)
            at = pl.ds(pl.multiple_of(u * (8 * RESP) + RESP * k, RESP), RESP)
            ch = resp[at, :].astype(jnp.float32)
            real = real + (ch[:ANT] * tx[:ANT] - ch[ANT:] * tx[ANT:])
            imag = imag + (ch[:ANT] * tx[ANT:] + ch[ANT:] * tx[:ANT])
        part[u] = jnp.concatenate(
            [jnp.sum(real, axis=0, keepdims=True), jnp.sum(imag, axis=0, keepdims=True)], axis=0
        )
        return carry

    lax.fori_loop(0, USERS, combine, 0, unroll=4)
    swap = pltpu.make_async_remote_copy(
        src_ref=part,
        dst_ref=other,
        send_sem=send_sems.at[len(PIECES)],
        recv_sem=recv_sems.at[len(PIECES)],
        device_id={"grp": 1 - grp},
        device_id_type=MESH,
    )
    swap.start()
    swap.wait()
    out[...] = (part[...] + other[...]) * (1.0 / math.sqrt(SECTOR_ANTENNAS))


VMEM = pl.BlockSpec(memory_space=pltpu.VMEM)
SMEM = pl.BlockSpec(memory_space=pltpu.SMEM)
ANY = pl.BlockSpec(memory_space=pl.ANY)


def call(kernel, name, mib, out_shape, in_specs, scratch, remote=None):
    extra = {} if remote is None else {"collective_id": remote, "has_side_effects": True}
    many = isinstance(out_shape, (tuple, list))
    return pl.pallas_call(
        kernel,
        name=name,
        out_shape=out_shape,
        in_specs=in_specs,
        out_specs=[VMEM] * len(out_shape) if many else VMEM,
        scratch_shapes=scratch,
        compiler_params=pltpu.CompilerParams(vmem_limit_bytes=mib * MIB, **extra),
    )


def shards(
    path_delay,
    path_angle,
    path_gain,
    slot_counts,
    slot_offsets,
    ray_link,
    nearby_sectors,
    serving_slot,
    symbols,
):
    f32, bf16, i32 = jnp.float32, jnp.bfloat16, jnp.int32
    got = call(
        deliver_kernel,
        "deliver",
        16,
        jax.ShapeDtypeStruct((CELLS, 8, 128), f32),
        [ANY, ANY, ANY, ANY, VMEM],
        [
            pltpu.SMEM((SLOTS,), i32),
            pltpu.SMEM((SLOTS,), i32),
            pltpu.SMEM((SLOTS,), i32),
            pltpu.VMEM((PATH_ROWS + 1, 8, 128), f32),
            pltpu.VMEM((HALF, 8, 128), f32),
            pltpu.SMEM((HALF + 1,), i32),
            pltpu.SemaphoreType.DMA((3,)),
            pltpu.SemaphoreType.DMA((4,)),
        ],
        remote=0,
    )(
        slot_counts,
        slot_offsets,
        ray_link,
        serving_slot,
        jnp.stack((path_delay, path_angle, path_gain[0], path_gain[1])).reshape(4, PATH_ROWS, 128),
    )
    over, table, raw = call(
        transmit_kernel,
        "transmit",
        24,
        (
            jax.ShapeDtypeStruct((CELLS * 8, 128), f32),
            jax.ShapeDtypeStruct((LINKS // 128, 128), i32),
            jax.ShapeDtypeStruct((CELL_SECTORS, RESP, 128), f32),
        ),
        [SMEM, SMEM, VMEM, VMEM],
        [
            pltpu.SMEM((LINKS // 128, 128), i32),
            pltpu.VMEM((USERS * 8, 128), f32),
            *SEED_SCRATCH,
            *SEED_SCRATCH,
            pltpu.SemaphoreType.DMA,
        ],
    )(serving_slot, nearby_sectors, got.reshape(CELLS * 8, 128), symbols)
    return call(
        receive_kernel,
        "receive",
        24,
        jax.ShapeDtypeStruct((USERS, 2, FRAME_TONES), f32),
        [SMEM, SMEM, VMEM, VMEM, VMEM],
        [
            pltpu.VMEM((CELL_SECTORS + 2 * REACH, RESP, 128), bf16),
            pltpu.VMEM((LINKS * RESP, 128), bf16),
            pltpu.VMEM((USERS, 2, FRAME_TONES), f32),
            pltpu.VMEM((USERS, 2, FRAME_TONES), f32),
            *SEED_SCRATCH,
            *SEED_SCRATCH,
            pltpu.VMEM((64, 128), f32),
            pltpu.VMEM((64, 128), f32),
            pltpu.SemaphoreType.DMA((len(PIECES) + 1,)),
            pltpu.SemaphoreType.DMA((len(PIECES) + 1,)),
        ],
        remote=1,
    )(nearby_sectors, table, got, over.reshape(CELLS, 8, 128), raw)


def solution(mesh):
    placed = (
        P("cell"),
        P("cell"),
        P(None, "cell"),
        P("cell"),
        P("cell"),
        P("cell"),
        P(None, "cell"),
        P("cell"),
        P("cell", None, None),
    )
    return jax.shard_map(
        shards, mesh=mesh, in_specs=placed, out_specs=P("cell", None, None), check_vma=False
    )
```
